32 devices in a mesh: groups: 1, dp: 32 (over z, y, x, core).
Axes of the slice: x: 2, y: 2, z: 4, core: 2. Of those that a mesh axis runs over, the one named last changes fastest.
Arguments:
- activations: bfloat16 [128, 8192], P(('groups', 'dp')), may hold values from -6 to 6
- cotangent: bfloat16 [128, 8192], P(('groups', 'dp')), may hold values from -6 to 6
- w_gate: bfloat16 [28672, 8192], P('dp'), may hold values from -0.0625 to 0.0625
- w_up: bfloat16 [28672, 8192], P('dp'), may hold values from -0.0625 to 0.0625
- w_down: bfloat16 [28672, 8192], P('dp'), may hold values from -0.03125 to 0.03125
- proj_model: bfloat16 [8192, 192], P('dp'), may hold values from -0.0625 to 0.0625
- proj_hidden: bfloat16 [28672, 192], P('dp'), may hold values from -0.03125 to 0.03125
- seq_ids: int32 [128], P('groups'), may hold values from 0 to 15, never falling along the last dimension, each value on 1 to 16 neighbouring positions
- targets: bfloat16 [256, 3, 64, 64], P(('groups', 'dp')), may hold values from -24 to 24
- target_domain: int32 [256], P(('groups', 'dp')), may hold values from 0 to 31, never falling along the last dimension, each value on 1 to 16 neighbouring positions
Outputs:
- sketches: float32 [16, 3, 64, 64], P('groups')
- scores: float32 [16, 32], P('groups')
The draws below stay inside these ranges and needn't reach their ends.
Inputs may be any that keep to these rules, and one draw needn't show every extreme that they name: `seq_ids`: never falling along the tokens; each of the 16 sequences has 1 to 16 tokens, one exactly 16. `target_domain`: never falling along the target examples; each of the 32 domains has 1 to 16 examples, one exactly 16.
All inputs are finite; a program needn't handle non-finite values.
Results may differ from the reference program's by a relative error of at most 0.0032.
Values may be sent and summed in bfloat16 or wider, within the bound.
No kernel may reach another device: no remote copies, remote signals or barrier semaphores. Data moves between devices by JAX's collectives and lax.ppermute only.
A program may use at most 128 MiB of HBM per device.

```python
import math
import jax
import jax.numpy as jnp
import numpy as np
from jax import lax

D = 8192
FF = 28672
RANK = 64
DOMAINS = 32
SEQS = 16
TOKENS = 128
TARGETS = 256
SEQ_MOST = 16
DOM_MOST = 16


def level_of(own_key, extent, cuts, low, top_value):
    loudness, own = 1.0, jax.random.fold_in(own_key, 6)
    for dim, blocks in cuts:
        steps = jnp.exp(jax.random.uniform(jax.random.fold_in(own, dim), (blocks,), jnp.float32, low / len(cuts), top_value / len(cuts)))
        loudness = loudness * jnp.repeat(steps, extent[dim] // blocks).reshape([-1 if axis == dim else 1 for axis in range(len(extent))])
    return loudness


def length_profile(amount, total, reach, skew):
    portions = [(1 << 20) // math.isqrt(rank ** skew) + 1 for rank in range(2, amount + 1)]
    rest, counts = total - reach - (amount - 1), [1] * (amount - 1)
    while rest > 0:
        candidates = [i for i in range(amount - 1) if counts[i] < reach]
        mass, budget = sum([portions[i] for i in candidates]), rest
        for i in candidates:
            extra = min(reach - counts[i], max(1, budget * portions[i] // mass), rest)
            counts[i] = counts[i] + extra
            rest = rest - extra
    return np.array([reach] + counts)


def ragged_sizes(rng, amount, total, limit, slope):
    if amount == 2:
        one = jax.random.randint(rng, (), max(1, total - limit), min(limit, total - 1) + 1)
        return jnp.stack([one, total - one])
    tallies = jnp.asarray(length_profile(amount, total, limit, slope), jnp.int32)
    couples = (amount - 1) // 2
    source_of, taker = tallies[1:1 + 2 * couples:2], tallies[2:2 + 2 * couples:2]
    room = jnp.minimum(source_of - 1, limit - taker)
    moved = jax.random.randint(jax.random.fold_in(rng, 1), (couples,), 0, 1 << 20) % (room + 1)
    tallies = tallies.at[1:1 + 2 * couples:2].set(source_of - moved).at[2:2 + 2 * couples:2].set(taker + moved)
    return tallies[jax.random.permutation(jax.random.fold_in(rng, 2), amount)]


def bell_draw(key, extent, spread, bound, shards=(), dtype=jnp.bfloat16):
    values = spread * jax.random.normal(key, extent, jnp.float32)
    if shards:
        values = values * level_of(key, extent, shards, -0.22, 0.18)
    return jnp.clip(values, -bound, bound).astype(dtype)


def setup_inputs(seed: int = 0, part: int = 0) -> dict:
    streams_of = jax.random.split(jax.random.key(seed), 11)
    part_splits = jax.random.split(jax.random.fold_in(streams_of[10], part), 11)
    activations = bell_draw(part_splits[0], (TOKENS, D), 1.0, 6.0, ((0, 32),))
    cotangent = bell_draw(part_splits[1], (TOKENS, D), 1.0, 6.0, ((0, 32),))
    w_gate = bell_draw(streams_of[2], (FF, D), D ** -0.5, 0.0625, ((0, 32),))
    w_up = bell_draw(streams_of[3], (FF, D), D ** -0.5, 0.0625, ((0, 32),))
    w_down = bell_draw(streams_of[4], (FF, D), FF ** -0.5, 0.03125, ((0, 32),))
    proj_model = bell_draw(streams_of[5], (D, 3 * RANK), D ** -0.5, 0.0625, ((0, 32),))
    proj_hidden = bell_draw(streams_of[6], (FF, 3 * RANK), FF ** -0.5, 0.03125, ((0, 32),))
    seq_ids = jnp.searchsorted(jnp.cumsum(ragged_sizes(part_splits[7], SEQS, TOKENS, SEQ_MOST, 2)), jnp.arange(TOKENS), side="right").astype(jnp.int32)
    targets = bell_draw(part_splits[8], (TARGETS, 3, RANK, RANK), 4.0, 24.0, ((0, 32),))
    target_domain = jnp.searchsorted(jnp.cumsum(ragged_sizes(part_splits[9], DOMAINS, TARGETS, DOM_MOST, 2)), jnp.arange(TARGETS), side="right").astype(jnp.int32)
    return dict(activations=activations, cotangent=cotangent, w_gate=w_gate, w_up=w_up, w_down=w_down, proj_model=proj_model, proj_hidden=proj_hidden, seq_ids=seq_ids, targets=targets, target_domain=target_domain)


def sequence_sketch(vectors, onehot):
    blocks = vectors.reshape(vectors.shape[0], 6, RANK)
    left_side = jnp.stack((blocks[:, 4], blocks[:, 5], blocks[:, 3]), 1)
    right_side = jnp.stack((blocks[:, 0], blocks[:, 1], blocks[:, 2]), 1)
    return jnp.einsum('ns,nka,nkb->skab', onehot, left_side, right_side, precision=lax.Precision.HIGHEST)

def reference(activations, cotangent, w_gate, w_up, w_down, proj_model, proj_hidden, seq_ids, targets, target_domain):
    pieces = 8
    width_block = FF // pieces
    in_model = jnp.dot(activations, proj_model[:, :2 * RANK], preferred_element_type=jnp.float32)
    out_down = jnp.dot(cotangent, proj_model[:, 2 * RANK:], preferred_element_type=jnp.float32)

    def hidden_block(inputs_block):
        gate_rows, up_rows, down_rows, proj_rows = inputs_block
        gate_value = jnp.dot(activations, gate_rows.T, preferred_element_type=jnp.float32)
        up_value = jnp.dot(activations, up_rows.T, preferred_element_type=jnp.float32)
        sigmoid_gate = jax.nn.sigmoid(gate_value)
        silu_gate = gate_value * sigmoid_gate
        hidden = (silu_gate * up_value).astype(jnp.bfloat16)
        grad_hidden = jnp.dot(cotangent, down_rows.T, preferred_element_type=jnp.float32)
        grad_gate = (grad_hidden * up_value * sigmoid_gate * (1.0 + gate_value * (1.0 - sigmoid_gate))).astype(jnp.bfloat16)
        grad_up = (grad_hidden * silu_gate).astype(jnp.bfloat16)
        in_down = jnp.dot(hidden, proj_rows[:, :RANK], preferred_element_type=jnp.float32)
        out_gate = jnp.dot(grad_gate, proj_rows[:, RANK:2 * RANK], preferred_element_type=jnp.float32)
        out_up = jnp.dot(grad_up, proj_rows[:, 2 * RANK:], preferred_element_type=jnp.float32)
        return jnp.concatenate([in_down, out_gate, out_up], 1)
    stacked = (w_gate.reshape(pieces, width_block, D), w_up.reshape(pieces, width_block, D), w_down.reshape(pieces, width_block, D), proj_hidden.reshape(pieces, width_block, 3 * RANK))
    hidden_terms = lax.optimization_barrier(jnp.sum(lax.map(hidden_block, stacked), axis=0))
    vectors = jnp.concatenate([in_model, out_down, hidden_terms], 1)
    onehot = (seq_ids[:, None] == jnp.arange(SEQS)[None, :]).astype(jnp.float32)
    sketches = sequence_sketch(vectors, onehot)
    flat_sketch = sketches.reshape(SEQS, 3 * RANK * RANK)
    domain_onehot = (target_domain[None, :] == jnp.arange(DOMAINS)[:, None]).astype(jnp.bfloat16)
    domain_sum = jnp.dot(domain_onehot, targets.reshape(TARGETS, 3 * RANK * RANK), preferred_element_type=jnp.float32)
    domain_count = lax.optimization_barrier(jnp.sum(domain_onehot.astype(jnp.float32), 1))
    domain_mean = domain_sum / domain_count[:, None]
    inverse_norm = lax.rsqrt(lax.optimization_barrier(jnp.sum(flat_sketch * flat_sketch, 1)) + 1e-06)
    scores = jnp.dot(flat_sketch, domain_mean.T, precision=lax.Precision.HIGHEST) * inverse_norm[:, None]
    return (sketches, scores)
```

```python
import functools

import jax
import jax.numpy as jnp
import numpy as np
from jax import lax
from jax.experimental import pallas as pl
from jax.experimental.pallas import tpu as pltpu
from jax.sharding import PartitionSpec as P

DOMAINS = 32
SEQS = 16
HIGHEST = lax.Precision.HIGHEST
F32 = jnp.float32
BF16 = jnp.bfloat16


def axis_sizes(count):
    if count == 32:
        return (4, 2, 2, 2)
    if count == 128:
        return (8, 8, 2)
    return (count,)


class Ring:
    def __init__(self, count):
        self.count = count
        self.sizes = axis_sizes(count)
        self.strides = [int(np.prod(self.sizes[i + 1 :])) for i in range(len(self.sizes))]
        self.me = lax.axis_index("dp")

    def coord(self, axis):
        return (self.me // self.strides[axis]) % self.sizes[axis]

    def shift(self, value, axis, amount):
        size, stride = self.sizes[axis], self.strides[axis]
        pairs = []
        for source in range(self.count):
            at = (source // stride) % size
            pairs.append((source, source + ((at + amount) % size - at) * stride))
        return lax.ppermute(value, "dp", pairs)

    def gather(self, rows, order):
        size = self.sizes[0]
        received = [rows] + [self.shift(rows, 0, k) for k in range(1, size)]
        at = self.coord(0)
        block = jnp.concatenate(
            [lax.select_n((at + size - j) % size, *received) for j in range(size)], 0
        )
        pieces = [(block, tuple(0 for _ in self.sizes))]
        for axis in order:
            grown = list(pieces)
            for k in range(1, self.sizes[axis]):
                for piece, back in pieces:
                    moved = tuple(k if i == axis else b for i, b in enumerate(back))
                    grown.append((self.shift(piece, axis, k), moved))
            pieces = grown
        slots = []
        for _, back in pieces:
            slot = 0
            for axis in range(1, len(self.sizes)):
                spot = (self.coord(axis) + self.sizes[axis] - back[axis]) % self.sizes[axis]
                slot = slot * self.sizes[axis] + spot
            slots.append(jnp.asarray(slot, jnp.int32))
        return [piece for piece, _ in pieces], jnp.stack(slots)

    def slot_order(self, per_token):
        size = self.sizes[0]
        rest = self.count // size
        return per_token.reshape(size, rest, -1).transpose(1, 0, 2).reshape(-1)


def exchange(blocks):
    return lax.all_to_all(blocks, "dp", split_axis=0, concat_axis=0, tiled=True)


def spread(block, count):
    return exchange(jnp.broadcast_to(block[None], (count,) + block.shape))


def place(slots, pieces, rows, into):
    for i, piece in enumerate(pieces):
        start = pl.multiple_of(slots[i] * rows, rows)
        into[pl.ds(start, rows), :] = piece[...]


def times_transposed(weight, tokens):
    return lax.dot_general(weight, tokens, (((1,), (1,)), ((), ())), preferred_element_type=F32)


def down_kernel(count, rows, slots, *refs):
    pieces, (weight, out, tokens) = refs[:count], refs[count:]
    place(slots, pieces, rows, tokens)
    part = times_transposed(weight[...], tokens[...])

    @pl.when(pl.program_id(0) == 0)
    def _():
        out[...] = part

    @pl.when(pl.program_id(0) > 0)
    def _():
        out[...] += part


def up_kernel(count, rows, slots, *refs):
    pieces = refs[:count]
    w_gate, w_up, grad_hidden, proj, left, tokens, gate, up = refs[count:]
    step = pl.program_id(0)
    place(slots, pieces, rows, tokens)
    gate_part = times_transposed(w_gate[...], tokens[...])
    up_part = times_transposed(w_up[...], tokens[...])

    @pl.when(step == 0)
    def _():
        gate[...] = gate_part
        up[...] = up_part

    @pl.when(step > 0)
    def _():
        gate[...] += gate_part
        up[...] += up_part

    @pl.when(step == pl.num_programs(0) - 1)
    def _():
        rank = left.shape[0] // 3
        gate_value, up_value, grad = gate[...], up[...], grad_hidden[...]
        s = 1.0 / (1.0 + jnp.exp(-gate_value))
        silu = gate_value * s
        hidden = (silu * up_value).astype(BF16)
        grad_gate = (grad * up_value * s * (1.0 + gate_value * (1.0 - s))).astype(BF16)
        grad_up = (grad * silu).astype(BF16)
        left[:rank, :] = jnp.dot(proj[rank : 2 * rank, :], grad_gate, preferred_element_type=F32)
        left[rank : 2 * rank, :] = jnp.dot(proj[2 * rank :, :], grad_up, preferred_element_type=F32)
        left[2 * rank :, :] = jnp.dot(proj[:rank, :], hidden, preferred_element_type=F32)


def chunk_of(width, rows):
    return min(width, 1024 if rows > 256 else 2048)


def piece_specs(pieces, chunk):
    return [pl.BlockSpec((piece.shape[0], chunk), lambda k, s: (0, k)) for piece in pieces]


def down_product(pieces, slots, weight):
    hidden, width = weight.shape
    rows = pieces[0].shape[0]
    tokens = rows * len(pieces)
    chunk = chunk_of(width, hidden)
    return pl.pallas_call(
        functools.partial(down_kernel, len(pieces), rows),
        out_shape=jax.ShapeDtypeStruct((hidden, tokens), F32),
        grid_spec=pltpu.PrefetchScalarGridSpec(
            num_scalar_prefetch=1,
            grid=(width // chunk,),
            in_specs=piece_specs(pieces, chunk)
            + [pl.BlockSpec((hidden, chunk), lambda k, s: (0, k))],
            out_specs=pl.BlockSpec((hidden, tokens), lambda k, s: (0, 0)),
            scratch_shapes=[pltpu.VMEM((tokens, chunk), BF16)],
        ),
        compiler_params=pltpu.CompilerParams(vmem_limit_bytes=40 * 2**20),
        cost_estimate=pl.CostEstimate(
            flops=2 * hidden * width * tokens, bytes_accessed=2 * hidden * width, transcendentals=0
        ),
        name="down_product",
    )(slots, *pieces, weight)


def up_product(pieces, slots, w_gate, w_up, grad_hidden, proj):
    hidden, width = w_gate.shape
    rows = pieces[0].shape[0]
    tokens = rows * len(pieces)
    chunk = chunk_of(width, hidden)
    whole = lambda shape: pl.BlockSpec(shape, lambda k, s: (0, 0))
    return pl.pallas_call(
        functools.partial(up_kernel, len(pieces), rows),
        out_shape=jax.ShapeDtypeStruct((proj.shape[0], tokens), F32),
        grid_spec=pltpu.PrefetchScalarGridSpec(
            num_scalar_prefetch=1,
            grid=(width // chunk,),
            in_specs=piece_specs(pieces, chunk)
            + [pl.BlockSpec((hidden, chunk), lambda k, s: (0, k))] * 2
            + [whole(grad_hidden.shape), whole(proj.shape)],
            out_specs=whole((proj.shape[0], tokens)),
            scratch_shapes=[
                pltpu.VMEM((tokens, chunk), BF16),
                pltpu.VMEM((hidden, tokens), F32),
                pltpu.VMEM((hidden, tokens), F32),
            ],
        ),
        compiler_params=pltpu.CompilerParams(vmem_limit_bytes=48 * 2**20),
        cost_estimate=pl.CostEstimate(
            flops=4 * hidden * width * tokens,
            bytes_accessed=4 * hidden * width,
            transcendentals=hidden * tokens,
        ),
        name="up_product",
    )(slots, *pieces, w_gate, w_up, grad_hidden, proj)


def model_columns(pieces, slots, offset, width):
    cut = jnp.stack([lax.dynamic_slice_in_dim(piece, offset, width, 1) for piece in pieces])
    order = jnp.argmax(slots[None, :] == jnp.arange(len(pieces))[:, None], axis=1)
    picks = [
        lax.dynamic_index_in_dim(cut, order[i], 0, keepdims=False) for i in range(len(pieces))
    ]
    return jnp.concatenate(picks, 0)


def on_device(
    count,
    activations,
    cotangent,
    w_gate,
    w_up,
    w_down,
    proj_model,
    proj_hidden,
    seq_ids,
    targets,
    target_domain,
):
    ring = Ring(count)
    rank = proj_model.shape[1] // 3
    model_cols = proj_model.shape[0]
    offset = ring.me * model_cols
    own_rank = -(-rank // count)
    padded_rank = own_rank * count

    inner = list(range(1, len(ring.sizes)))
    flipped = inner[:-1][::-1] + inner[-1:]
    out_pieces, out_slots = ring.gather(cotangent, inner)
    in_pieces, in_slots = ring.gather(activations, flipped)
    tokens = count * activations.shape[0]

    examples = targets.shape[0]
    cut = jnp.pad(targets, ((0, 0), (0, 0), (0, padded_rank - rank), (0, 0)))
    cut = cut.reshape(examples, 3, count, own_rank, rank).transpose(2, 0, 1, 3, 4)
    cut = cut.reshape(count, examples, 3 * own_rank * rank)
    tags = jnp.broadcast_to(target_domain.astype(BF16)[None, :, None], (count, examples, 128))
    held = exchange(jnp.concatenate([cut, tags], 2)).reshape(count * examples, -1)
    example_domain = held[:, -1].astype(jnp.int32)
    domain_onehot = (example_domain[None, :] == jnp.arange(DOMAINS)[:, None]).astype(BF16)
    domain_sum = jnp.dot(domain_onehot, held[:, :-128], preferred_element_type=F32)
    domain_count = jnp.sum(domain_onehot.astype(F32), 1)
    domain_mean = (domain_sum / domain_count[:, None]).reshape(DOMAINS, 3, own_rank, rank)

    in_columns = model_columns(in_pieces, in_slots, offset, model_cols)
    out_columns = model_columns(out_pieces, out_slots, offset, model_cols)
    proj_t = proj_model.T
    right = jnp.concatenate(
        [
            times_transposed(proj_t[: 2 * rank], in_columns),
            times_transposed(proj_t[2 * rank :], out_columns),
        ],
        0,
    ).reshape(3, rank, tokens)

    def cut_rows(values):
        values = jnp.pad(values, ((0, 0), (0, padded_rank - rank), (0, 0)))
        values = values.reshape(3, count, own_rank, tokens).transpose(1, 0, 2, 3)
        return values.reshape(count, 3 * own_rank, tokens)

    def join_rows(values):
        values = values.reshape(count, 3, own_rank, tokens).transpose(1, 0, 2, 3)
        return values.reshape(3, padded_rank, tokens)[:, :rank]

    own_right = jnp.sum(exchange(cut_rows(right)), 0)
    right = join_rows(spread(own_right, count))

    grad_hidden = down_product(out_pieces, out_slots, w_down)
    left = up_product(in_pieces, in_slots, w_gate, w_up, grad_hidden, proj_hidden.T)
    own_left = jnp.sum(exchange(cut_rows(left.reshape(3, rank, tokens))), 0)

    ids = ring.slot_order(seq_ids)
    onehot = (ids[None, :] == jnp.arange(SEQS)[:, None]).astype(F32)
    own_rows = own_left.reshape(3, 1, own_rank, tokens) * onehot[None, :, None, :]
    own_sketch = jnp.einsum("ksat,kbt->skab", own_rows, right, precision=HIGHEST)
    own_scores = jnp.einsum("skab,dkab->sd", own_sketch, domain_mean, precision=HIGHEST)

    score_rows = own_scores.reshape(-1, tokens)
    shared = spread(jnp.concatenate([own_left, score_rows], 0), count)
    left = join_rows(shared[:, : 3 * own_rank])
    total = jnp.sum(shared[:, 3 * own_rank :], 0).reshape(SEQS, DOMAINS)
    rows = left[:, None] * onehot[None, :, None, :]
    sketches = jnp.einsum("ksat,kbt->skab", rows, right, precision=HIGHEST)
    flat = sketches.reshape(SEQS, -1)
    inverse_norm = lax.rsqrt(jnp.sum(flat * flat, 1) + 1e-06)
    return sketches, total * inverse_norm[:, None]


def solution(mesh):
    in_specs = (
        P(("groups", "dp"), None),
        P(("groups", "dp"), None),
        P("dp", None),
        P("dp", None),
        P("dp", None),
        P("dp", None),
        P("dp", None),
        P("groups"),
        P(("groups", "dp"), None, None, None),
        P(("groups", "dp")),
    )
    out_specs = (P("groups", None, None, None), P("groups", None))
    return jax.shard_map(
        functools.partial(on_device, mesh.shape["dp"]),
        mesh=mesh,
        in_specs=in_specs,
        out_specs=out_specs,
        check_vma=False,
    )
```

```python
import functools

import jax
import jax.numpy as jnp
import numpy as np
from jax import lax
from jax.experimental import pallas as pl
from jax.experimental.pallas import tpu as pltpu
from jax.sharding import PartitionSpec as P

DOMAINS = 32
SEQS = 16
GROUP = 8
HIGHEST = lax.Precision.HIGHEST
F32 = jnp.float32
BF16 = jnp.bfloat16
VMEM = pl.BlockSpec(memory_space=pltpu.VMEM)


def axis_sizes(count):
    if count == 32:
        return (4, 2, 2, 2)
    if count == 128:
        return (8, 8, 2)
    return (count,)


def strides_of(sizes):
    return [int(np.prod(sizes[i + 1 :])) for i in range(len(sizes))]


def shift(value, sizes, axis, amount):
    size, stride = sizes[axis], strides_of(sizes)[axis]
    pairs = []
    for source in range(int(np.prod(sizes))):
        at = (source // stride) % size
        pairs.append((source, source + ((at + amount) % size - at) * stride))
    return lax.ppermute(value, "dp", pairs)


def gather_first(rows, sizes):
    size = sizes[0]
    rest = int(np.prod(sizes)) // size
    groups = [[r + z * rest for z in range(size)] for r in range(rest)]
    copies = jnp.broadcast_to(rows[None], (size,) + rows.shape)
    return lax.all_to_all(
        copies, "dp", split_axis=0, concat_axis=0, axis_index_groups=groups, tiled=True
    )


def gather_rest(block, sizes, order):
    pieces = [(block, tuple(0 for _ in sizes))]
    for axis in order:
        grown = list(pieces)
        for k in range(1, sizes[axis]):
            for piece, back in pieces:
                moved = tuple(k if i == axis else b for i, b in enumerate(back))
                grown.append((shift(piece, sizes, axis, k), moved))
        pieces = grown
    return [piece for piece, _ in pieces], [back for _, back in pieces]


def slot_order(per_token, sizes):
    rest = int(np.prod(sizes)) // sizes[0]
    each = per_token.shape[0] // (sizes[0] * rest)
    split = per_token.reshape((sizes[0], rest, each) + per_token.shape[1:])
    return jnp.swapaxes(split, 0, 1).reshape(per_token.shape)


def exchange(blocks):
    return lax.all_to_all(blocks, "dp", split_axis=0, concat_axis=0, tiled=True)


def transposed_dot(left, right, precision=None):
    return lax.dot_general(
        left, right, (((1,), (1,)), ((), ())), precision=precision, preferred_element_type=F32
    )


def place_pieces(pieces, backs, sizes, into):
    me = lax.axis_index("dp")
    strides = strides_of(sizes)
    rows = pieces[0].shape[0] // 2
    for piece, back in zip(pieces, backs):
        slot = 0
        for axis in range(1, len(sizes)):
            at = lax.rem(lax.div(me, strides[axis]), sizes[axis])
            slot = slot * sizes[axis] + lax.rem(at + sizes[axis] - back[axis], sizes[axis])
        start = pl.multiple_of(slot * rows, rows)
        for side in range(2):
            into[side, pl.ds(start, rows), :] = piece[side * rows : (side + 1) * rows, :]


def stream_products(weights, first, tokens, sums, buffers, arrived):
    chunk = buffers.shape[3]
    steps = tokens.shape[2] // chunk
    sides = (1, 0, 0)

    def copy(step, w):
        slot = lax.rem(step, 2)
        columns = pl.ds(pl.multiple_of(first + step * chunk, chunk), chunk)
        return pltpu.make_async_copy(
            weights[w].at[:, columns], buffers.at[slot, w], arrived.at[slot, w]
        )

    def fetch():
        for step in range(min(2, steps)):
            for w in range(3):
                copy(step, w).start()

    def run():
        @pl.loop(0, steps)
        def _(step):
            columns = pl.ds(pl.multiple_of(step * chunk, chunk), chunk)
            for w in range(3):
                copy(step, w).wait()
                sums[w] += transposed_dot(
                    buffers[lax.rem(step, 2), w], tokens[sides[w], :, columns]
                )

                @pl.when(step + 2 < steps)
                def _():
                    copy(step + 2, w).start()

    return fetch, run


def first_half_kernel(backs, sizes, *refs):
    pieces, refs = refs[: len(backs)], refs[len(backs) :]
    w_down, w_gate, w_up, sums, tokens, buffers, arrived = refs
    fetch, run = stream_products((w_down, w_gate, w_up), 0, tokens, sums, buffers, arrived)
    fetch()
    place_pieces(pieces, backs, sizes, tokens)
    sums[...] = jnp.zeros_like(sums)
    run()


def second_half_kernel(backs, sizes, *refs):
    pieces, refs = refs[: len(backs)], refs[len(backs) :]
    before, proj, w_down, w_gate, w_up, left, sums, tokens, stacked, buffers, arrived = refs
    first = tokens.shape[2]
    fetch, run = stream_products((w_down, w_gate, w_up), first, tokens, sums, buffers, arrived)
    fetch()
    place_pieces(pieces, backs, sizes, tokens)
    sums[...] = before[...]
    run()
    hidden_units = sums.shape[1]
    tile = 128 if hidden_units % 128 == 0 else 32

    @pl.loop(0, hidden_units // tile)
    def _(step):
        rows = pl.ds(pl.multiple_of(step * tile, tile), tile)
        grad, gate_value, up_value = sums[0, rows, :], sums[1, rows, :], sums[2, rows, :]
        s = 1.0 / (1.0 + jnp.exp(-gate_value))
        silu = gate_value * s
        stacked[0, rows, :] = (
            grad * up_value * s * (1.0 + gate_value * (1.0 - s))
        ).astype(BF16)
        stacked[1, rows, :] = (grad * silu).astype(BF16)
        stacked[2, rows, :] = (silu * up_value).astype(BF16)

    left[...] = sum(
        jnp.dot(proj[k], stacked[k], preferred_element_type=F32) for k in range(3)
    ).reshape(left.shape)


def products(pieces, backs, sizes, weights, before=None, proj=None):
    w_down, w_gate, w_up = weights
    hidden, width = w_gate.shape
    rows, half = pieces[0].shape
    tokens = rows // 2 * len(pieces)
    chunk = min(half, 1024)
    any_space = pl.BlockSpec(memory_space=pl.ANY)
    common = dict(
        compiler_params=pltpu.CompilerParams(vmem_limit_bytes=48 * 2**20),
        cost_estimate=pl.CostEstimate(
            flops=6 * hidden * half * tokens,
            bytes_accessed=6 * hidden * half,
            transcendentals=hidden * tokens,
        ),
    )
    scratch = [
        pltpu.VMEM((2, tokens, half), BF16),
        pltpu.VMEM((2, 3, hidden, chunk), BF16),
        pltpu.SemaphoreType.DMA((2, 3)),
    ]
    sums = (3, hidden, tokens)
    if before is None:
        return pl.pallas_call(
            functools.partial(first_half_kernel, backs, sizes),
            out_shape=jax.ShapeDtypeStruct(sums, F32),
            in_specs=[VMEM] * len(pieces) + [any_space] * 3,
            out_specs=VMEM,
            scratch_shapes=scratch,
            name="first_half",
            **common,
        )(*pieces, w_down, w_gate, w_up)
    count = int(np.prod(sizes))
    return pl.pallas_call(
        functools.partial(second_half_kernel, backs, sizes),
        out_shape=jax.ShapeDtypeStruct((count, GROUP, tokens), F32),
        in_specs=[VMEM] * (len(pieces) + 2) + [any_space] * 3,
        out_specs=VMEM,
        scratch_shapes=[pltpu.VMEM(sums, F32), scratch[0], pltpu.VMEM(sums, BF16)] + scratch[1:],
        name="second_half",
        **common,
    )(*pieces, before, proj, w_down, w_gate, w_up)


def score_kernel(left, right, ids, mean, out):
    tokens = ids.shape[1]
    own = jnp.sum(left[...], 0)
    onehot = (ids[...] == lax.broadcasted_iota(jnp.int32, (SEQS, tokens), 0)).astype(F32)
    rows = jnp.concatenate([onehot * own[r : r + 1, :] for r in range(GROUP)], 0)
    sketch = transposed_dot(rows, right[...].reshape(-1, tokens), HIGHEST)
    sketch = jnp.concatenate([sketch[r * SEQS : (r + 1) * SEQS] for r in range(GROUP)], 1)
    scores = transposed_dot(sketch, mean[...], HIGHEST)
    half = SEQS // 2
    tail = jnp.concatenate(
        [scores[:half], scores[half:], jnp.zeros((half, tokens - 2 * DOMAINS), F32)], 1
    )
    out[:, :GROUP, :] = jnp.broadcast_to(own[None], (out.shape[0],) + own.shape)
    out[:, GROUP:, :] = jnp.broadcast_to(tail[None], (out.shape[0],) + tail.shape)


def sketch_kernel(own_rank, rank, shared, right, ids, sketches, scores):
    count, height, tokens = shared.shape
    onehot = ids[...] == lax.broadcasted_iota(jnp.int32, (SEQS, tokens), 0)
    onehot = onehot.astype(F32).astype(BF16)
    norm = jnp.zeros((SEQS, 1), F32)
    for k in range(3):
        split = []
        for source, first in ((shared, 0), (right, 0)):
            rows = jnp.concatenate(
                [source[:, first + k * own_rank + i, :] for i in range(own_rank)], 0
            )[:rank]
            high = rows.astype(BF16)
            low = (rows - high.astype(F32)).astype(BF16)
            split.append((high, low))
        (left_high, left_low), (right_high, right_low) = split
        left = jnp.concatenate([left_high, left_high, left_low], 1)
        right_k = jnp.concatenate([right_high, right_low, right_high], 1)
        masks = jnp.concatenate([onehot] * 3, 1)
        rows = jnp.concatenate([left * masks[s : s + 1, :] for s in range(SEQS)], 0)
        sketch = transposed_dot(rows, right_k).reshape(SEQS, rank, rank)
        sketches[:, k] = sketch
        norm += jnp.sum(jnp.sum(sketch * sketch, 1), 1, keepdims=True)
    tail = jnp.sum(shared[:, GROUP:, :], 0)
    total = jnp.concatenate([tail[:, :DOMAINS], tail[:, DOMAINS : 2 * DOMAINS]], 0)
    scores[...] = total * lax.rsqrt(norm + 1e-06)


def on_device(
    count,
    activations,
    cotangent,
    w_gate,
    w_up,
    w_down,
    proj_model,
    proj_hidden,
    seq_ids,
    targets,
    target_domain,
):
    sizes = axis_sizes(count)
    rank = proj_model.shape[1] // 3
    model_cols, hidden = proj_model.shape[0], proj_hidden.shape[0]
    own_rank = -(-rank // count)
    padded = own_rank * count
    each, width = activations.shape
    tokens = count * each
    half = width // 2
    examples = targets.shape[0]

    both = jnp.concatenate([activations, cotangent], 0)
    blocks = []
    for h in range(2):
        first = gather_first(both[:, h * half : (h + 1) * half], sizes)
        first = first.reshape(sizes[0], 2, each, half).transpose(1, 0, 2, 3)
        blocks.append(first.reshape(2 * sizes[0] * each, half))
    inner = list(range(1, len(sizes)))
    pieces_0, backs_0 = gather_rest(blocks[0], sizes, inner)
    pieces_1, backs_1 = gather_rest(blocks[1], sizes, inner[:-1][::-1] + inner[-1:])

    def scatter_rows(values, k):
        values = jnp.pad(values, ((0, padded - rank), (0, 0)))
        values = values.reshape(own_rank, count, -1).transpose(1, 0, 2)
        low = k * own_rank
        return jnp.pad(values, ((0, 0), (low, GROUP - low - own_rank), (0, 0))).reshape(
            count * GROUP, -1
        )

    columns = both.reshape(2 * each, count, model_cols).transpose(1, 0, 2)
    cut = jnp.pad(targets, ((0, 0), (0, 0), (0, padded - rank), (0, 0)))
    cut = cut.reshape(examples, 3, own_rank, count, rank).transpose(3, 0, 1, 2, 4)
    cut = cut.reshape(count, examples, 3 * own_rank * rank)
    tags = jnp.broadcast_to(target_domain.astype(BF16)[None, :, None], (count, examples, 128))
    tall = max(2 * each, examples)
    sent = [
        jnp.pad(part, ((0, 0), (0, tall - part.shape[1]), (0, 0))) for part in (cut, tags, columns)
    ]
    held = exchange(jnp.concatenate(sent, 2))

    entries = 3 * own_rank * rank
    held_targets = held[:, :examples, : entries + 128].reshape(count * examples, -1)
    domains = held_targets[:, -1].astype(F32)
    domain_onehot = (domains[None, :] == jnp.arange(DOMAINS, dtype=F32)[:, None]).astype(BF16)
    domain_sum = jnp.dot(domain_onehot, held_targets[:, :entries], preferred_element_type=F32)
    domain_count = jnp.sum(domain_onehot.astype(F32), 1)
    mean = (domain_sum / domain_count[:, None]).reshape(DOMAINS, 3, own_rank, rank)
    mean = jnp.pad(mean, ((0, 0), (0, 0), (0, 0), (0, padded - rank)))
    mean = mean.reshape(DOMAINS, 3, own_rank, own_rank, count).transpose(0, 1, 2, 4, 3)
    mean = mean[:, :, :, :, None, :] * jnp.eye(3, dtype=F32)[None, :, None, None, :, None]
    mean = mean.reshape(DOMAINS, 3 * own_rank, count, 3 * own_rank)
    spare = GROUP - 3 * own_rank
    mean = jnp.pad(mean, ((0, 0), (0, spare), (0, 0), (0, spare)))
    mean = mean.reshape(DOMAINS, GROUP * count * GROUP)

    held_columns = held[:, : 2 * each, entries + 128 :].reshape(count, 2, each, model_cols)
    sides = [
        slot_order(held_columns[:, side].reshape(tokens, model_cols), sizes) for side in range(2)
    ]
    proj_t = proj_model.T
    proj_in = scatter_rows(proj_t[:rank], 0) + scatter_rows(proj_t[rank : 2 * rank], 1)
    proj_out = scatter_rows(proj_t[2 * rank :], 2)
    right = transposed_dot(proj_in, sides[0]) + transposed_dot(proj_out, sides[1])
    own_right = jnp.sum(exchange(right.reshape(count, GROUP, tokens)), 0)
    right = exchange(jnp.broadcast_to(own_right[None], (count, GROUP, tokens)))

    proj_h = proj_hidden.T
    proj_left = jnp.stack(
        [
            scatter_rows(proj_h[rank : 2 * rank], 0),
            scatter_rows(proj_h[2 * rank :], 1),
            scatter_rows(proj_h[:rank], 2),
        ]
    )
    ids = slot_order(seq_ids, sizes)[None, :]

    weights = (w_down, w_gate, w_up)
    sums = products(pieces_0, backs_0, sizes, weights)
    left = exchange(products(pieces_1, backs_1, sizes, weights, sums, proj_left))

    shared = exchange(
        pl.pallas_call(
            score_kernel,
            out_shape=jax.ShapeDtypeStruct((count, 2 * GROUP, tokens), F32),
            in_specs=[VMEM] * 4,
            out_specs=VMEM,
            compiler_params=pltpu.CompilerParams(vmem_limit_bytes=32 * 2**20),
            name="own_scores",
        )(left, right, ids, mean)
    )
    return pl.pallas_call(
        functools.partial(sketch_kernel, own_rank, rank),
        out_shape=(
            jax.ShapeDtypeStruct((SEQS, 3, rank, rank), F32),
            jax.ShapeDtypeStruct((SEQS, DOMAINS), F32),
        ),
        in_specs=[VMEM] * 3,
        out_specs=(VMEM, VMEM),
        compiler_params=pltpu.CompilerParams(vmem_limit_bytes=40 * 2**20),
        name="sketches",
    )(shared, right, ids)


def solution(mesh):
    in_specs = (
        P(("groups", "dp"), None),
        P(("groups", "dp"), None),
        P("dp", None),
        P("dp", None),
        P("dp", None),
        P("dp", None),
        P("dp", None),
        P("groups"),
        P(("groups", "dp"), None, None, None),
        P(("groups", "dp")),
    )
    out_specs = (P("groups", None, None, None), P("groups", None))
    return jax.shard_map(
        functools.partial(on_device, mesh.shape["dp"]),
        mesh=mesh,
        in_specs=in_specs,
        out_specs=out_specs,
        check_vma=False,
    )
```

```python
import functools

import jax
import jax.numpy as jnp
import numpy as np
from jax import lax
from jax.experimental import pallas as pl
from jax.experimental.pallas import tpu as pltpu
from jax.sharding import PartitionSpec as P

DOMAINS = 32
SEQS = 16
HIGHEST = lax.Precision.HIGHEST
F32 = jnp.float32
BF16 = jnp.bfloat16
VMEM = pl.BlockSpec(memory_space=pltpu.VMEM)
ANY = pl.BlockSpec(memory_space=pl.ANY)


def axis_sizes(count):
    if count == 32:
        return (4, 2, 2, 2)
    if count == 128:
        return (8, 8, 2)
    return (count, 1)


def strides_of(sizes):
    return [int(np.prod(sizes[i + 1 :])) for i in range(len(sizes))]


def shift(value, sizes, axis, amount):
    size, stride = sizes[axis], strides_of(sizes)[axis]
    pairs = []
    for source in range(int(np.prod(sizes))):
        at = (source // stride) % size
        pairs.append((source, source + ((at + amount) % size - at) * stride))
    return lax.ppermute(value, "dp", pairs)


def coordinate(me, sizes, axis):
    return lax.rem(lax.div(me, strides_of(sizes)[axis]), sizes[axis])


def gather_pieces(rows, sizes, order):
    line = [rows] + [shift(rows, sizes, 0, k) for k in range(1, sizes[0])]
    pieces = [(jnp.concatenate(line, 0), tuple(0 for _ in sizes))]
    for axis in order:
        grown = list(pieces)
        for k in range(1, sizes[axis]):
            for piece, back in pieces:
                moved = tuple(k if i == axis else b for i, b in enumerate(back))
                grown.append((shift(piece, sizes, axis, k), moved))
        pieces = grown
    return [piece for piece, _ in pieces], [back for _, back in pieces]


def gather_stack(value, sizes, order):
    for axis in order:
        moved = [value] + [shift(value, sizes, axis, k) for k in range(1, sizes[axis])]
        value = jnp.stack(moved) if len(moved) > 1 else value[None]
    return value


def slot_order(per_token, sizes):
    rest = int(np.prod(sizes[1:]))
    return per_token.reshape(sizes[0], rest, -1).transpose(1, 0, 2).reshape(-1)


def exchange(blocks, groups=None):
    return lax.all_to_all(
        blocks, "dp", split_axis=0, concat_axis=0, axis_index_groups=groups, tiled=True
    )


def transposed_dot(left, right, precision=None):
    return lax.dot_general(
        left, right, (((1,), (1,)), ((), ())), precision=precision, preferred_element_type=F32
    )


def place_pieces(pieces, backs, sizes, into):
    me = lax.axis_index("dp")
    rows = pieces[0].shape[0]
    for piece, back in zip(pieces, backs):
        slot = 0
        for axis in range(1, len(sizes)):
            at = coordinate(me, sizes, axis) + sizes[axis] - back[axis]
            slot = slot * sizes[axis] + lax.rem(at, sizes[axis])
        into[pl.ds(pl.multiple_of(slot * rows, rows), rows), :] = piece[...]


def stream_products(weights, tokens, sums, buffers, arrived):
    depth, chunk = buffers.shape[0], buffers.shape[3]
    steps = tokens.shape[1] // chunk

    def copy(step, w):
        slot = lax.rem(step, depth)
        columns = pl.ds(pl.multiple_of(step * chunk, chunk), chunk)
        return pltpu.make_async_copy(
            weights[w].at[:, columns], buffers.at[slot, w], arrived.at[slot, w]
        )

    def fetch():
        for step in range(min(depth, steps)):
            for w in range(len(weights)):
                copy(step, w).start()

    def run():
        @pl.loop(0, steps)
        def _(step):
            columns = pl.ds(pl.multiple_of(step * chunk, chunk), chunk)
            for w in range(len(weights)):
                copy(step, w).wait()
                sums[w] += transposed_dot(buffers[lax.rem(step, depth), w], tokens[:, columns])

                @pl.when(step + depth < steps)
                def _():
                    copy(step + depth, w).start()

    return fetch, run


def model_side(proj, tokens, model_cols):
    window = proj.shape[1]
    start = lax.div(lax.axis_index("dp") * model_cols, window) * window
    columns = pl.ds(pl.multiple_of(start, window), window)
    return transposed_dot(proj, tokens[:, columns])


def input_kernel(backs, sizes, model_cols, *refs):
    pieces, refs = refs[: len(backs)], refs[len(backs) :]
    proj, w_gate, w_up, sums, right, tokens, buffers, arrived = refs
    fetch, run = stream_products((w_gate, w_up), tokens, sums, buffers, arrived)
    fetch()
    place_pieces(pieces, backs, sizes, tokens)
    sums[...] = jnp.zeros_like(sums)
    right[...] = model_side(proj[: right.shape[0], :], tokens, model_cols)
    run()


def gradient_kernel(backs, sizes, model_cols, *refs):
    pieces, refs = refs[: len(backs)], refs[len(backs) :]
    forward, right, proj, proj_h, w_down, out, sums, tokens, stacked, buffers, arrived = refs
    fetch, run = stream_products((w_down,), tokens, sums, buffers, arrived)
    fetch()
    place_pieces(pieces, backs, sizes, tokens)
    sums[...] = jnp.zeros_like(sums)
    rank = proj.shape[0] // 3
    last = model_side(proj[2 * rank :, :], tokens, model_cols)
    run()
    hidden_units, count = sums.shape[1:]
    tile = 128 if hidden_units % 128 == 0 else 32

    @pl.loop(0, hidden_units // tile)
    def _(step):
        rows = pl.ds(pl.multiple_of(step * tile, tile), tile)
        grad, gate_value, up_value = sums[0, rows, :], forward[0, rows, :], forward[1, rows, :]
        s = 1.0 / (1.0 + jnp.exp(-gate_value))
        silu = gate_value * s
        stacked[0, rows, :] = (
            grad * up_value * s * (1.0 + gate_value * (1.0 - s))
        ).astype(BF16)
        stacked[1, rows, :] = (grad * silu).astype(BF16)
        stacked[2, rows, :] = (silu * up_value).astype(BF16)

    sides = [
        jnp.dot(proj_h[p * rank : (p + 1) * rank, :], stacked[k], preferred_element_type=F32)
        for k, p in enumerate((1, 2, 0))
    ]
    every = jnp.concatenate(sides + [right[...], last], 0)
    size, each = sizes[0], count // int(np.prod(sizes))
    line = size * each
    source = lax.broadcasted_iota(jnp.int32, (count, count), 0)
    target = lax.broadcasted_iota(jnp.int32, (count, count), 1)
    back = lax.rem(lax.div(source, each), size)
    at = lax.rem(coordinate(lax.axis_index("dp"), sizes, 0) + size - back, size)
    place = lax.div(source, line) * line + at * each + lax.rem(source, each)
    order = (place == target).astype(F32)
    out[...] = jnp.dot(every, order, precision=HIGHEST, preferred_element_type=F32).reshape(
        out.shape
    )


def kernel_options(weights, tokens):
    hidden, width = weights[0].shape
    return dict(
        compiler_params=pltpu.CompilerParams(vmem_limit_bytes=44 * 2**20),
        cost_estimate=pl.CostEstimate(
            flops=2 * len(weights) * hidden * width * tokens,
            bytes_accessed=2 * len(weights) * hidden * width,
            transcendentals=hidden * tokens,
        ),
    )


def stream_scratch(weights, tokens, depth):
    hidden, width = weights[0].shape
    chunk = min(width, 1024)
    return [
        pltpu.VMEM((tokens, width), BF16),
        pltpu.VMEM((depth, len(weights), hidden, chunk), BF16),
        pltpu.SemaphoreType.DMA((depth, len(weights))),
    ]


def input_products(pieces, backs, sizes, model_cols, proj, weights):
    hidden = weights[0].shape[0]
    tokens = pieces[0].shape[0] * len(pieces)
    return pl.pallas_call(
        functools.partial(input_kernel, backs, sizes, model_cols),
        out_shape=(
            jax.ShapeDtypeStruct((2, hidden, tokens), F32),
            jax.ShapeDtypeStruct((proj.shape[0] // 3 * 2, tokens), F32),
        ),
        in_specs=[VMEM] * (len(pieces) + 1) + [ANY] * 2,
        out_specs=(VMEM, VMEM),
        scratch_shapes=stream_scratch(weights, tokens, 2),
        name="input_products",
        **kernel_options(weights, tokens),
    )(*pieces, proj, *weights)


def gradient_products(pieces, backs, sizes, model_cols, forward, right, proj, proj_h, w_down):
    hidden = w_down.shape[0]
    tokens = pieces[0].shape[0] * len(pieces)
    rest = int(np.prod(sizes[1:]))
    scratch = stream_scratch((w_down,), tokens, 4)
    return pl.pallas_call(
        functools.partial(gradient_kernel, backs, sizes, model_cols),
        out_shape=jax.ShapeDtypeStruct((rest, 2 * proj.shape[0] // rest, tokens), F32),
        in_specs=[VMEM] * (len(pieces) + 4) + [ANY],
        out_specs=VMEM,
        scratch_shapes=[pltpu.VMEM((1, hidden, tokens), F32), scratch[0]]
        + [pltpu.VMEM((3, hidden, tokens), BF16)]
        + scratch[1:],
        name="gradient_products",
        **kernel_options((w_down,), tokens),
    )(*pieces, forward, right, proj, proj_h, w_down)


def sum_kernel(values, out):
    total = jnp.sum(values[...], 0)
    out[...] = jnp.broadcast_to(total[None], out.shape)


def sum_copies(values, copies):
    return pl.pallas_call(
        sum_kernel,
        out_shape=jax.ShapeDtypeStruct((copies,) + values.shape[1:], F32),
        in_specs=[VMEM],
        out_specs=VMEM,
        name="sum_copies",
    )(values)


def halves(value):
    high = value.astype(BF16)
    return high, (value - high.astype(F32)).astype(BF16)


def sketch_kernel(sizes, order, vectors, means, ids, sketches, scores, lefts, turned):
    count = int(np.prod(sizes))
    rank = sketches.shape[2]
    tokens = ids.shape[1]
    own_rank = means.shape[2] // rank
    every = vectors[...].reshape(6 * rank, tokens)
    onehot = (ids[...] == lax.broadcasted_iota(jnp.int32, (SEQS, tokens), 0)).astype(F32)
    masks = jnp.concatenate([onehot.astype(BF16)] * 3, 1)
    norm = jnp.zeros((SEQS, 1), F32)
    if own_rank * count > rank:
        lefts[...] = jnp.zeros_like(lefts)
    for k in range(3):
        left = every[k * rank : (k + 1) * rank]
        right = every[(3 + k) * rank : (4 + k) * rank]
        left_high, left_low = halves(left)
        right_high, right_low = halves(right)
        left_three = jnp.concatenate([left_high, left_high, left_low], 1)
        right_three = jnp.concatenate([right_high, right_low, right_high], 1)
        rows = jnp.concatenate([left_three * masks[s : s + 1, :] for s in range(SEQS)], 0)
        sketch = transposed_dot(rows, right_three).reshape(SEQS, rank, rank)
        sketches[:, k] = sketch
        norm += jnp.sum(jnp.sum(sketch * sketch, 1), 1, keepdims=True)

        for i in range(own_rank):
            part = left[i * count : (i + 1) * count]
            lefts[k, : part.shape[0], i * tokens : (i + 1) * tokens] = part
        mean = means[:, k * DOMAINS : (k + 1) * DOMAINS, :].reshape(-1, own_rank * rank)
        result = 0.0
        for part in (right_high, right_low):
            empty = jnp.zeros_like(part)
            wide = jnp.concatenate(
                [
                    jnp.concatenate([part if i == c else empty for c in range(own_rank)], 1)
                    for i in range(own_rank)
                ],
                0,
            )
            result += jnp.dot(mean, wide, preferred_element_type=F32)
        turned[k] = result.reshape(count, DOMAINS, own_rank * tokens)

    me = lax.axis_index("dp")

    def add(device, total):
        place, step = 0, 1
        for axis in order:
            size = sizes[axis]
            back = coordinate(me, sizes, axis) + size - coordinate(device, sizes, axis)
            place += lax.rem(back, size) * step
            step *= size
        for k in range(3):
            total += turned[k, place] * lefts[k, pl.ds(device, 1), :]
        return total

    total = lax.fori_loop(0, count, add, jnp.zeros((DOMAINS, own_rank * tokens), F32))
    total = sum(total[:, i * tokens : (i + 1) * tokens] for i in range(own_rank))
    scores[...] = transposed_dot(onehot, total, HIGHEST) * lax.rsqrt(norm + 1e-06)


def on_device(
    count,
    activations,
    cotangent,
    w_gate,
    w_up,
    w_down,
    proj_model,
    proj_hidden,
    seq_ids,
    targets,
    target_domain,
):
    sizes = axis_sizes(count)
    rank = proj_model.shape[1] // 3
    model_cols = proj_model.shape[0]
    own_rank = -(-rank // count)
    padded = own_rank * count
    tokens = count * activations.shape[0]
    examples = targets.shape[0]
    inner = list(range(1, len(sizes)))
    flipped = inner[:-1][::-1] + inner[-1:]

    in_pieces, in_backs = gather_pieces(activations, sizes, flipped)
    out_pieces, out_backs = gather_pieces(cotangent, sizes, inner)

    cut = jnp.pad(targets, ((0, 0), (0, 0), (0, padded - rank), (0, 0)))
    cut = cut.reshape(examples, 3, own_rank, count, rank).transpose(3, 0, 1, 2, 4)
    entries = 3 * own_rank * rank
    cut = cut.reshape(count, examples, entries)
    tags = jnp.broadcast_to(target_domain.astype(BF16)[None, :, None], (count, examples, 128))
    sent, _ = lax.optimization_barrier((jnp.concatenate([cut, tags], 2), in_pieces[1]))
    held = exchange(sent).reshape(count * examples, -1)
    domains = held[:, -1].astype(F32)
    domain_onehot = (domains[None, :] == jnp.arange(DOMAINS, dtype=F32)[:, None]).astype(BF16)
    domain_sum = jnp.dot(domain_onehot, held[:, :entries], preferred_element_type=F32)
    domain_count = jnp.sum(domain_onehot.astype(F32), 1)
    mean = (domain_sum / domain_count[:, None]).astype(BF16)
    mean = mean.reshape(DOMAINS, 3, own_rank * rank).transpose(1, 0, 2)
    mean_order = [0] + flipped
    means = gather_stack(mean.reshape(3 * DOMAINS, -1), sizes, mean_order)
    means = means.reshape((count,) + means.shape[-2:])

    window = max(model_cols, 128)
    proj_m = proj_model.T
    if window > model_cols:
        at = lax.rem(lax.axis_index("dp"), window // model_cols)
        spots = [
            jnp.where(at == i, proj_m, jnp.zeros_like(proj_m)) for i in range(window // model_cols)
        ]
        proj_m = jnp.concatenate(spots, 1)

    forward, right = input_products(
        in_pieces, in_backs, sizes, model_cols, proj_m, (w_gate, w_up)
    )
    vectors = gradient_products(
        out_pieces, out_backs, sizes, model_cols, forward, right, proj_m, proj_hidden.T, w_down
    )
    first, rest = sizes[0], count // sizes[0]
    planes = [[z * rest + r for r in range(rest)] for z in range(first)]
    lines = [[z * rest + r for z in range(first)] for r in range(rest)]
    vectors = sum_copies(exchange(vectors, planes), first)
    vectors = sum_copies(exchange(vectors, lines), rest)
    vectors = exchange(vectors, planes)

    return pl.pallas_call(
        functools.partial(sketch_kernel, sizes, mean_order),
        out_shape=(
            jax.ShapeDtypeStruct((SEQS, 3, rank, rank), F32),
            jax.ShapeDtypeStruct((SEQS, DOMAINS), F32),
        ),
        in_specs=[VMEM] * 3,
        out_specs=(VMEM, VMEM),
        scratch_shapes=[
            pltpu.VMEM((3, count, own_rank * tokens), F32),
            pltpu.VMEM((3, count, DOMAINS, own_rank * tokens), F32),
        ],
        compiler_params=pltpu.CompilerParams(vmem_limit_bytes=52 * 2**20),
        name="sketches",
    )(vectors, means, slot_order(seq_ids, sizes)[None, :])


def solution(mesh):
    in_specs = (
        P(("groups", "dp"), None),
        P(("groups", "dp"), None),
        P("dp", None),
        P("dp", None),
        P("dp", None),
        P("dp", None),
        P("dp", None),
        P("groups"),
        P(("groups", "dp"), None, None, None),
        P(("groups", "dp")),
    )
    out_specs = (P("groups", None, None, None), P("groups", None))
    return jax.shard_map(
        functools.partial(on_device, mesh.shape["dp"]),
        mesh=mesh,
        in_specs=in_specs,
        out_specs=out_specs,
        check_vma=False,
    )
```

```python
import functools

import jax
import jax.numpy as jnp
import numpy as np
from jax import lax
from jax.experimental import pallas as pl
from jax.experimental.pallas import tpu as pltpu
from jax.sharding import PartitionSpec as P

DOMAINS = 32
SEQS = 16
HIGHEST = lax.Precision.HIGHEST
F32 = jnp.float32
BF16 = jnp.bfloat16
VMEM = pl.BlockSpec(memory_space=pltpu.VMEM)
ANY = pl.BlockSpec(memory_space=pl.ANY)


def axis_sizes(count):
    if count == 32:
        return (4, 2, 2, 2)
    if count == 128:
        return (8, 8, 2)
    return (count, 1)


def strides_of(sizes):
    return [int(np.prod(sizes[i + 1 :])) for i in range(len(sizes))]


def shift(value, sizes, axis, amount):
    size, stride = sizes[axis], strides_of(sizes)[axis]
    pairs = []
    for source in range(int(np.prod(sizes))):
        at = (source // stride) % size
        pairs.append((source, source + ((at + amount) % size - at) * stride))
    return lax.ppermute(value, "dp", pairs)


def coordinate(me, sizes, axis):
    return lax.rem(lax.div(me, strides_of(sizes)[axis]), sizes[axis])


def gather_pieces(rows, sizes, order):
    line = [rows] + [shift(rows, sizes, 0, k) for k in range(1, sizes[0])]
    pieces = [(jnp.concatenate(line, 0), tuple(0 for _ in sizes))]
    for axis in order:
        grown = list(pieces)
        for k in range(1, sizes[axis]):
            for piece, back in pieces:
                moved = tuple(k if i == axis else b for i, b in enumerate(back))
                grown.append((shift(piece, sizes, axis, k), moved))
        pieces = grown
    return [piece for piece, _ in pieces], [back for _, back in pieces]


def slot_order(per_token, sizes):
    rest = int(np.prod(sizes[1:]))
    return per_token.reshape(sizes[0], rest, -1).transpose(1, 0, 2).reshape(-1)


def exchange(blocks, groups=None):
    return lax.all_to_all(
        blocks, "dp", split_axis=0, concat_axis=0, axis_index_groups=groups, tiled=True
    )


def transposed_dot(left, right, precision=None):
    return lax.dot_general(
        left, right, (((1,), (1,)), ((), ())), precision=precision, preferred_element_type=F32
    )


def place_pieces(pieces, backs, sizes, into):
    me = lax.axis_index("dp")
    rows = pieces[0].shape[0]
    for piece, back in zip(pieces, backs):
        slot = 0
        for axis in range(1, len(sizes)):
            at = coordinate(me, sizes, axis) + sizes[axis] - back[axis]
            slot = slot * sizes[axis] + lax.rem(at, sizes[axis])
        into[pl.ds(pl.multiple_of(slot * rows, rows), rows), :] = piece[...]


def model_side(proj, tokens, model_cols):
    window = proj.shape[1]
    start = lax.div(lax.axis_index("dp") * model_cols, window) * window
    columns = pl.ds(pl.multiple_of(start, window), window)
    return transposed_dot(proj, tokens[:, columns])


def product_kernel(backs, sizes, model_cols, *refs):
    pieces, refs = refs[: len(backs[0])], refs[len(backs[0]) :]
    out_pieces, refs = refs[: len(backs[1])], refs[len(backs[1]) :]
    proj, proj_h, w_gate, w_up, w_down, out, sums, tokens, stacked, buffers, arrived = refs
    weights, sides = (w_gate, w_up, w_down), (0, 0, 1)
    depth, chunk = buffers.shape[0], buffers.shape[3]
    steps = tokens.shape[2] // chunk

    def copy(step, w):
        slot = lax.rem(step, depth)
        columns = pl.ds(pl.multiple_of(step * chunk, chunk), chunk)
        return pltpu.make_async_copy(
            weights[w].at[:, columns], buffers.at[slot, w], arrived.at[slot, w]
        )

    for step in range(min(depth, steps)):
        for w in range(3):
            copy(step, w).start()
    place_pieces(pieces, backs[0], sizes, tokens.at[0])
    place_pieces(out_pieces, backs[1], sizes, tokens.at[1])
    sums[...] = jnp.zeros_like(sums)
    rank = proj.shape[0] // 3
    right = [
        model_side(proj[: 2 * rank, :], tokens.at[0], model_cols),
        model_side(proj[2 * rank :, :], tokens.at[1], model_cols),
    ]

    @pl.loop(0, steps)
    def _(step):
        columns = pl.ds(pl.multiple_of(step * chunk, chunk), chunk)
        for w in range(3):
            copy(step, w).wait()
            sums[w] += transposed_dot(
                buffers[lax.rem(step, depth), w], tokens[sides[w], :, columns]
            )

            @pl.when(step + depth < steps)
            def _():
                copy(step + depth, w).start()

    hidden_units, count = sums.shape[1:]
    tile = 128 if hidden_units % 128 == 0 else 32

    @pl.loop(0, hidden_units // tile)
    def _(step):
        rows = pl.ds(pl.multiple_of(step * tile, tile), tile)
        gate_value, up_value, grad = sums[0, rows, :], sums[1, rows, :], sums[2, rows, :]
        s = 1.0 / (1.0 + jnp.exp(-gate_value))
        silu = gate_value * s
        stacked[0, rows, :] = (
            grad * up_value * s * (1.0 + gate_value * (1.0 - s))
        ).astype(BF16)
        stacked[1, rows, :] = (grad * silu).astype(BF16)
        stacked[2, rows, :] = (silu * up_value).astype(BF16)

    sides = [
        jnp.dot(proj_h[p * rank : (p + 1) * rank, :], stacked[k], preferred_element_type=F32)
        for k, p in enumerate((1, 2, 0))
    ]
    every = jnp.concatenate(sides + right, 0)
    size, each = sizes[0], count // int(np.prod(sizes))
    line = size * each
    source = lax.broadcasted_iota(jnp.int32, (count, count), 0)
    target = lax.broadcasted_iota(jnp.int32, (count, count), 1)
    back = lax.rem(lax.div(source, each), size)
    at = lax.rem(coordinate(lax.axis_index("dp"), sizes, 0) + size - back, size)
    place = lax.div(source, line) * line + at * each + lax.rem(source, each)
    order = (place == target).astype(F32)
    every = jnp.dot(every, order, precision=HIGHEST, preferred_element_type=F32)
    used = every.shape[0] // out.shape[1]
    out[:used] = every.reshape((used,) + out.shape[1:])
    if used < out.shape[0]:
        out[used:] = jnp.zeros_like(out[used:])


def products(in_pieces, out_pieces, backs, sizes, proj, proj_h, w_gate, w_up, w_down):
    hidden, width = w_gate.shape
    count = int(np.prod(sizes))
    tokens = in_pieces[0].shape[0] * len(in_pieces)
    model_cols = width // count
    chunk = min(width, 1024)
    height = 8 * -(-2 * proj.shape[0] // (8 * count))
    return pl.pallas_call(
        functools.partial(product_kernel, backs, sizes, model_cols),
        out_shape=jax.ShapeDtypeStruct((count, height, tokens), F32),
        in_specs=[VMEM] * (len(in_pieces) + len(out_pieces) + 2) + [ANY] * 3,
        out_specs=VMEM,
        scratch_shapes=[
            pltpu.VMEM((3, hidden, tokens), F32),
            pltpu.VMEM((2, tokens, width), BF16),
            pltpu.VMEM((3, hidden, tokens), BF16),
            pltpu.VMEM((2, 3, hidden, chunk), BF16),
            pltpu.SemaphoreType.DMA((2, 3)),
        ],
        compiler_params=pltpu.CompilerParams(vmem_limit_bytes=44 * 2**20),
        cost_estimate=pl.CostEstimate(
            flops=6 * hidden * width * tokens,
            bytes_accessed=6 * hidden * width,
            transcendentals=hidden * tokens,
        ),
        name="products",
    )(*in_pieces, *out_pieces, proj, proj_h, w_gate, w_up, w_down)


def sum_kernel(values, out):
    total = jnp.sum(values[...], 0)
    out[...] = jnp.broadcast_to(total[None], out.shape)


def sum_copies(values):
    return pl.pallas_call(
        sum_kernel,
        out_shape=jax.ShapeDtypeStruct(values.shape, F32),
        in_specs=[VMEM],
        out_specs=VMEM,
        name="sum_copies",
    )(values)


def halves(value):
    high = value.astype(BF16)
    return high, (value - high.astype(F32)).astype(BF16)


def rows_of(vectors, rank):
    height, tokens = vectors.shape[1:]
    return vectors[: 6 * rank // height].reshape(6 * rank, tokens)


def onehot_of(ids, tokens):
    return (ids == lax.broadcasted_iota(jnp.int32, (SEQS, tokens), 0)).astype(F32)


def target_kernel(rank, vectors, ids, targets, domains, out):
    tokens = ids.shape[1]
    examples = targets.shape[0]
    every = rows_of(vectors, rank)
    total = jnp.zeros((examples, tokens), F32)
    for k in range(3):
        left = every[k * rank : (k + 1) * rank]
        target = targets[:, k].reshape(examples * rank, rank)
        turned = sum(
            jnp.dot(target, part, preferred_element_type=F32)
            for part in halves(every[(3 + k) * rank : (4 + k) * rank])
        )
        total += jnp.sum(turned.reshape(examples, rank, tokens) * left[None], 1)
    scores = transposed_dot(total, onehot_of(ids[...], tokens), HIGHEST)
    parts = [scores, domains[...].astype(F32), jnp.ones((examples, 1), F32)]
    rest = out.shape[2] - SEQS - 2
    parts = jnp.concatenate(parts + [jnp.zeros((examples, rest), F32)], 1)
    out[...] = jnp.broadcast_to(parts[None], out.shape)


def sketch_kernel(rank, vectors, ids, sketches, norms):
    tokens = ids.shape[1]
    every = rows_of(vectors, rank)
    masks = jnp.concatenate([onehot_of(ids[...], tokens).astype(BF16)] * 3, 1)
    norm = jnp.zeros((SEQS, 1), F32)
    for k in range(3):
        left_high, left_low = halves(every[k * rank : (k + 1) * rank])
        right_high, right_low = halves(every[(3 + k) * rank : (4 + k) * rank])
        left = jnp.concatenate([left_high, left_high, left_low], 1)
        right = jnp.concatenate([right_high, right_low, right_high], 1)
        rows = jnp.concatenate([left * masks[s : s + 1, :] for s in range(SEQS)], 0)
        sketch = transposed_dot(rows, right).reshape(SEQS, rank, rank)
        sketches[:, k] = sketch
        norm += jnp.sum(jnp.sum(sketch * sketch, 1), 1, keepdims=True)
    norms[...] = jnp.broadcast_to(norm, norms.shape)


def score_kernel(parts, norms, scores):
    every = parts[...].reshape(-1, parts.shape[2])
    domain = lax.broadcasted_iota(jnp.int32, (every.shape[0], DOMAINS), 1).astype(F32)
    onehot = (every[:, SEQS : SEQS + 1] == domain).astype(F32)
    total = lax.dot_general(
        every, onehot, (((0,), (0,)), ((), ())), precision=HIGHEST, preferred_element_type=F32
    )
    mean = total[:SEQS] / total[SEQS + 1 : SEQS + 2]
    scores[...] = mean * lax.rsqrt(norms[:, :DOMAINS] + 1e-06)


def on_device(
    count,
    activations,
    cotangent,
    w_gate,
    w_up,
    w_down,
    proj_model,
    proj_hidden,
    seq_ids,
    targets,
    target_domain,
):
    sizes = axis_sizes(count)
    rank = proj_model.shape[1] // 3
    model_cols = proj_model.shape[0]
    tokens = count * activations.shape[0]
    examples = targets.shape[0]
    inner = list(range(1, len(sizes)))
    flipped = inner[:-1][::-1] + inner[-1:]

    in_pieces, in_backs = gather_pieces(activations, sizes, flipped)
    out_pieces, out_backs = gather_pieces(cotangent, sizes, inner)

    window = max(model_cols, 128)
    proj_m = proj_model.T
    if window > model_cols:
        at = lax.rem(lax.axis_index("dp"), window // model_cols)
        spots = [
            jnp.where(at == i, proj_m, jnp.zeros_like(proj_m)) for i in range(window // model_cols)
        ]
        proj_m = jnp.concatenate(spots, 1)

    vectors = products(
        in_pieces,
        out_pieces,
        (in_backs, out_backs),
        sizes,
        proj_m,
        proj_hidden.T,
        w_gate,
        w_up,
        w_down,
    )
    vectors = exchange(sum_copies(exchange(vectors)))

    ids = slot_order(seq_ids, sizes)[None, :]
    parts = pl.pallas_call(
        functools.partial(target_kernel, rank),
        out_shape=jax.ShapeDtypeStruct((count, examples, 128), F32),
        in_specs=[VMEM] * 4,
        out_specs=VMEM,
        compiler_params=pltpu.CompilerParams(vmem_limit_bytes=32 * 2**20),
        name="target_products",
    )(vectors, ids, targets, target_domain[:, None])
    parts, vectors = lax.optimization_barrier((parts, vectors))
    parts = exchange(parts)
    sketches, norms = pl.pallas_call(
        functools.partial(sketch_kernel, rank),
        out_shape=(
            jax.ShapeDtypeStruct((SEQS, 3, rank, rank), F32),
            jax.ShapeDtypeStruct((SEQS, 128), F32),
        ),
        in_specs=[VMEM] * 2,
        out_specs=(VMEM, VMEM),
        compiler_params=pltpu.CompilerParams(vmem_limit_bytes=40 * 2**20),
        name="sketches",
    )(vectors, ids)
    scores = pl.pallas_call(
        score_kernel,
        out_shape=jax.ShapeDtypeStruct((SEQS, DOMAINS), F32),
        in_specs=[VMEM] * 2,
        out_specs=VMEM,
        name="scores",
    )(parts, norms)
    return sketches, scores


def solution(mesh):
    in_specs = (
        P(("groups", "dp"), None),
        P(("groups", "dp"), None),
        P("dp", None),
        P("dp", None),
        P("dp", None),
        P("dp", None),
        P("dp", None),
        P("groups"),
        P(("groups", "dp"), None, None, None),
        P(("groups", "dp")),
    )
    out_specs = (P("groups", None, None, None), P("groups", None))
    return jax.shard_map(
        functools.partial(on_device, mesh.shape["dp"]),
        mesh=mesh,
        in_specs=in_specs,
        out_specs=out_specs,
        check_vma=False,
    )
```

```python
import functools

import jax
import jax.numpy as jnp
import numpy as np
from jax import lax
from jax.experimental import pallas as pl
from jax.experimental.pallas import tpu as pltpu
from jax.sharding import PartitionSpec as P

DOMAINS = 32
SEQS = 16
HIGHEST = lax.Precision.HIGHEST
F32 = jnp.float32
BF16 = jnp.bfloat16
VMEM = pl.BlockSpec(memory_space=pltpu.VMEM)
HBM = pl.BlockSpec(memory_space=pltpu.HBM)


def axis_sizes(count):
    if count == 32:
        return (4, 2, 2, 2)
    if count == 128:
        return (8, 8, 2)
    return (count, 1)


def strides_of(sizes):
    return [int(np.prod(sizes[i + 1 :])) for i in range(len(sizes))]


def shift(value, sizes, axis, amount):
    size, stride = sizes[axis], strides_of(sizes)[axis]
    pairs = []
    for source in range(int(np.prod(sizes))):
        at = (source // stride) % size
        pairs.append((source, source + ((at + amount) % size - at) * stride))
    return lax.ppermute(value, "dp", pairs)


def coordinate(me, sizes, axis):
    return lax.rem(lax.div(me, strides_of(sizes)[axis]), sizes[axis])


def gather_rows(rows, sizes, order):
    backs = [tuple(0 for _ in sizes)]

    def moved(axis, amount):
        return [tuple(amount if i == axis else b for i, b in enumerate(back)) for back in backs]

    def received(piece, axis):
        return [shift(piece, sizes, axis, k) for k in range(1, sizes[axis])]

    piece = lax.optimization_barrier(jnp.concatenate([rows] + received(rows, 0), 0))
    for axis in order[:-1]:
        piece = jnp.concatenate([piece] + received(piece, axis), 0)
        backs = sum([moved(axis, k) for k in range(1, sizes[axis])], backs)
    pieces = [(piece, backs)]
    for axis in order[-1:]:
        others = zip(received(piece, axis), range(1, sizes[axis]))
        pieces += [(other, moved(axis, k)) for other, k in others]
    core = len(sizes) - 1
    for piece, backs in list(pieces):
        others = zip(received(piece, core), range(1, sizes[core]))
        pieces += [(other, moved(core, k)) for other, k in others]
    return [piece for piece, _ in pieces], [backs for _, backs in pieces]


def slot_order(per_token, sizes):
    rest = int(np.prod(sizes[1:]))
    return per_token.reshape(sizes[0], rest, -1).transpose(1, 0, 2).reshape(-1)


def exchange(blocks, groups=None):
    return lax.all_to_all(
        blocks, "dp", split_axis=0, concat_axis=0, axis_index_groups=groups, tiled=True
    )


def transposed_dot(left, right, precision=None):
    return lax.dot_general(
        left, right, (((1,), (1,)), ((), ())), precision=precision, preferred_element_type=F32
    )


def place_pieces(pieces, backs, sizes, into):
    me = lax.axis_index("dp")
    for piece, lines in zip(pieces, backs):
        rows = piece.shape[0] // len(lines)
        for i, back in enumerate(lines):
            slot = 0
            for axis in range(1, len(sizes)):
                at = coordinate(me, sizes, axis) + sizes[axis] - back[axis]
                slot = slot * sizes[axis] + lax.rem(at, sizes[axis])
            start = pl.multiple_of(slot * rows, rows)
            into[pl.ds(start, rows), :] = piece[i * rows : (i + 1) * rows, :]


def model_side(proj, tokens, model_cols):
    window = proj.shape[1]
    start = lax.div(lax.axis_index("dp") * model_cols, window) * window
    columns = pl.ds(pl.multiple_of(start, window), window)
    return transposed_dot(proj, tokens[:, columns])


def product_kernel(backs, sizes, model_cols, *refs):
    pieces, refs = refs[: len(backs[0])], refs[len(backs[0]) :]
    out_pieces, refs = refs[: len(backs[1])], refs[len(backs[1]) :]
    proj, *weights, out, sums, tokens, stacked, buffers, arrived = refs
    sides = (0, 0, 1)
    depth, _, block, chunk = buffers.shape
    hidden_units, count = sums.shape[1:]
    steps = tokens.shape[2] // chunk
    total = steps * (hidden_units // block)

    def places(step):
        rows = pl.ds(pl.multiple_of(lax.div(step, steps) * block, block), block)
        return rows, pl.ds(pl.multiple_of(lax.rem(step, steps) * chunk, chunk), chunk)

    def copy(step, w):
        slot = lax.rem(step, depth)
        return pltpu.make_async_copy(
            weights[w].at[places(step)], buffers.at[slot, w], arrived.at[slot, w]
        )

    for step in range(min(depth, total)):
        for w in range(3):
            copy(step, w).start()
    place_pieces(pieces, backs[0], sizes, tokens.at[0])
    place_pieces(out_pieces, backs[1], sizes, tokens.at[1])
    sums[...] = jnp.zeros_like(sums)

    @pl.loop(0, total)
    def _(step):
        rows, columns = places(step)
        for w in range(3):
            copy(step, w).wait()
            sums[w, rows, :] += transposed_dot(
                buffers[lax.rem(step, depth), w], tokens[sides[w], :, columns]
            )

            @pl.when(step + depth < total)
            def _():
                copy(step + depth, w).start()

    rank = proj.shape[0] // 3
    window = proj.shape[1] - hidden_units
    right = [
        model_side(proj[: 2 * rank, :window], tokens.at[0], model_cols),
        model_side(proj[2 * rank :, :window], tokens.at[1], model_cols),
    ]
    tile = 128 if hidden_units % 128 == 0 else 32

    @pl.loop(0, hidden_units // tile)
    def _(step):
        rows = pl.ds(pl.multiple_of(step * tile, tile), tile)
        gate_value, up_value, grad = sums[0, rows, :], sums[1, rows, :], sums[2, rows, :]
        s = 1.0 / (1.0 + jnp.exp(-gate_value))
        silu = gate_value * s
        stacked[0, rows, :] = (
            grad * up_value * s * (1.0 + gate_value * (1.0 - s))
        ).astype(BF16)
        stacked[1, rows, :] = (grad * silu).astype(BF16)
        stacked[2, rows, :] = (silu * up_value).astype(BF16)

    sides = [
        jnp.dot(proj[p * rank : (p + 1) * rank, window:], stacked[k], preferred_element_type=F32)
        for k, p in enumerate((1, 2, 0))
    ]
    every = jnp.concatenate(sides + right, 0)
    size, each = sizes[0], count // int(np.prod(sizes))
    line = size * each
    source = lax.broadcasted_iota(jnp.int32, (count, count), 0)
    target = lax.broadcasted_iota(jnp.int32, (count, count), 1)
    back = lax.rem(lax.div(source, each), size)
    at = lax.rem(coordinate(lax.axis_index("dp"), sizes, 0) + size - back, size)
    place = lax.div(source, line) * line + at * each + lax.rem(source, each)
    order = (place == target).astype(F32)
    every = jnp.dot(every, order, precision=HIGHEST, preferred_element_type=F32)
    used = every.shape[0] // out.shape[1]
    out[:used] = every.reshape((used,) + out.shape[1:])
    if used < out.shape[0]:
        out[used:] = jnp.zeros_like(out[used:])


def products(in_pieces, out_pieces, backs, sizes, proj, w_gate, w_up, w_down):
    hidden, width = w_gate.shape
    count = int(np.prod(sizes))
    tokens = sum(piece.shape[0] for piece in in_pieces)
    model_cols = width // count
    chunk = min(width, 2048)
    block = hidden // 2 if hidden % 32 == 0 and hidden > 256 else hidden
    height = 8 * -(-2 * proj.shape[0] // (8 * count))
    return pl.pallas_call(
        functools.partial(product_kernel, backs, sizes, model_cols),
        out_shape=jax.ShapeDtypeStruct((count, height, tokens), F32),
        in_specs=[VMEM] * (len(in_pieces) + len(out_pieces) + 1) + [HBM] * 3,
        out_specs=VMEM,
        scratch_shapes=[
            pltpu.VMEM((3, hidden, tokens), F32),
            pltpu.VMEM((2, tokens, width), BF16),
            pltpu.VMEM((3, hidden, tokens), BF16),
            pltpu.VMEM((2, 3, block, chunk), BF16),
            pltpu.SemaphoreType.DMA((2, 3)),
        ],
        compiler_params=pltpu.CompilerParams(vmem_limit_bytes=44 * 2**20),
        cost_estimate=pl.CostEstimate(
            flops=6 * hidden * width * tokens,
            bytes_accessed=6 * hidden * width,
            transcendentals=hidden * tokens,
        ),
        name="products",
    )(*in_pieces, *out_pieces, proj, w_gate, w_up, w_down)


def small_kernel(megabytes):
    return pltpu.CompilerParams(vmem_limit_bytes=megabytes * 2**20)


def sum_kernel(values, out):
    total = values[0]
    for i in range(1, values.shape[0]):
        total += values[i]
    for i in range(out.shape[0]):
        out[i] = total


def sum_copies(values):
    return pl.pallas_call(
        sum_kernel,
        out_shape=jax.ShapeDtypeStruct(values.shape, F32),
        in_specs=[VMEM],
        out_specs=VMEM,
        compiler_params=small_kernel(8),
        name="sum_copies",
    )(values)


def halves(value):
    high = value.astype(BF16)
    return high, (value - high.astype(F32)).astype(BF16)


def rows_of(vectors, rank):
    height, tokens = vectors.shape[1:]
    return vectors[: 6 * rank // height].reshape(6 * rank, tokens)


def onehot_of(ids, tokens):
    return (ids == lax.broadcasted_iota(jnp.int32, (SEQS, tokens), 0)).astype(F32)


def target_kernel(rank, vectors, ids, targets, domains, out):
    tokens = ids.shape[1]
    examples = targets.shape[0]
    every = rows_of(vectors, rank)
    total = jnp.zeros((examples, tokens), F32)
    for k in range(3):
        left = every[k * rank : (k + 1) * rank]
        target = targets[:, k].reshape(examples * rank, rank)
        turned = sum(
            jnp.dot(target, part, preferred_element_type=F32)
            for part in halves(every[(3 + k) * rank : (4 + k) * rank])
        )
        total += jnp.sum(turned.reshape(examples, rank, tokens) * left[None], 1)
    domain = lax.broadcasted_iota(jnp.int32, (DOMAINS, examples), 0)
    domains = (domains[...] == domain).astype(F32)
    total = jnp.dot(domains, total, precision=HIGHEST, preferred_element_type=F32)
    scores = transposed_dot(onehot_of(ids[...], tokens), total, HIGHEST)
    counts = transposed_dot(jnp.ones((SEQS // 2, examples), F32), domains, HIGHEST)
    rest = out.shape[2] - 3 * DOMAINS
    parts = [scores[: SEQS // 2], scores[SEQS // 2 :], counts, jnp.zeros((SEQS // 2, rest), F32)]
    parts = jnp.concatenate(parts, 1)
    for i in range(out.shape[0]):
        out[i] = parts


def sketch_kernel(rank, vectors, ids, sketches, norms):
    tokens = ids.shape[1]
    every = rows_of(vectors, rank)
    masks = jnp.concatenate([onehot_of(ids[...], tokens).astype(BF16)] * 3, 1)
    norm = jnp.zeros((SEQS, 1), F32)
    for k in range(3):
        left_high, left_low = halves(every[k * rank : (k + 1) * rank])
        right_high, right_low = halves(every[(3 + k) * rank : (4 + k) * rank])
        left = jnp.concatenate([left_high, left_high, left_low], 1)
        right = jnp.concatenate([right_high, right_low, right_high], 1)
        rows = jnp.concatenate([left * masks[s : s + 1, :] for s in range(SEQS)], 0)
        sketch = transposed_dot(rows, right).reshape(SEQS, rank, rank)
        sketches[:, k] = sketch
        norm += jnp.sum(jnp.sum(sketch * sketch, 1), 1, keepdims=True)
    norms[...] = jnp.broadcast_to(norm, norms.shape)


def score_kernel(parts, norms, scores):
    total = parts[0]
    for i in range(1, parts.shape[0]):
        total += parts[i]
    counts = total[:, 2 * DOMAINS : 3 * DOMAINS]
    half = SEQS // 2
    for i in range(2):
        mean = total[:, i * DOMAINS : (i + 1) * DOMAINS] / counts
        norm = norms[i * half : (i + 1) * half, :DOMAINS]
        scores[i * half : (i + 1) * half, :] = mean * lax.rsqrt(norm + 1e-06)


def on_device(
    count,
    activations,
    cotangent,
    w_gate,
    w_up,
    w_down,
    proj_model,
    proj_hidden,
    seq_ids,
    targets,
    target_domain,
):
    sizes = axis_sizes(count)
    rank = proj_model.shape[1] // 3
    model_cols = proj_model.shape[0]
    tokens = count * activations.shape[0]
    inner = list(range(1, len(sizes) - 1))
    in_pieces, in_backs = gather_rows(activations, sizes, inner)
    out_pieces, out_backs = gather_rows(cotangent, sizes, inner[::-1])

    window = max(model_cols, 128)
    proj_m = proj_model.T
    if window > model_cols:
        at = lax.rem(lax.axis_index("dp"), window // model_cols)
        spots = [
            jnp.where(at == i, proj_m, jnp.zeros_like(proj_m)) for i in range(window // model_cols)
        ]
        proj_m = jnp.concatenate(spots, 1)

    vectors = products(
        in_pieces,
        out_pieces,
        (in_backs, out_backs),
        sizes,
        jnp.concatenate([proj_m, proj_hidden.T], 1),
        w_gate,
        w_up,
        w_down,
    )
    vectors = exchange(sum_copies(exchange(vectors)))

    ids = slot_order(seq_ids, sizes)[None, :]
    parts = pl.pallas_call(
        functools.partial(target_kernel, rank),
        out_shape=jax.ShapeDtypeStruct((count, SEQS // 2, 128), F32),
        in_specs=[VMEM] * 4,
        out_specs=VMEM,
        compiler_params=small_kernel(16),
        name="target_products",
    )(vectors, ids, targets, target_domain[None, :])
    parts, vectors = lax.optimization_barrier((parts, vectors))
    parts = exchange(parts)
    sketches, norms = pl.pallas_call(
        functools.partial(sketch_kernel, rank),
        out_shape=(
            jax.ShapeDtypeStruct((SEQS, 3, rank, rank), F32),
            jax.ShapeDtypeStruct((SEQS, 128), F32),
        ),
        in_specs=[VMEM] * 2,
        out_specs=(VMEM, VMEM),
        compiler_params=small_kernel(24),
        name="sketches",
    )(vectors, ids)
    scores = pl.pallas_call(
        score_kernel,
        out_shape=jax.ShapeDtypeStruct((SEQS, DOMAINS), F32),
        in_specs=[VMEM] * 2,
        out_specs=VMEM,
        compiler_params=small_kernel(4),
        name="scores",
    )(parts, norms)
    return sketches, scores


def solution(mesh):
    in_specs = (
        P(("groups", "dp"), None),
        P(("groups", "dp"), None),
        P("dp", None),
        P("dp", None),
        P("dp", None),
        P("dp", None),
        P("dp", None),
        P("groups"),
        P(("groups", "dp"), None, None, None),
        P(("groups", "dp")),
    )
    out_specs = (P("groups", None, None, None), P("groups", None))
    return jax.shard_map(
        functools.partial(on_device, mesh.shape["dp"]),
        mesh=mesh,
        in_specs=in_specs,
        out_specs=out_specs,
        check_vma=False,
    )
```

```python
import functools

import jax
import jax.numpy as jnp
import numpy as np
from jax import lax
from jax.experimental import pallas as pl
from jax.experimental.pallas import tpu as pltpu
from jax.sharding import PartitionSpec as P

DOMAINS = 32
SEQS = 16
HIGHEST = lax.Precision.HIGHEST
F32 = jnp.float32
BF16 = jnp.bfloat16
VMEM = pl.BlockSpec(memory_space=pltpu.VMEM)
HBM = pl.BlockSpec(memory_space=pltpu.HBM)


def axis_sizes(count):
    if count == 32:
        return (4, 2, 2, 2)
    if count == 128:
        return (8, 8, 2)
    return (count, 1)


def strides_of(sizes):
    return [int(np.prod(sizes[i + 1 :])) for i in range(len(sizes))]


def shift(value, sizes, axis, amount):
    size, stride = sizes[axis], strides_of(sizes)[axis]
    pairs = []
    for source in range(int(np.prod(sizes))):
        at = (source // stride) % size
        pairs.append((source, source + ((at + amount) % size - at) * stride))
    return lax.ppermute(value, "dp", pairs)


def coordinate(me, sizes, axis):
    return lax.rem(lax.div(me, strides_of(sizes)[axis]), sizes[axis])


def received(piece, sizes, axis):
    return [shift(piece, sizes, axis, k) for k in range(1, sizes[axis])]


def gather_lines(parts, sizes):
    rows = parts[0].shape[0]
    both = lax.optimization_barrier(jnp.concatenate(parts, 0))
    blocks = [both] + received(both, sizes, 0)
    lines = [
        jnp.concatenate([block[i * rows : (i + 1) * rows] for block in blocks], 0)
        for i in range(len(parts))
    ]
    return [lax.optimization_barrier(line) for line in lines]


def gather_plane(piece, sizes, order):
    backs = [tuple(0 for _ in sizes)]

    def moved(axis, amount):
        return [tuple(amount if i == axis else b for i, b in enumerate(back)) for back in backs]

    first = None
    for axis in order[:-1]:
        others = received(piece, sizes, axis)
        first = others[0] if first is None else first
        piece = jnp.concatenate([piece] + others, 0)
        backs = sum([moved(axis, k) for k in range(1, sizes[axis])], backs)
    pieces = [(piece, backs)]
    for axis in order[-1:]:
        others = zip(received(piece, sizes, axis), range(1, sizes[axis]))
        pieces += [(other, moved(axis, k)) for other, k in others]
    core = len(sizes) - 1
    for piece, backs in list(pieces):
        others = zip(received(piece, sizes, core), range(1, sizes[core]))
        pieces += [(other, moved(core, k)) for other, k in others]
    first = pieces[0][0] if first is None else first
    return [piece for piece, _ in pieces], [backs for _, backs in pieces], first


def slot_order(per_token, sizes):
    rest = int(np.prod(sizes[1:]))
    return per_token.reshape(sizes[0], rest, -1).transpose(1, 0, 2).reshape(-1)


def exchange(blocks, groups=None):
    return lax.all_to_all(
        blocks, "dp", split_axis=0, concat_axis=0, axis_index_groups=groups, tiled=True
    )


def transposed_dot(left, right, precision=None):
    return lax.dot_general(
        left, right, (((1,), (1,)), ((), ())), precision=precision, preferred_element_type=F32
    )


def place_pieces(pieces, backs, sizes, into):
    me = lax.axis_index("dp")
    for piece, lines in zip(pieces, backs):
        rows = piece.shape[0] // len(lines)
        for i, back in enumerate(lines):
            slot = 0
            for axis in range(1, len(sizes)):
                at = coordinate(me, sizes, axis) + sizes[axis] - back[axis]
                slot = slot * sizes[axis] + lax.rem(at, sizes[axis])
            start = pl.multiple_of(slot * rows, rows)
            into[pl.ds(start, rows), :] = piece[i * rows : (i + 1) * rows, :]


def model_side(proj, tokens, model_cols):
    window = proj.shape[1]
    start = lax.div(lax.axis_index("dp") * model_cols, window) * window
    columns = pl.ds(pl.multiple_of(start, window), window)
    return transposed_dot(proj, tokens[:, columns])


def product_kernel(backs, sizes, model_cols, *refs):
    pieces, refs = refs[: len(backs[0])], refs[len(backs[0]) :]
    out_pieces, refs = refs[: len(backs[1])], refs[len(backs[1]) :]
    proj, w_down, *weights, out, sums, tokens, stacked, buffers, arrived = refs
    streamed = len(weights)
    depth, _, block, chunk = buffers.shape
    hidden_units, count = sums.shape[1:]
    steps = tokens.shape[2] // chunk
    total = steps * (hidden_units // block)

    def places(step):
        rows = pl.ds(pl.multiple_of(lax.div(step, steps) * block, block), block)
        return rows, pl.ds(pl.multiple_of(lax.rem(step, steps) * chunk, chunk), chunk)

    def copy(step, w):
        slot = lax.rem(step, depth)
        return pltpu.make_async_copy(
            weights[w].at[places(step)], buffers.at[slot, w], arrived.at[slot, w]
        )

    for step in range(min(depth, total)):
        for w in range(streamed):
            copy(step, w).start()
    place_pieces(pieces, backs[0], sizes, tokens.at[0])
    place_pieces(out_pieces, backs[1], sizes, tokens.at[1])
    sums[...] = jnp.zeros_like(sums)

    @pl.loop(0, total)
    def _(step):
        rows, columns = places(step)
        sums[2, rows, :] += transposed_dot(w_down[rows, columns], tokens[1, :, columns])
        for w in range(streamed):
            copy(step, w).wait()
            sums[w, rows, :] += transposed_dot(
                buffers[lax.rem(step, depth), w], tokens[0, :, columns]
            )

            @pl.when(step + depth < total)
            def _():
                copy(step + depth, w).start()

    rank = proj.shape[0] // 3
    window = proj.shape[1] - hidden_units
    right = [
        model_side(proj[: 2 * rank, :window], tokens.at[0], model_cols),
        model_side(proj[2 * rank :, :window], tokens.at[1], model_cols),
    ]
    tile = 128 if hidden_units % 128 == 0 else 32

    @pl.loop(0, hidden_units // tile)
    def _(step):
        rows = pl.ds(pl.multiple_of(step * tile, tile), tile)
        gate_value, up_value, grad = sums[0, rows, :], sums[1, rows, :], sums[2, rows, :]
        s = 1.0 / (1.0 + jnp.exp(-gate_value))
        silu = gate_value * s
        stacked[0, rows, :] = (
            grad * up_value * s * (1.0 + gate_value * (1.0 - s))
        ).astype(BF16)
        stacked[1, rows, :] = (grad * silu).astype(BF16)
        stacked[2, rows, :] = (silu * up_value).astype(BF16)

    sides = [
        jnp.dot(proj[p * rank : (p + 1) * rank, window:], stacked[k], preferred_element_type=F32)
        for k, p in enumerate((1, 2, 0))
    ]
    every = jnp.concatenate(sides + right, 0)
    size, each = sizes[0], count // int(np.prod(sizes))
    line = size * each
    source = lax.broadcasted_iota(jnp.int32, (count, count), 0)
    target = lax.broadcasted_iota(jnp.int32, (count, count), 1)
    back = lax.rem(lax.div(source, each), size)
    at = lax.rem(coordinate(lax.axis_index("dp"), sizes, 0) + size - back, size)
    place = lax.div(source, line) * line + at * each + lax.rem(source, each)
    order = (place == target).astype(F32)
    every = jnp.dot(every, order, precision=HIGHEST, preferred_element_type=F32)
    used = every.shape[0] // out.shape[1]
    out[:used] = every.reshape((used,) + out.shape[1:])
    if used < out.shape[0]:
        out[used:] = jnp.zeros_like(out[used:])


def small_kernel(megabytes):
    return pltpu.CompilerParams(vmem_limit_bytes=megabytes * 2**20)


def near_kernel(proj_m, proj_h, weight, proj, near, arrived):
    window = proj_m.shape[1]
    copies = [
        pltpu.make_async_copy(weight, near, arrived.at[0]),
        pltpu.make_async_copy(proj_m, proj.at[:, :window], arrived.at[1]),
        pltpu.make_async_copy(proj_h, proj.at[:, window:], arrived.at[2]),
    ]
    for copy in copies:
        copy.start()
    for copy in copies:
        copy.wait()


def bring_near(proj_m, proj_h, weight):
    columns = proj_m.shape[1] + proj_h.shape[1]
    size = 2 * weight.shape[0] * weight.shape[1]
    return pl.pallas_call(
        near_kernel,
        out_shape=(
            jax.ShapeDtypeStruct((proj_m.shape[0], columns), BF16),
            jax.ShapeDtypeStruct(weight.shape, BF16),
        ),
        in_specs=[HBM] * 3,
        out_specs=(VMEM, VMEM),
        scratch_shapes=[pltpu.SemaphoreType.DMA((3,))],
        compiler_params=small_kernel(34),
        cost_estimate=pl.CostEstimate(flops=0, bytes_accessed=2 * size, transcendentals=0),
        name="bring_near",
    )(proj_m, proj_h, weight)


def products(in_pieces, out_pieces, backs, sizes, proj, w_down, w_gate, w_up):
    hidden, width = w_gate.shape
    count = int(np.prod(sizes))
    tokens = sum(piece.shape[0] for piece in in_pieces)
    model_cols = width // count
    chunk = min(width, 2048)
    block = hidden // 2 if hidden % 32 == 0 and hidden > 256 else hidden
    height = 8 * -(-2 * proj.shape[0] // (8 * count))
    return pl.pallas_call(
        functools.partial(product_kernel, backs, sizes, model_cols),
        out_shape=jax.ShapeDtypeStruct((count, height, tokens), F32),
        in_specs=[VMEM] * (len(in_pieces) + len(out_pieces) + 2) + [HBM] * 2,
        out_specs=VMEM,
        scratch_shapes=[
            pltpu.VMEM((3, hidden, tokens), F32),
            pltpu.VMEM((2, tokens, width), BF16),
            pltpu.VMEM((3, hidden, tokens), BF16),
            pltpu.VMEM((2, 2, block, chunk), BF16),
            pltpu.SemaphoreType.DMA((2, 2)),
        ],
        compiler_params=pltpu.CompilerParams(vmem_limit_bytes=28 * 2**20),
        cost_estimate=pl.CostEstimate(
            flops=6 * hidden * width * tokens,
            bytes_accessed=6 * hidden * width,
            transcendentals=hidden * tokens,
        ),
        name="products",
    )(*in_pieces, *out_pieces, proj, w_down, w_gate, w_up)


def sum_kernel(values, out):
    total = values[0]
    for i in range(1, values.shape[0]):
        total += values[i]
    for i in range(out.shape[0]):
        out[i] = total


def sum_copies(values):
    return pl.pallas_call(
        sum_kernel,
        out_shape=jax.ShapeDtypeStruct(values.shape, F32),
        in_specs=[VMEM],
        out_specs=VMEM,
        compiler_params=small_kernel(8),
        name="sum_copies",
    )(values)


def halves(value):
    high = value.astype(BF16)
    return high, (value - high.astype(F32)).astype(BF16)


def rows_of(vectors, rank):
    height, tokens = vectors.shape[1:]
    return vectors[: 6 * rank // height].reshape(6 * rank, tokens)


def onehot_of(ids, tokens):
    return (ids == lax.broadcasted_iota(jnp.int32, (SEQS, tokens), 0)).astype(F32)


def target_kernel(rank, vectors, ids, targets, domains, out):
    tokens = ids.shape[1]
    examples = targets.shape[0]
    every = rows_of(vectors, rank)
    total = jnp.zeros((examples, tokens), F32)
    for k in range(3):
        left = every[k * rank : (k + 1) * rank]
        target = targets[:, k].reshape(examples * rank, rank)
        turned = sum(
            jnp.dot(target, part, preferred_element_type=F32)
            for part in halves(every[(3 + k) * rank : (4 + k) * rank])
        )
        total += jnp.sum(turned.reshape(examples, rank, tokens) * left[None], 1)
    domain = lax.broadcasted_iota(jnp.int32, (DOMAINS, examples), 0)
    domains = (domains[...] == domain).astype(F32)
    total = jnp.dot(domains, total, precision=HIGHEST, preferred_element_type=F32)
    scores = transposed_dot(onehot_of(ids[...], tokens), total, HIGHEST)
    counts = transposed_dot(jnp.ones((SEQS // 2, examples), F32), domains, HIGHEST)
    rest = out.shape[2] - 3 * DOMAINS
    parts = [scores[: SEQS // 2], scores[SEQS // 2 :], counts, jnp.zeros((SEQS // 2, rest), F32)]
    parts = jnp.concatenate(parts, 1)
    for i in range(out.shape[0]):
        out[i] = parts


def sketch_kernel(rank, vectors, ids, sketches, norms):
    tokens = ids.shape[1]
    every = rows_of(vectors, rank)
    masks = jnp.concatenate([onehot_of(ids[...], tokens).astype(BF16)] * 3, 1)
    norm = jnp.zeros((SEQS, 1), F32)
    for k in range(3):
        left_high, left_low = halves(every[k * rank : (k + 1) * rank])
        right_high, right_low = halves(every[(3 + k) * rank : (4 + k) * rank])
        left = jnp.concatenate([left_high, left_high, left_low], 1)
        right = jnp.concatenate([right_high, right_low, right_high], 1)
        rows = jnp.concatenate([left * masks[s : s + 1, :] for s in range(SEQS)], 0)
        sketch = transposed_dot(rows, right).reshape(SEQS, rank, rank)
        sketches[:, k] = sketch
        norm += jnp.sum(jnp.sum(sketch * sketch, 1), 1, keepdims=True)
    norms[...] = jnp.broadcast_to(norm, norms.shape)


def score_kernel(parts, norms, scores):
    total = parts[0]
    for i in range(1, parts.shape[0]):
        total += parts[i]
    counts = total[:, 2 * DOMAINS : 3 * DOMAINS]
    half = SEQS // 2
    for i in range(2):
        mean = total[:, i * DOMAINS : (i + 1) * DOMAINS] / counts
        norm = norms[i * half : (i + 1) * half, :DOMAINS]
        scores[i * half : (i + 1) * half, :] = mean * lax.rsqrt(norm + 1e-06)


def on_device(
    count,
    activations,
    cotangent,
    w_gate,
    w_up,
    w_down,
    proj_model,
    proj_hidden,
    seq_ids,
    targets,
    target_domain,
):
    sizes = axis_sizes(count)
    rank = proj_model.shape[1] // 3
    model_cols = proj_model.shape[0]
    tokens = count * activations.shape[0]
    inner = list(range(1, len(sizes) - 1))
    in_line, out_line = gather_lines([activations, cotangent], sizes)
    in_pieces, in_backs, in_first = gather_plane(in_line, sizes, inner)
    out_pieces, out_backs, out_first = gather_plane(out_line, sizes, inner[::-1])

    window = max(model_cols, 128)
    proj_m = proj_model.T
    if window > model_cols:
        at = lax.rem(lax.axis_index("dp"), window // model_cols)
        spots = [
            jnp.where(at == i, proj_m, jnp.zeros_like(proj_m)) for i in range(window // model_cols)
        ]
        proj_m = jnp.concatenate(spots, 1)

    held = lax.optimization_barrier((proj_m, proj_hidden.T, w_down, in_first, out_first))
    near = bring_near(*held[:3])
    vectors = products(
        in_pieces,
        out_pieces,
        (in_backs, out_backs),
        sizes,
        *near,
        w_gate,
        w_up,
    )
    vectors = exchange(sum_copies(exchange(vectors)))

    ids = slot_order(seq_ids, sizes)[None, :]
    parts = pl.pallas_call(
        functools.partial(target_kernel, rank),
        out_shape=jax.ShapeDtypeStruct((count, SEQS // 2, 128), F32),
        in_specs=[VMEM] * 4,
        out_specs=VMEM,
        compiler_params=small_kernel(16),
        name="target_products",
    )(vectors, ids, targets, target_domain[None, :])
    parts, vectors = lax.optimization_barrier((parts, vectors))
    parts = exchange(parts)
    sketches, norms = pl.pallas_call(
        functools.partial(sketch_kernel, rank),
        out_shape=(
            jax.ShapeDtypeStruct((SEQS, 3, rank, rank), F32),
            jax.ShapeDtypeStruct((SEQS, 128), F32),
        ),
        in_specs=[VMEM] * 2,
        out_specs=(VMEM, VMEM),
        compiler_params=small_kernel(24),
        name="sketches",
    )(vectors, ids)
    scores = pl.pallas_call(
        score_kernel,
        out_shape=jax.ShapeDtypeStruct((SEQS, DOMAINS), F32),
        in_specs=[VMEM] * 2,
        out_specs=VMEM,
        compiler_params=small_kernel(4),
        name="scores",
    )(parts, norms)
    return sketches, scores


def solution(mesh):
    in_specs = (
        P(("groups", "dp"), None),
        P(("groups", "dp"), None),
        P("dp", None),
        P("dp", None),
        P("dp", None),
        P("dp", None),
        P("dp", None),
        P("groups"),
        P(("groups", "dp"), None, None, None),
        P(("groups", "dp")),
    )
    out_specs = (P("groups", None, None, None), P("groups", None))
    return jax.shard_map(
        functools.partial(on_device, mesh.shape["dp"]),
        mesh=mesh,
        in_specs=in_specs,
        out_specs=out_specs,
        check_vma=False,
    )
```

```python
import functools

import jax
import jax.numpy as jnp
import numpy as np
from jax import lax
from jax.experimental import pallas as pl
from jax.experimental.pallas import tpu as pltpu
from jax.sharding import PartitionSpec as P

DOMAINS = 32
SEQS = 16
HIGHEST = lax.Precision.HIGHEST
F32 = jnp.float32
BF16 = jnp.bfloat16
VMEM = pl.BlockSpec(memory_space=pltpu.VMEM)
HBM = pl.BlockSpec(memory_space=pltpu.HBM)


def axis_sizes(count):
    if count == 32:
        return (4, 2, 2, 2)
    if count == 128:
        return (8, 8, 2)
    return (count, 1)


def strides_of(sizes):
    return [int(np.prod(sizes[i + 1 :])) for i in range(len(sizes))]


def shift(value, sizes, axis, amount):
    size, stride = sizes[axis], strides_of(sizes)[axis]
    pairs = []
    for source in range(int(np.prod(sizes))):
        at = (source // stride) % size
        pairs.append((source, source + ((at + amount) % size - at) * stride))
    return lax.ppermute(value, "dp", pairs)


def partner(value, sizes, axis, bit):
    size, stride = sizes[axis], strides_of(sizes)[axis]
    pairs = []
    for source in range(int(np.prod(sizes))):
        at = (source // stride) % size
        pairs.append((source, source + ((at ^ bit) - at) * stride))
    return lax.ppermute(value, "dp", pairs)


def spread_axis(value, sizes, axis):
    if sizes[axis] == 4:
        far, near = partner(value, sizes, axis, 2), partner(value, sizes, axis, 1)
        return [value, near, far, partner(far, sizes, axis, 1)]
    return [value] + [shift(value, sizes, axis, k) for k in range(1, sizes[axis])]


def origin(at, distance, size):
    if size == 4:
        return lax.bitwise_xor(at, distance)
    return lax.rem(at + size - distance, size)


def coordinate(me, sizes, axis):
    return lax.rem(lax.div(me, strides_of(sizes)[axis]), sizes[axis])


def gather_lines(parts, sizes, others):
    rows = parts[0].shape[0]
    both = lax.optimization_barrier(jnp.concatenate(parts, 0))
    blocks = spread_axis(both, sizes, 0)
    lines = [
        jnp.concatenate([block[i * rows : (i + 1) * rows] for block in blocks], 0)
        for i in range(len(parts))
    ]
    made = lax.optimization_barrier((*lines, *others))
    return made[: len(lines)], made[len(lines) :]


def gather_stack(value, sizes, order):
    for axis in order:
        value = jnp.stack(spread_axis(value, sizes, axis))
    return value


def gather_plane(piece, sizes, order):
    backs = [tuple(0 for _ in sizes)]

    def moved(axis, amount):
        return [tuple(amount if i == axis else b for i, b in enumerate(back)) for back in backs]

    first = None
    for axis in order[:-1]:
        others = spread_axis(piece, sizes, axis)[1:]
        first = others[0] if first is None else first
        piece = jnp.concatenate([piece] + others, 0)
        backs = sum([moved(axis, k) for k in range(1, sizes[axis])], backs)
    pieces = [(piece, backs)]
    for axis in order[-1:]:
        others = zip(spread_axis(piece, sizes, axis)[1:], range(1, sizes[axis]))
        pieces += [(other, moved(axis, k)) for other, k in others]
    core = len(sizes) - 1
    for piece, backs in list(pieces):
        others = zip(spread_axis(piece, sizes, core)[1:], range(1, sizes[core]))
        pieces += [(other, moved(core, k)) for other, k in others]
    first = pieces[0][0] if first is None else first
    return [piece for piece, _ in pieces], [backs for _, backs in pieces], first


def slot_order(per_token, sizes):
    rest = int(np.prod(sizes[1:]))
    return per_token.reshape(sizes[0], rest, -1).transpose(1, 0, 2).reshape(-1)


def exchange(blocks, groups=None):
    return lax.all_to_all(
        blocks, "dp", split_axis=0, concat_axis=0, axis_index_groups=groups, tiled=True
    )


def transposed_dot(left, right, precision=None):
    return lax.dot_general(
        left, right, (((1,), (1,)), ((), ())), precision=precision, preferred_element_type=F32
    )


def place_pieces(pieces, backs, sizes, into):
    me = lax.axis_index("dp")
    for piece, lines in zip(pieces, backs):
        rows = piece.shape[0] // len(lines)
        for i, back in enumerate(lines):
            slot = 0
            for axis in range(1, len(sizes)):
                at = origin(coordinate(me, sizes, axis), back[axis], sizes[axis])
                slot = slot * sizes[axis] + at
            start = pl.multiple_of(slot * rows, rows)
            into[pl.ds(start, rows), :] = piece[i * rows : (i + 1) * rows, :]


def model_side(proj, tokens, model_cols):
    window = proj.shape[1]
    start = lax.div(lax.axis_index("dp") * model_cols, window) * window
    columns = pl.ds(pl.multiple_of(start, window), window)
    return transposed_dot(proj, tokens[:, columns])


def product_kernel(backs, sizes, model_cols, *refs):
    pieces, refs = refs[: len(backs[0])], refs[len(backs[0]) :]
    out_pieces, refs = refs[: len(backs[1])], refs[len(backs[1]) :]
    proj, *weights, out, sums, tokens, stacked, buffers, arrived = refs
    sides = (0, 0, 1)
    depth, _, block, chunk = buffers.shape
    hidden_units, count = sums.shape[1:]
    steps = tokens.shape[2] // chunk
    total = steps * (hidden_units // block)

    def places(step):
        rows = pl.ds(pl.multiple_of(lax.div(step, steps) * block, block), block)
        return rows, pl.ds(pl.multiple_of(lax.rem(step, steps) * chunk, chunk), chunk)

    def copy(step, w):
        slot = lax.rem(step, depth)
        return pltpu.make_async_copy(
            weights[w].at[places(step)], buffers.at[slot, w], arrived.at[slot, w]
        )

    for step in range(min(depth, total)):
        for w in range(3):
            copy(step, w).start()
    place_pieces(pieces, backs[0], sizes, tokens.at[0])
    place_pieces(out_pieces, backs[1], sizes, tokens.at[1])
    sums[...] = jnp.zeros_like(sums)

    @pl.loop(0, total)
    def _(step):
        rows, columns = places(step)
        for w in range(3):
            copy(step, w).wait()
            sums[w, rows, :] += transposed_dot(
                buffers[lax.rem(step, depth), w], tokens[sides[w], :, columns]
            )

            @pl.when(step + depth < total)
            def _():
                copy(step + depth, w).start()

    rank = proj.shape[0] // 3
    window = proj.shape[1] - hidden_units
    right = [
        model_side(proj[: 2 * rank, :window], tokens.at[0], model_cols),
        model_side(proj[2 * rank :, :window], tokens.at[1], model_cols),
    ]
    tile = 128 if hidden_units % 128 == 0 else 32

    @pl.loop(0, hidden_units // tile)
    def _(step):
        rows = pl.ds(pl.multiple_of(step * tile, tile), tile)
        gate_value, up_value, grad = sums[0, rows, :], sums[1, rows, :], sums[2, rows, :]
        s = 1.0 / (1.0 + jnp.exp(-gate_value))
        silu = gate_value * s
        stacked[0, rows, :] = (
            grad * up_value * s * (1.0 + gate_value * (1.0 - s))
        ).astype(BF16)
        stacked[1, rows, :] = (grad * silu).astype(BF16)
        stacked[2, rows, :] = (silu * up_value).astype(BF16)

    sides = [
        jnp.dot(proj[p * rank : (p + 1) * rank, window:], stacked[k], preferred_element_type=F32)
        for k, p in enumerate((1, 2, 0))
    ]
    every = jnp.concatenate(sides + right, 0)
    size, each = sizes[0], count // int(np.prod(sizes))
    line = size * each
    source = lax.broadcasted_iota(jnp.int32, (count, count), 0)
    target = lax.broadcasted_iota(jnp.int32, (count, count), 1)
    back = lax.rem(lax.div(source, each), size)
    at = origin(coordinate(lax.axis_index("dp"), sizes, 0), back, size)
    place = lax.div(source, line) * line + at * each + lax.rem(source, each)
    order = (place == target).astype(F32)
    every = jnp.dot(every, order, precision=HIGHEST, preferred_element_type=F32)
    used = every.shape[0] // out.shape[1]
    out[:used] = every.reshape((used,) + out.shape[1:])
    if used < out.shape[0]:
        out[used:] = jnp.zeros_like(out[used:])


def small_kernel(megabytes):
    return pltpu.CompilerParams(vmem_limit_bytes=megabytes * 2**20)


def products(in_pieces, out_pieces, backs, sizes, proj, w_gate, w_up, w_down):
    hidden, width = w_gate.shape
    count = int(np.prod(sizes))
    tokens = sum(piece.shape[0] for piece in in_pieces)
    model_cols = width // count
    chunk = min(width, 2048)
    block = hidden // 2 if hidden % 32 == 0 and hidden > 256 else hidden
    height = 8 * -(-2 * proj.shape[0] // (8 * count))
    return pl.pallas_call(
        functools.partial(product_kernel, backs, sizes, model_cols),
        out_shape=jax.ShapeDtypeStruct((count, height, tokens), F32),
        in_specs=[VMEM] * (len(in_pieces) + len(out_pieces) + 1) + [HBM] * 3,
        out_specs=VMEM,
        scratch_shapes=[
            pltpu.VMEM((3, hidden, tokens), F32),
            pltpu.VMEM((2, tokens, width), BF16),
            pltpu.VMEM((3, hidden, tokens), BF16),
            pltpu.VMEM((2, 3, block, chunk), BF16),
            pltpu.SemaphoreType.DMA((2, 3)),
        ],
        compiler_params=pltpu.CompilerParams(vmem_limit_bytes=44 * 2**20),
        cost_estimate=pl.CostEstimate(
            flops=6 * hidden * width * tokens,
            bytes_accessed=6 * hidden * width,
            transcendentals=hidden * tokens,
        ),
        name="products",
    )(*in_pieces, *out_pieces, proj, w_gate, w_up, w_down)


def sum_kernel(values, out):
    total = values[0]
    for i in range(1, values.shape[0]):
        total += values[i]
    for i in range(out.shape[0]):
        out[i] = total


def sum_copies(values):
    return pl.pallas_call(
        sum_kernel,
        out_shape=jax.ShapeDtypeStruct(values.shape, F32),
        in_specs=[VMEM],
        out_specs=VMEM,
        compiler_params=small_kernel(8),
        name="sum_copies",
    )(values)


def halves(value):
    high = value.astype(BF16)
    return high, (value - high.astype(F32)).astype(BF16)


def rows_of(vectors, rank):
    height, tokens = vectors.shape[1:]
    return vectors[: 6 * rank // height].reshape(6 * rank, tokens)


def onehot_of(ids, tokens):
    return (ids == lax.broadcasted_iota(jnp.int32, (SEQS, tokens), 0)).astype(F32)


def sketch_kernel(sizes, order, vectors, means, ids, sketches, scores, lefts, turned):
    count = int(np.prod(sizes))
    rank = sketches.shape[2]
    tokens = ids.shape[1]
    own_rank = means.shape[2] // rank
    every = rows_of(vectors, rank)
    onehot = onehot_of(ids[...], tokens)
    masks = jnp.concatenate([onehot.astype(BF16)] * 3, 1)
    norm = jnp.zeros((SEQS, 1), F32)
    if own_rank * count > rank:
        lefts[...] = jnp.zeros_like(lefts)
    for k in range(3):
        left = every[k * rank : (k + 1) * rank]
        right = every[(3 + k) * rank : (4 + k) * rank]
        left_high, left_low = halves(left)
        right_high, right_low = halves(right)
        left_three = jnp.concatenate([left_high, left_high, left_low], 1)
        right_three = jnp.concatenate([right_high, right_low, right_high], 1)
        rows = jnp.concatenate([left_three * masks[s : s + 1, :] for s in range(SEQS)], 0)
        sketch = transposed_dot(rows, right_three).reshape(SEQS, rank, rank)
        sketches[:, k] = sketch
        norm += jnp.sum(jnp.sum(sketch * sketch, 1), 1, keepdims=True)

        for i in range(own_rank):
            part = left[i * count : (i + 1) * count]
            lefts[k, : part.shape[0], i * tokens : (i + 1) * tokens] = part
        mean = means[:, k * DOMAINS : (k + 1) * DOMAINS, :].reshape(-1, own_rank * rank)
        result = 0.0
        for part in (right_high, right_low):
            empty = jnp.zeros_like(part)
            wide = jnp.concatenate(
                [
                    jnp.concatenate([part if i == c else empty for c in range(own_rank)], 1)
                    for i in range(own_rank)
                ],
                0,
            )
            result += jnp.dot(mean, wide, preferred_element_type=F32)
        turned[k] = result.reshape(count, DOMAINS, own_rank * tokens)

    me = lax.axis_index("dp")

    def add(device, total):
        place, step = 0, 1
        for axis in order:
            back = origin(
                coordinate(me, sizes, axis), coordinate(device, sizes, axis), sizes[axis]
            )
            place += back * step
            step *= sizes[axis]
        for k in range(3):
            total += turned[k, place] * lefts[k, pl.ds(device, 1), :]
        return total

    total = lax.fori_loop(0, count, add, jnp.zeros((DOMAINS, own_rank * tokens), F32))
    total = sum(total[:, i * tokens : (i + 1) * tokens] for i in range(own_rank))
    scores[...] = transposed_dot(onehot, total, HIGHEST) * lax.rsqrt(norm + 1e-06)


def on_device(
    count,
    activations,
    cotangent,
    w_gate,
    w_up,
    w_down,
    proj_model,
    proj_hidden,
    seq_ids,
    targets,
    target_domain,
):
    sizes = axis_sizes(count)
    rank = proj_model.shape[1] // 3
    model_cols = proj_model.shape[0]
    own_rank = -(-rank // count)
    padded = own_rank * count
    tokens = count * activations.shape[0]
    examples = targets.shape[0]
    inner = list(range(1, len(sizes) - 1))

    window = max(model_cols, 128)
    proj_m = proj_model.T
    if window > model_cols:
        at = lax.rem(lax.axis_index("dp"), window // model_cols)
        spots = [
            jnp.where(at == i, proj_m, jnp.zeros_like(proj_m)) for i in range(window // model_cols)
        ]
        proj_m = jnp.concatenate(spots, 1)
    proj = jnp.concatenate([proj_m, proj_hidden.T], 1)

    cut = jnp.pad(targets, ((0, 0), (0, 0), (0, padded - rank), (0, 0)))
    cut = cut.reshape(examples, 3, own_rank, count, rank).transpose(3, 0, 1, 2, 4)
    entries = 3 * own_rank * rank
    cut = cut.reshape(count, examples, entries)
    tags = jnp.broadcast_to(target_domain.astype(BF16)[None, :, None], (count, examples, 128))
    sent = jnp.concatenate([cut, tags], 2)

    (in_line, out_line), (proj, sent) = gather_lines([activations, cotangent], sizes, [proj, sent])
    in_pieces, in_backs, in_first = gather_plane(in_line, sizes, inner)
    out_pieces, out_backs, out_first = gather_plane(out_line, sizes, inner[::-1])
    sent, _, _ = lax.optimization_barrier((sent, in_first, out_first))
    held = exchange(sent).reshape(count * examples, -1)

    vectors = products(
        in_pieces, out_pieces, (in_backs, out_backs), sizes, proj, w_gate, w_up, w_down
    )
    vectors, held = lax.optimization_barrier((vectors, held))
    vectors = exchange(sum_copies(exchange(vectors)))

    domains = held[:, -1].astype(F32)
    domain_onehot = (domains[None, :] == jnp.arange(DOMAINS, dtype=F32)[:, None]).astype(BF16)
    domain_sum = jnp.dot(domain_onehot, held[:, :entries], preferred_element_type=F32)
    domain_count = jnp.sum(domain_onehot.astype(F32), 1)
    mean = (domain_sum / domain_count[:, None]).astype(BF16)
    mean = mean.reshape(DOMAINS, 3, own_rank * rank).transpose(1, 0, 2)
    mean_order = [0] + inner + [len(sizes) - 1]
    means = gather_stack(mean.reshape(3 * DOMAINS, -1), sizes, mean_order)
    means = means.reshape((count,) + means.shape[-2:])

    return pl.pallas_call(
        functools.partial(sketch_kernel, sizes, mean_order),
        out_shape=(
            jax.ShapeDtypeStruct((SEQS, 3, rank, rank), F32),
            jax.ShapeDtypeStruct((SEQS, DOMAINS), F32),
        ),
        in_specs=[VMEM] * 3,
        out_specs=(VMEM, VMEM),
        scratch_shapes=[
            pltpu.VMEM((3, count, own_rank * tokens), F32),
            pltpu.VMEM((3, count, DOMAINS, own_rank * tokens), F32),
        ],
        compiler_params=small_kernel(24 if tokens < 256 else 52),
        name="sketches",
    )(vectors, means, slot_order(seq_ids, sizes)[None, :])


def solution(mesh):
    in_specs = (
        P(("groups", "dp"), None),
        P(("groups", "dp"), None),
        P("dp", None),
        P("dp", None),
        P("dp", None),
        P("dp", None),
        P("dp", None),
        P("groups"),
        P(("groups", "dp"), None, None, None),
        P(("groups", "dp")),
    )
    out_specs = (P("groups", None, None, None), P("groups", None))
    return jax.shard_map(
        functools.partial(on_device, mesh.shape["dp"]),
        mesh=mesh,
        in_specs=in_specs,
        out_specs=out_specs,
        check_vma=False,
    )
```

```python
import functools

import jax
import jax.numpy as jnp
import numpy as np
from jax import lax
from jax.experimental import pallas as pl
from jax.experimental.pallas import tpu as pltpu
from jax.sharding import PartitionSpec as P

DOMAINS = 32
SEQS = 16
HIGHEST = lax.Precision.HIGHEST
F32 = jnp.float32
BF16 = jnp.bfloat16
VMEM = pl.BlockSpec(memory_space=pltpu.VMEM)
HBM = pl.BlockSpec(memory_space=pltpu.HBM)


def axis_sizes(count):
    if count == 32:
        return (4, 2, 2, 2)
    if count == 128:
        return (8, 8, 2)
    return (count, 1)


def strides_of(sizes):
    return [int(np.prod(sizes[i + 1 :])) for i in range(len(sizes))]


def shift(value, sizes, axis, amount):
    size, stride = sizes[axis], strides_of(sizes)[axis]
    pairs = []
    for source in range(int(np.prod(sizes))):
        at = (source // stride) % size
        pairs.append((source, source + ((at + amount) % size - at) * stride))
    return lax.ppermute(value, "dp", pairs)


def partner(value, sizes, axis, bit):
    size, stride = sizes[axis], strides_of(sizes)[axis]
    pairs = []
    for source in range(int(np.prod(sizes))):
        at = (source // stride) % size
        pairs.append((source, source + ((at ^ bit) - at) * stride))
    return lax.ppermute(value, "dp", pairs)


def spread_axis(value, sizes, axis):
    if sizes[axis] == 4:
        far, near = partner(value, sizes, axis, 2), partner(value, sizes, axis, 1)
        return [value, near, far, partner(far, sizes, axis, 1)]
    return [value] + [shift(value, sizes, axis, k) for k in range(1, sizes[axis])]


def origin(at, distance, size):
    if size == 4:
        return lax.bitwise_xor(at, distance)
    return lax.rem(at + size - distance, size)


def coordinate(me, sizes, axis):
    return lax.rem(lax.div(me, strides_of(sizes)[axis]), sizes[axis])


def gather_lines(parts, sizes, others):
    rows = parts[0].shape[0]
    both = lax.optimization_barrier(jnp.concatenate(parts, 0))
    blocks = spread_axis(both, sizes, 0)
    lines = [
        jnp.concatenate([block[i * rows : (i + 1) * rows] for block in blocks], 0)
        for i in range(len(parts))
    ]
    made = lax.optimization_barrier((*lines, *others))
    return made[: len(lines)], made[len(lines) :]


def gather_stack(value, sizes, order):
    for axis in order:
        value = jnp.stack(spread_axis(value, sizes, axis))
    return value


def gather_plane(piece, sizes, order):
    backs = [tuple(0 for _ in sizes)]

    def moved(axis, amount):
        return [tuple(amount if i == axis else b for i, b in enumerate(back)) for back in backs]

    first = None
    for axis in order[:-1]:
        others = spread_axis(piece, sizes, axis)[1:]
        first = others[0] if first is None else first
        piece = jnp.concatenate([piece] + others, 0)
        backs = sum([moved(axis, k) for k in range(1, sizes[axis])], backs)
    pieces = [(piece, backs)]
    for axis in order[-1:]:
        others = zip(spread_axis(piece, sizes, axis)[1:], range(1, sizes[axis]))
        pieces += [(other, moved(axis, k)) for other, k in others]
    core = len(sizes) - 1
    for piece, backs in list(pieces):
        others = zip(spread_axis(piece, sizes, core)[1:], range(1, sizes[core]))
        pieces += [(other, moved(core, k)) for other, k in others]
    first = pieces[0][0] if first is None else first
    return [piece for piece, _ in pieces], [backs for _, backs in pieces], first


def slot_order(per_token, sizes):
    rest = int(np.prod(sizes[1:]))
    return per_token.reshape(sizes[0], rest, -1).transpose(1, 0, 2).reshape(-1)


def exchange(blocks, groups=None):
    return lax.all_to_all(
        blocks, "dp", split_axis=0, concat_axis=0, axis_index_groups=groups, tiled=True
    )


def transposed_dot(left, right, precision=None):
    return lax.dot_general(
        left, right, (((1,), (1,)), ((), ())), precision=precision, preferred_element_type=F32
    )


def place_pieces(pieces, backs, sizes, into):
    me = lax.axis_index("dp")
    for piece, lines in zip(pieces, backs):
        rows = piece.shape[0] // len(lines)
        for i, back in enumerate(lines):
            slot = 0
            for axis in range(1, len(sizes)):
                at = origin(coordinate(me, sizes, axis), back[axis], sizes[axis])
                slot = slot * sizes[axis] + at
            start = pl.multiple_of(slot * rows, rows)
            into[pl.ds(start, rows), :] = piece[i * rows : (i + 1) * rows, :]


def model_side(proj, tokens, model_cols):
    window = proj.shape[1]
    start = lax.div(lax.axis_index("dp") * model_cols, window) * window
    columns = pl.ds(pl.multiple_of(start, window), window)
    return transposed_dot(proj, tokens[:, columns])


def product_kernel(backs, sizes, model_cols, *refs):
    pieces, refs = refs[: len(backs[0])], refs[len(backs[0]) :]
    out_pieces, refs = refs[: len(backs[1])], refs[len(backs[1]) :]
    proj, *weights, out, sums, tokens, stacked, buffers, arrived = refs
    sides = (0, 0, 1)
    depth, _, block, chunk = buffers.shape
    hidden_units, count = sums.shape[1:]
    steps = tokens.shape[2] // chunk
    total = steps * (hidden_units // block)

    def places(step):
        rows = pl.ds(pl.multiple_of(lax.div(step, steps) * block, block), block)
        return rows, pl.ds(pl.multiple_of(lax.rem(step, steps) * chunk, chunk), chunk)

    def copy(step, w):
        slot = lax.rem(step, depth)
        return pltpu.make_async_copy(
            weights[w].at[places(step)], buffers.at[slot, w], arrived.at[slot, w]
        )

    for step in range(min(depth, total)):
        for w in range(3):
            copy(step, w).start()
    place_pieces(pieces, backs[0], sizes, tokens.at[0])
    place_pieces(out_pieces, backs[1], sizes, tokens.at[1])
    sums[...] = jnp.zeros_like(sums)

    @pl.loop(0, total)
    def _(step):
        rows, columns = places(step)
        for w in range(3):
            copy(step, w).wait()
            sums[w, rows, :] += transposed_dot(
                buffers[lax.rem(step, depth), w], tokens[sides[w], :, columns]
            )

            @pl.when(step + depth < total)
            def _():
                copy(step + depth, w).start()

    rank = proj.shape[0] // 3
    window = proj.shape[1] - hidden_units
    right = [
        model_side(proj[: 2 * rank, :window], tokens.at[0], model_cols),
        model_side(proj[2 * rank :, :window], tokens.at[1], model_cols),
    ]
    tile = 128 if hidden_units % 128 == 0 else 32

    @pl.loop(0, hidden_units // tile)
    def _(step):
        rows = pl.ds(pl.multiple_of(step * tile, tile), tile)
        gate_value, up_value, grad = sums[0, rows, :], sums[1, rows, :], sums[2, rows, :]
        s = 1.0 / (1.0 + jnp.exp(-gate_value))
        silu = gate_value * s
        stacked[0, rows, :] = (
            grad * up_value * s * (1.0 + gate_value * (1.0 - s))
        ).astype(BF16)
        stacked[1, rows, :] = (grad * silu).astype(BF16)
        stacked[2, rows, :] = (silu * up_value).astype(BF16)

    sides = [
        jnp.dot(proj[p * rank : (p + 1) * rank, window:], stacked[k], preferred_element_type=F32)
        for k, p in enumerate((1, 2, 0))
    ]
    every = jnp.concatenate(sides + right, 0)
    size, each = sizes[0], count // int(np.prod(sizes))
    line = size * each
    source = lax.broadcasted_iota(jnp.int32, (count, count), 0)
    target = lax.broadcasted_iota(jnp.int32, (count, count), 1)
    back = lax.rem(lax.div(source, each), size)
    at = origin(coordinate(lax.axis_index("dp"), sizes, 0), back, size)
    place = lax.div(source, line) * line + at * each + lax.rem(source, each)
    order = (place == target).astype(F32)
    every = jnp.dot(every, order, precision=HIGHEST, preferred_element_type=F32)
    used = every.shape[0] // out.shape[1]
    out[:used] = every.reshape((used,) + out.shape[1:])
    if used < out.shape[0]:
        out[used:] = jnp.zeros_like(out[used:])


def small_kernel(megabytes):
    return pltpu.CompilerParams(vmem_limit_bytes=megabytes * 2**20)


def products(in_pieces, out_pieces, backs, sizes, proj, w_gate, w_up, w_down):
    hidden, width = w_gate.shape
    count = int(np.prod(sizes))
    tokens = sum(piece.shape[0] for piece in in_pieces)
    model_cols = width // count
    chunk = min(width, 2048)
    block = hidden // 2 if hidden % 32 == 0 and hidden > 256 else hidden
    height = 8 * -(-2 * proj.shape[0] // (8 * count))
    return pl.pallas_call(
        functools.partial(product_kernel, backs, sizes, model_cols),
        out_shape=jax.ShapeDtypeStruct((count, height, tokens), F32),
        in_specs=[VMEM] * (len(in_pieces) + len(out_pieces) + 1) + [HBM] * 3,
        out_specs=VMEM,
        scratch_shapes=[
            pltpu.VMEM((3, hidden, tokens), F32),
            pltpu.VMEM((2, tokens, width), BF16),
            pltpu.VMEM((3, hidden, tokens), BF16),
            pltpu.VMEM((2, 3, block, chunk), BF16),
            pltpu.SemaphoreType.DMA((2, 3)),
        ],
        compiler_params=pltpu.CompilerParams(vmem_limit_bytes=44 * 2**20),
        cost_estimate=pl.CostEstimate(
            flops=6 * hidden * width * tokens,
            bytes_accessed=6 * hidden * width,
            transcendentals=hidden * tokens,
        ),
        name="products",
    )(*in_pieces, *out_pieces, proj, w_gate, w_up, w_down)


def sum_kernel(values, out):
    total = values[0]
    for i in range(1, values.shape[0]):
        total += values[i]
    for i in range(out.shape[0]):
        out[i] = total


def sum_copies(values):
    return pl.pallas_call(
        sum_kernel,
        out_shape=jax.ShapeDtypeStruct(values.shape, F32),
        in_specs=[VMEM],
        out_specs=VMEM,
        compiler_params=small_kernel(8),
        name="sum_copies",
    )(values)


def halves(value):
    high = value.astype(BF16)
    return high, (value - high.astype(F32)).astype(BF16)


def rows_of(vectors, rank):
    height, tokens = vectors.shape[1:]
    return vectors[: 6 * rank // height].reshape(6 * rank, tokens)


def onehot_of(ids, tokens):
    return (ids == lax.broadcasted_iota(jnp.int32, (SEQS, tokens), 0)).astype(F32)


def sketch_kernel(sizes, order, vectors, means, ids, sketches, scores, lefts, turned):
    count = int(np.prod(sizes))
    rank = sketches.shape[2]
    tokens = ids.shape[1]
    own_rank = means.shape[2] // rank
    every = rows_of(vectors, rank)
    onehot = onehot_of(ids[...], tokens)
    masks = jnp.concatenate([onehot.astype(BF16)] * 3, 1)
    norm = jnp.zeros((SEQS, 1), F32)
    if own_rank * count > rank:
        lefts[...] = jnp.zeros_like(lefts)
    for k in range(3):
        left = every[k * rank : (k + 1) * rank]
        right = every[(3 + k) * rank : (4 + k) * rank]
        left_high, left_low = halves(left)
        right_high, right_low = halves(right)
        left_three = jnp.concatenate([left_high, left_high, left_low], 1)
        right_three = jnp.concatenate([right_high, right_low, right_high], 1)
        rows = jnp.concatenate([left_three * masks[s : s + 1, :] for s in range(SEQS)], 0)
        sketch = transposed_dot(rows, right_three).reshape(SEQS, rank, rank)
        sketches[:, k] = sketch
        norm += jnp.sum(jnp.sum(sketch * sketch, 1), 1, keepdims=True)

        for i in range(own_rank):
            part = left[i * count : (i + 1) * count]
            lefts[k, : part.shape[0], i * tokens : (i + 1) * tokens] = part
        mean = means[:, k * DOMAINS : (k + 1) * DOMAINS, :].reshape(-1, own_rank * rank)
        result = 0.0
        for part in (right_high, right_low):
            empty = jnp.zeros_like(part)
            wide = jnp.concatenate(
                [
                    jnp.concatenate([part if i == c else empty for c in range(own_rank)], 1)
                    for i in range(own_rank)
                ],
                0,
            )
            result += jnp.dot(mean, wide, preferred_element_type=F32)
        turned[k] = result.reshape(count, DOMAINS, own_rank * tokens)

    me = lax.axis_index("dp")

    def add(device, total):
        place, step = 0, 1
        for axis in order:
            back = origin(
                coordinate(me, sizes, axis), coordinate(device, sizes, axis), sizes[axis]
            )
            place += back * step
            step *= sizes[axis]
        for k in range(3):
            total += turned[k, place] * lefts[k, pl.ds(device, 1), :]
        return total

    total = lax.fori_loop(0, count, add, jnp.zeros((DOMAINS, own_rank * tokens), F32))
    total = sum(total[:, i * tokens : (i + 1) * tokens] for i in range(own_rank))
    scores[...] = transposed_dot(onehot, total, HIGHEST) * lax.rsqrt(norm + 1e-06)


def on_device(
    count,
    activations,
    cotangent,
    w_gate,
    w_up,
    w_down,
    proj_model,
    proj_hidden,
    seq_ids,
    targets,
    target_domain,
):
    sizes = axis_sizes(count)
    rank = proj_model.shape[1] // 3
    model_cols = proj_model.shape[0]
    own_rank = -(-rank // count)
    padded = own_rank * count
    tokens = count * activations.shape[0]
    examples = targets.shape[0]
    inner = list(range(1, len(sizes) - 1))

    window = max(model_cols, 128)
    proj_m = proj_model.T
    if window > model_cols:
        at = lax.rem(lax.axis_index("dp"), window // model_cols)
        spots = [
            jnp.where(at == i, proj_m, jnp.zeros_like(proj_m)) for i in range(window // model_cols)
        ]
        proj_m = jnp.concatenate(spots, 1)
    proj = jnp.concatenate([proj_m, proj_hidden.T], 1)

    cut = jnp.pad(targets, ((0, 0), (0, 0), (0, padded - rank), (0, 0)))
    cut = cut.reshape(examples, 3, own_rank, count, rank).transpose(3, 0, 1, 2, 4)
    entries = 3 * own_rank * rank
    cut = cut.reshape(count, examples, entries)
    tags = jnp.broadcast_to(target_domain.astype(BF16)[None, :, None], (count, examples, 128))
    sent = jnp.concatenate([cut, tags], 2)

    (in_line, out_line), (proj, sent) = gather_lines([activations, cotangent], sizes, [proj, sent])
    in_pieces, in_backs, in_first = gather_plane(in_line, sizes, inner)
    out_pieces, out_backs, out_first = gather_plane(out_line, sizes, inner[::-1])
    held = exchange(sent).reshape(count * examples, -1)
    held, _, _ = lax.optimization_barrier((held, in_first, out_first))
    domains = held[:, -1].astype(F32)
    domain_onehot = (domains[None, :] == jnp.arange(DOMAINS, dtype=F32)[:, None]).astype(BF16)
    domain_sum = jnp.dot(domain_onehot, held[:, :entries], preferred_element_type=F32)
    domain_count = jnp.sum(domain_onehot.astype(F32), 1)
    mean = (domain_sum / domain_count[:, None]).astype(BF16)
    mean = mean.reshape(DOMAINS, 3, own_rank * rank).transpose(1, 0, 2)
    means = gather_stack(mean.reshape(3 * DOMAINS, -1), sizes, [0])

    vectors = products(
        in_pieces, out_pieces, (in_backs, out_backs), sizes, proj, w_gate, w_up, w_down
    )
    for axis in inner[:-1]:
        means = gather_stack(means, sizes, [axis])
    vectors, means = lax.optimization_barrier((vectors, means))
    vectors = sum_copies(exchange(vectors))
    means = gather_stack(means, sizes, inner[-1:])
    vectors, means = lax.optimization_barrier((vectors, means))
    vectors = exchange(vectors)
    means = gather_stack(means, sizes, [len(sizes) - 1])
    means = means.reshape((count,) + means.shape[-2:])
    mean_order = [0] + inner + [len(sizes) - 1]

    return pl.pallas_call(
        functools.partial(sketch_kernel, sizes, mean_order),
        out_shape=(
            jax.ShapeDtypeStruct((SEQS, 3, rank, rank), F32),
            jax.ShapeDtypeStruct((SEQS, DOMAINS), F32),
        ),
        in_specs=[VMEM] * 3,
        out_specs=(VMEM, VMEM),
        scratch_shapes=[
            pltpu.VMEM((3, count, own_rank * tokens), F32),
            pltpu.VMEM((3, count, DOMAINS, own_rank * tokens), F32),
        ],
        compiler_params=small_kernel(24 if tokens < 256 else 52),
        name="sketches",
    )(vectors, means, slot_order(seq_ids, sizes)[None, :])


def solution(mesh):
    in_specs = (
        P(("groups", "dp"), None),
        P(("groups", "dp"), None),
        P("dp", None),
        P("dp", None),
        P("dp", None),
        P("dp", None),
        P("dp", None),
        P("groups"),
        P(("groups", "dp"), None, None, None),
        P(("groups", "dp")),
    )
    out_specs = (P("groups", None, None, None), P("groups", None))
    return jax.shard_map(
        functools.partial(on_device, mesh.shape["dp"]),
        mesh=mesh,
        in_specs=in_specs,
        out_specs=out_specs,
        check_vma=False,
    )
```

```python
import functools

import jax
import jax.numpy as jnp
import numpy as np
from jax import lax
from jax.experimental import pallas as pl
from jax.experimental.pallas import tpu as pltpu
from jax.sharding import PartitionSpec as P

DOMAINS = 32
SEQS = 16
HIGHEST = lax.Precision.HIGHEST
F32 = jnp.float32
BF16 = jnp.bfloat16
VMEM = pl.BlockSpec(memory_space=pltpu.VMEM)
HBM = pl.BlockSpec(memory_space=pltpu.HBM)


def axis_sizes(count):
    if count == 32:
        return (4, 2, 2, 2)
    if count == 128:
        return (8, 8, 2)
    return (count, 1)


def strides_of(sizes):
    return [int(np.prod(sizes[i + 1 :])) for i in range(len(sizes))]


def shift(value, sizes, axis, amount):
    size, stride = sizes[axis], strides_of(sizes)[axis]
    pairs = []
    for source in range(int(np.prod(sizes))):
        at = (source // stride) % size
        pairs.append((source, source + ((at + amount) % size - at) * stride))
    return lax.ppermute(value, "dp", pairs)


def partner(value, sizes, axis, bit):
    size, stride = sizes[axis], strides_of(sizes)[axis]
    pairs = []
    for source in range(int(np.prod(sizes))):
        at = (source // stride) % size
        pairs.append((source, source + ((at ^ bit) - at) * stride))
    return lax.ppermute(value, "dp", pairs)


def spread_axis(value, sizes, axis):
    if sizes[axis] == 4:
        far, near = partner(value, sizes, axis, 2), partner(value, sizes, axis, 1)
        return [value, near, far, partner(far, sizes, axis, 1)]
    return [value] + [shift(value, sizes, axis, k) for k in range(1, sizes[axis])]


def origin(at, distance, size):
    if size == 4:
        return lax.bitwise_xor(at, distance)
    return lax.rem(at + size - distance, size)


def coordinate(me, sizes, axis):
    return lax.rem(lax.div(me, strides_of(sizes)[axis]), sizes[axis])


def gather_lines(parts, sizes, others):
    rows = parts[0].shape[0]
    both = lax.optimization_barrier(jnp.concatenate(parts, 0))
    blocks = spread_axis(both, sizes, 0)
    lines = [
        jnp.concatenate([block[i * rows : (i + 1) * rows] for block in blocks], 0)
        for i in range(len(parts))
    ]
    made = lax.optimization_barrier((*lines, *others))
    return made[: len(lines)], made[len(lines) :]


def gather_plane(piece, sizes, order):
    backs = [tuple(0 for _ in sizes)]

    def moved(axis, amount):
        return [tuple(amount if i == axis else b for i, b in enumerate(back)) for back in backs]

    for axis in order[:-1]:
        others = spread_axis(piece, sizes, axis)[1:]
        piece = jnp.concatenate([piece] + others, 0)
        backs = sum([moved(axis, k) for k in range(1, sizes[axis])], backs)
    pieces = [(piece, backs)]
    for axis in order[-1:]:
        others = zip(spread_axis(piece, sizes, axis)[1:], range(1, sizes[axis]))
        pieces += [(other, moved(axis, k)) for other, k in others]
    core = len(sizes) - 1
    for piece, backs in list(pieces):
        others = zip(spread_axis(piece, sizes, core)[1:], range(1, sizes[core]))
        pieces += [(other, moved(core, k)) for other, k in others]
    return [piece for piece, _ in pieces], [backs for _, backs in pieces]


def slot_order(per_token, sizes):
    rest = int(np.prod(sizes[1:]))
    return per_token.reshape(sizes[0], rest, -1).transpose(1, 0, 2).reshape(-1)


def exchange(blocks, groups=None):
    return lax.all_to_all(
        blocks, "dp", split_axis=0, concat_axis=0, axis_index_groups=groups, tiled=True
    )


def transposed_dot(left, right, precision=None):
    return lax.dot_general(
        left, right, (((1,), (1,)), ((), ())), precision=precision, preferred_element_type=F32
    )


def place_pieces(pieces, backs, sizes, into):
    me = lax.axis_index("dp")
    for piece, lines in zip(pieces, backs):
        rows = piece.shape[0] // len(lines)
        for i, back in enumerate(lines):
            slot = 0
            for axis in range(1, len(sizes)):
                at = origin(coordinate(me, sizes, axis), back[axis], sizes[axis])
                slot = slot * sizes[axis] + at
            start = pl.multiple_of(slot * rows, rows)
            into[pl.ds(start, rows), :] = piece[i * rows : (i + 1) * rows, :]


def model_side(proj, tokens, model_cols):
    window = proj.shape[1]
    start = lax.div(lax.axis_index("dp") * model_cols, window) * window
    columns = pl.ds(pl.multiple_of(start, window), window)
    return transposed_dot(proj, tokens[:, columns])


def product_kernel(backs, sizes, model_cols, *refs):
    pieces, refs = refs[: len(backs[0])], refs[len(backs[0]) :]
    out_pieces, refs = refs[: len(backs[1])], refs[len(backs[1]) :]
    proj, *weights, out, sums, tokens, stacked, buffers, arrived = refs
    sides = (0, 0, 1)
    depth, _, block, chunk = buffers.shape
    hidden_units, count = sums.shape[1:]
    steps = tokens.shape[2] // chunk
    total = steps * (hidden_units // block)

    part = block // 2 if block % 32 == 0 else block

    def places(step):
        rows = pl.ds(pl.multiple_of(lax.div(step, steps) * block, block), block)
        return rows, pl.ds(pl.multiple_of(lax.rem(step, steps) * chunk, chunk), chunk)

    def copy(step, w):
        slot = lax.rem(step, depth)
        return pltpu.make_async_copy(
            weights[w].at[places(step)], buffers.at[slot, w], arrived.at[slot, w]
        )

    for step in range(min(depth, total)):
        for w in range(3):
            copy(step, w).start()
    place_pieces(pieces, backs[0], sizes, tokens.at[0])
    place_pieces(out_pieces, backs[1], sizes, tokens.at[1])
    sums[...] = jnp.zeros_like(sums)

    @pl.loop(0, total)
    def _(step):
        _, columns = places(step)
        first = lax.div(step, steps) * block
        for w in range(3):
            copy(step, w).wait()
            for i in range(0, block, part):
                rows = pl.ds(pl.multiple_of(first + i, part), part)
                sums[w, rows, :] += transposed_dot(
                    buffers[lax.rem(step, depth), w, i : i + part, :], tokens[sides[w], :, columns]
                )

            @pl.when(step + depth < total)
            def _():
                copy(step + depth, w).start()

    rank = proj.shape[0] // 3
    window = proj.shape[1] - hidden_units
    right = [
        model_side(proj[: 2 * rank, :window], tokens.at[0], model_cols),
        model_side(proj[2 * rank :, :window], tokens.at[1], model_cols),
    ]
    tile = 128 if hidden_units % 128 == 0 else 32

    @pl.loop(0, hidden_units // tile)
    def _(step):
        rows = pl.ds(pl.multiple_of(step * tile, tile), tile)
        gate_value, up_value, grad = sums[0, rows, :], sums[1, rows, :], sums[2, rows, :]
        s = 1.0 / (1.0 + jnp.exp(-gate_value))
        silu = gate_value * s
        stacked[0, rows, :] = (
            grad * up_value * s * (1.0 + gate_value * (1.0 - s))
        ).astype(BF16)
        stacked[1, rows, :] = (grad * silu).astype(BF16)
        stacked[2, rows, :] = (silu * up_value).astype(BF16)

    sides = [
        jnp.dot(proj[p * rank : (p + 1) * rank, window:], stacked[k], preferred_element_type=F32)
        for k, p in enumerate((1, 2, 0))
    ]
    every = jnp.concatenate(sides + right, 0)
    size, each = sizes[0], count // int(np.prod(sizes))
    line = size * each
    source = lax.broadcasted_iota(jnp.int32, (count, count), 0)
    target = lax.broadcasted_iota(jnp.int32, (count, count), 1)
    back = lax.rem(lax.div(source, each), size)
    at = origin(coordinate(lax.axis_index("dp"), sizes, 0), back, size)
    place = lax.div(source, line) * line + at * each + lax.rem(source, each)
    order = (place == target).astype(F32)
    every = jnp.dot(every, order, precision=HIGHEST, preferred_element_type=F32)
    used = every.shape[0] // out.shape[1]
    out[:used] = every.reshape((used,) + out.shape[1:])
    if used < out.shape[0]:
        out[used:] = jnp.zeros_like(out[used:])


def small_kernel(megabytes):
    return pltpu.CompilerParams(vmem_limit_bytes=megabytes * 2**20)


def products(in_pieces, out_pieces, backs, sizes, proj, w_gate, w_up, w_down):
    hidden, width = w_gate.shape
    count = int(np.prod(sizes))
    tokens = sum(piece.shape[0] for piece in in_pieces)
    model_cols = width // count
    chunk = min(width, 2048)
    block = hidden // 2 if hidden % 32 == 0 and hidden > 256 else hidden
    height = 8 * -(-2 * proj.shape[0] // (8 * count))
    return pl.pallas_call(
        functools.partial(product_kernel, backs, sizes, model_cols),
        out_shape=jax.ShapeDtypeStruct((count, height, tokens), F32),
        in_specs=[VMEM] * (len(in_pieces) + len(out_pieces) + 1) + [HBM] * 3,
        out_specs=VMEM,
        scratch_shapes=[
            pltpu.VMEM((3, hidden, tokens), F32),
            pltpu.VMEM((2, tokens, width), BF16),
            pltpu.VMEM((3, hidden, tokens), BF16),
            pltpu.VMEM((2, 3, block, chunk), BF16),
            pltpu.SemaphoreType.DMA((2, 3)),
        ],
        compiler_params=pltpu.CompilerParams(vmem_limit_bytes=40 * 2**20),
        cost_estimate=pl.CostEstimate(
            flops=6 * hidden * width * tokens,
            bytes_accessed=6 * hidden * width,
            transcendentals=hidden * tokens,
        ),
        name="products",
    )(*in_pieces, *out_pieces, proj, w_gate, w_up, w_down)


def sum_kernel(values, out):
    total = values[0]
    for i in range(1, values.shape[0]):
        total += values[i]
    for i in range(out.shape[0]):
        out[i] = total


def sum_copies(values):
    return pl.pallas_call(
        sum_kernel,
        out_shape=jax.ShapeDtypeStruct(values.shape, F32),
        in_specs=[VMEM],
        out_specs=VMEM,
        compiler_params=small_kernel(8),
        name="sum_copies",
    )(values)


def halves(value):
    high = value.astype(BF16)
    return high, (value - high.astype(F32)).astype(BF16)


def rows_of(vectors, rank):
    height, tokens = vectors.shape[1:]
    return vectors[: 6 * rank // height].reshape(6 * rank, tokens)


def onehot_of(ids, tokens):
    return (ids == lax.broadcasted_iota(jnp.int32, (SEQS, tokens), 0)).astype(F32)


def target_kernel(rank, vectors, ids, targets, domains, out):
    tokens = ids.shape[1]
    examples = targets.shape[0]
    every = rows_of(vectors, rank)
    total = jnp.zeros((examples, tokens), F32)
    for k in range(3):
        left = every[k * rank : (k + 1) * rank]
        target = targets[:, k].reshape(examples * rank, rank)
        turned = sum(
            jnp.dot(target, part, preferred_element_type=F32)
            for part in halves(every[(3 + k) * rank : (4 + k) * rank])
        )
        total += jnp.sum(turned.reshape(examples, rank, tokens) * left[None], 1)
    domain = lax.broadcasted_iota(jnp.int32, (DOMAINS, examples), 0)
    domains = (domains[...] == domain).astype(F32)
    total = jnp.dot(domains, total, precision=HIGHEST, preferred_element_type=F32)
    scores = transposed_dot(onehot_of(ids[...], tokens), total, HIGHEST)
    counts = transposed_dot(jnp.ones((SEQS // 2, examples), F32), domains, HIGHEST)
    rest = out.shape[2] - 3 * DOMAINS
    parts = [scores[: SEQS // 2], scores[SEQS // 2 :], counts, jnp.zeros((SEQS // 2, rest), F32)]
    parts = jnp.concatenate(parts, 1)
    for i in range(out.shape[0]):
        out[i] = parts


def sketch_kernel(rank, vectors, ids, sketches, norms):
    tokens = ids.shape[1]
    every = rows_of(vectors, rank)
    masks = jnp.concatenate([onehot_of(ids[...], tokens).astype(BF16)] * 3, 1)
    norm = jnp.zeros((SEQS, 1), F32)
    for k in range(3):
        left_high, left_low = halves(every[k * rank : (k + 1) * rank])
        right_high, right_low = halves(every[(3 + k) * rank : (4 + k) * rank])
        left = jnp.concatenate([left_high, left_high, left_low], 1)
        right = jnp.concatenate([right_high, right_low, right_high], 1)
        rows = jnp.concatenate([left * masks[s : s + 1, :] for s in range(SEQS)], 0)
        sketch = transposed_dot(rows, right).reshape(SEQS, rank, rank)
        sketches[:, k] = sketch
        norm += jnp.sum(jnp.sum(sketch * sketch, 1), 1, keepdims=True)
    norms[...] = jnp.broadcast_to(norm, norms.shape)


def score_kernel(parts, norms, scores):
    total = parts[0]
    for i in range(1, parts.shape[0]):
        total += parts[i]
    counts = total[:, 2 * DOMAINS : 3 * DOMAINS]
    half = SEQS // 2
    for i in range(2):
        mean = total[:, i * DOMAINS : (i + 1) * DOMAINS] / counts
        norm = norms[i * half : (i + 1) * half, :DOMAINS]
        scores[i * half : (i + 1) * half, :] = mean * lax.rsqrt(norm + 1e-06)


def on_device(
    count,
    activations,
    cotangent,
    w_gate,
    w_up,
    w_down,
    proj_model,
    proj_hidden,
    seq_ids,
    targets,
    target_domain,
):
    sizes = axis_sizes(count)
    rank = proj_model.shape[1] // 3
    model_cols = proj_model.shape[0]
    inner = list(range(1, len(sizes) - 1))

    window = max(model_cols, 128)
    proj_m = proj_model.T
    if window > model_cols:
        at = lax.rem(lax.axis_index("dp"), window // model_cols)
        spots = [
            jnp.where(at == i, proj_m, jnp.zeros_like(proj_m)) for i in range(window // model_cols)
        ]
        proj_m = jnp.concatenate(spots, 1)
    proj = jnp.concatenate([proj_m, proj_hidden.T], 1)

    (in_line, out_line), (proj,) = gather_lines([activations, cotangent], sizes, [proj])
    in_pieces, in_backs = gather_plane(in_line, sizes, inner)
    out_pieces, out_backs = gather_plane(out_line, sizes, inner[::-1])
    vectors = products(
        in_pieces, out_pieces, (in_backs, out_backs), sizes, proj, w_gate, w_up, w_down
    )
    vectors = exchange(sum_copies(exchange(vectors)))

    ids = slot_order(seq_ids, sizes)[None, :]
    parts = pl.pallas_call(
        functools.partial(target_kernel, rank),
        out_shape=jax.ShapeDtypeStruct((count, SEQS // 2, 128), F32),
        in_specs=[VMEM] * 4,
        out_specs=VMEM,
        compiler_params=small_kernel(16),
        name="target_products",
    )(vectors, ids, targets, target_domain[None, :])
    parts, vectors = lax.optimization_barrier((parts, vectors))
    parts = exchange(parts)
    sketches, norms = pl.pallas_call(
        functools.partial(sketch_kernel, rank),
        out_shape=(
            jax.ShapeDtypeStruct((SEQS, 3, rank, rank), F32),
            jax.ShapeDtypeStruct((SEQS, 128), F32),
        ),
        in_specs=[VMEM] * 2,
        out_specs=(VMEM, VMEM),
        compiler_params=small_kernel(24),
        name="sketches",
    )(vectors, ids)
    scores = pl.pallas_call(
        score_kernel,
        out_shape=jax.ShapeDtypeStruct((SEQS, DOMAINS), F32),
        in_specs=[VMEM] * 2,
        out_specs=VMEM,
        compiler_params=small_kernel(4),
        name="scores",
    )(parts, norms)
    return sketches, scores


def solution(mesh):
    in_specs = (
        P(("groups", "dp"), None),
        P(("groups", "dp"), None),
        P("dp", None),
        P("dp", None),
        P("dp", None),
        P("dp", None),
        P("dp", None),
        P("groups"),
        P(("groups", "dp"), None, None, None),
        P(("groups", "dp")),
    )
    out_specs = (P("groups", None, None, None), P("groups", None))
    return jax.shard_map(
        functools.partial(on_device, mesh.shape["dp"]),
        mesh=mesh,
        in_specs=in_specs,
        out_specs=out_specs,
        check_vma=False,
    )
```

```python
import functools

import jax
import jax.numpy as jnp
import numpy as np
from jax import lax
from jax.experimental import pallas as pl
from jax.experimental.pallas import tpu as pltpu
from jax.sharding import PartitionSpec as P

DOMAINS = 32
SEQS = 16
HIGHEST = lax.Precision.HIGHEST
F32 = jnp.float32
BF16 = jnp.bfloat16
VMEM = pl.BlockSpec(memory_space=pltpu.VMEM)
HBM = pl.BlockSpec(memory_space=pltpu.HBM)


def axis_sizes(count):
    if count == 32:
        return (4, 2, 2, 2)
    if count == 128:
        return (8, 8, 2)
    return (count, 1)


def strides_of(sizes):
    return [int(np.prod(sizes[i + 1 :])) for i in range(len(sizes))]


def shift(value, sizes, axis, amount):
    size, stride = sizes[axis], strides_of(sizes)[axis]
    pairs = []
    for source in range(int(np.prod(sizes))):
        at = (source // stride) % size
        pairs.append((source, source + ((at + amount) % size - at) * stride))
    return lax.ppermute(value, "dp", pairs)


def coordinate(me, sizes, axis):
    return lax.rem(lax.div(me, strides_of(sizes)[axis]), sizes[axis])


def gather_rows(rows, own, made, sizes, order):
    backs = [tuple(0 for _ in sizes)]

    def moved(axis, amount):
        return [tuple(amount if i == axis else b for i, b in enumerate(back)) for back in backs]

    def received(piece, axis):
        return [shift(piece, sizes, axis, k) for k in range(1, sizes[axis])]

    piece = jnp.concatenate([own] + received(rows, 0), 0)
    piece, *made = lax.optimization_barrier((piece, *made))
    for axis in order[:-1]:
        piece = jnp.concatenate([piece] + received(piece, axis), 0)
        backs = sum([moved(axis, k) for k in range(1, sizes[axis])], backs)
    pieces = [(piece, backs)]
    for axis in order[-1:]:
        others = zip(received(piece, axis), range(1, sizes[axis]))
        pieces += [(other, moved(axis, k)) for other, k in others]
    core = len(sizes) - 1
    for piece, backs in list(pieces):
        others = zip(received(piece, core), range(1, sizes[core]))
        pieces += [(other, moved(core, k)) for other, k in others]
    return [piece for piece, _ in pieces], [backs for _, backs in pieces], made


def slot_order(per_token, sizes):
    rest = int(np.prod(sizes[1:]))
    return per_token.reshape(sizes[0], rest, -1).transpose(1, 0, 2).reshape(-1)


def exchange(blocks, groups=None):
    return lax.all_to_all(
        blocks, "dp", split_axis=0, concat_axis=0, axis_index_groups=groups, tiled=True
    )


def transposed_dot(left, right, precision=None):
    return lax.dot_general(
        left, right, (((1,), (1,)), ((), ())), precision=precision, preferred_element_type=F32
    )


def place_pieces(pieces, backs, sizes, into):
    me = lax.axis_index("dp")
    for piece, lines in zip(pieces, backs):
        rows = piece.shape[0] // len(lines)
        for i, back in enumerate(lines):
            slot = 0
            for axis in range(1, len(sizes)):
                at = coordinate(me, sizes, axis) + sizes[axis] - back[axis]
                slot = slot * sizes[axis] + lax.rem(at, sizes[axis])
            start = pl.multiple_of(slot * rows, rows)
            into[pl.ds(start, rows), :] = piece[i * rows : (i + 1) * rows, :]


def model_side(proj, tokens, model_cols):
    window = proj.shape[1]
    start = lax.div(lax.axis_index("dp") * model_cols, window) * window
    columns = pl.ds(pl.multiple_of(start, window), window)
    return transposed_dot(proj, tokens[:, columns])


def product_kernel(backs, sizes, model_cols, *refs):
    pieces, refs = refs[: len(backs[0])], refs[len(backs[0]) :]
    out_pieces, refs = refs[: len(backs[1])], refs[len(backs[1]) :]
    proj, *weights, out, sums, tokens, stacked, buffers, arrived = refs
    sides = (0, 0, 1)
    depth, _, block, chunk = buffers.shape
    hidden_units, count = sums.shape[1:]
    steps = tokens.shape[2] // chunk
    total = steps * (hidden_units // block)

    def places(step):
        rows = pl.ds(pl.multiple_of(lax.div(step, steps) * block, block), block)
        return rows, pl.ds(pl.multiple_of(lax.rem(step, steps) * chunk, chunk), chunk)

    def copy(step, w):
        slot = lax.rem(step, depth)
        return pltpu.make_async_copy(
            weights[w].at[places(step)], buffers.at[slot, w], arrived.at[slot, w]
        )

    for step in range(min(depth, total)):
        for w in range(3):
            copy(step, w).start()
    place_pieces(pieces, backs[0], sizes, tokens.at[0])
    place_pieces(out_pieces, backs[1], sizes, tokens.at[1])
    sums[...] = jnp.zeros_like(sums)

    @pl.loop(0, total)
    def _(step):
        rows, columns = places(step)
        for w in range(3):
            copy(step, w).wait()
            sums[w, rows, :] += transposed_dot(
                buffers[lax.rem(step, depth), w], tokens[sides[w], :, columns]
            )

            @pl.when(step + depth < total)
            def _():
                copy(step + depth, w).start()

    rank = proj.shape[0] // 3
    window = proj.shape[1] - hidden_units
    right = [
        model_side(proj[: 2 * rank, :window], tokens.at[0], model_cols),
        model_side(proj[2 * rank :, :window], tokens.at[1], model_cols),
    ]
    tile = 128 if hidden_units % 128 == 0 else 32

    @pl.loop(0, hidden_units // tile)
    def _(step):
        rows = pl.ds(pl.multiple_of(step * tile, tile), tile)
        gate_value, up_value, grad = sums[0, rows, :], sums[1, rows, :], sums[2, rows, :]
        s = 1.0 / (1.0 + jnp.exp(-gate_value))
        silu = gate_value * s
        stacked[0, rows, :] = (
            grad * up_value * s * (1.0 + gate_value * (1.0 - s))
        ).astype(BF16)
        stacked[1, rows, :] = (grad * silu).astype(BF16)
        stacked[2, rows, :] = (silu * up_value).astype(BF16)

    sides = [
        jnp.dot(proj[p * rank : (p + 1) * rank, window:], stacked[k], preferred_element_type=F32)
        for k, p in enumerate((1, 2, 0))
    ]
    every = jnp.concatenate(sides + right, 0)
    size, each = sizes[0], count // int(np.prod(sizes))
    line = size * each
    source = lax.broadcasted_iota(jnp.int32, (count, count), 0)
    target = lax.broadcasted_iota(jnp.int32, (count, count), 1)
    back = lax.rem(lax.div(source, each), size)
    at = lax.rem(coordinate(lax.axis_index("dp"), sizes, 0) + size - back, size)
    place = lax.div(source, line) * line + at * each + lax.rem(source, each)
    order = (place == target).astype(F32)
    every = jnp.dot(every, order, precision=HIGHEST, preferred_element_type=F32)
    used = every.shape[0] // out.shape[1]
    out[:used] = every.reshape((used,) + out.shape[1:])
    if used < out.shape[0]:
        out[used:] = jnp.zeros_like(out[used:])


def products(in_pieces, out_pieces, backs, sizes, proj, w_gate, w_up, w_down):
    hidden, width = w_gate.shape
    count = int(np.prod(sizes))
    tokens = sum(piece.shape[0] for piece in in_pieces)
    model_cols = width // count
    chunk = min(width, 2048)
    block = hidden // 2 if hidden % 32 == 0 and hidden > 256 else hidden
    height = 16 * -(-2 * proj.shape[0] // (16 * count))
    return pl.pallas_call(
        functools.partial(product_kernel, backs, sizes, model_cols),
        out_shape=jax.ShapeDtypeStruct((count, height, tokens), F32),
        in_specs=[VMEM] * (len(in_pieces) + len(out_pieces) + 1) + [HBM] * 3,
        out_specs=VMEM,
        scratch_shapes=[
            pltpu.VMEM((3, hidden, tokens), F32),
            pltpu.VMEM((2, tokens, width), BF16),
            pltpu.VMEM((3, hidden, tokens), BF16),
            pltpu.VMEM((2, 3, block, chunk), BF16),
            pltpu.SemaphoreType.DMA((2, 3)),
        ],
        compiler_params=pltpu.CompilerParams(vmem_limit_bytes=44 * 2**20),
        cost_estimate=pl.CostEstimate(
            flops=6 * hidden * width * tokens,
            bytes_accessed=6 * hidden * width,
            transcendentals=hidden * tokens,
        ),
        name="products",
    )(*in_pieces, *out_pieces, proj, w_gate, w_up, w_down)


def small_kernel(megabytes):
    return pltpu.CompilerParams(vmem_limit_bytes=megabytes * 2**20)


def sum_kernel(values, out):
    total = values[0]
    for i in range(1, values.shape[0]):
        total += values[i]
    for i in range(out.shape[0]):
        out[i] = total.astype(BF16)


def sum_copies(values):
    return pl.pallas_call(
        sum_kernel,
        out_shape=jax.ShapeDtypeStruct(values.shape, BF16),
        in_specs=[VMEM],
        out_specs=VMEM,
        compiler_params=small_kernel(8),
        name="sum_copies",
    )(values)


def rows_of(vectors, rank):
    height, tokens = vectors.shape[1:]
    return vectors[: 6 * rank // height].reshape(6 * rank, tokens)


def onehot_of(ids, tokens):
    return (ids == lax.broadcasted_iota(jnp.int32, (SEQS, tokens), 0)).astype(F32)


def target_kernel(rank, vectors, ids, targets, domains, out):
    tokens = ids.shape[1]
    examples = targets.shape[0]
    every = rows_of(vectors, rank)
    total = jnp.zeros((examples, tokens), F32)
    for k in range(3):
        left = every[k * rank : (k + 1) * rank]
        target = targets[:, k].reshape(examples * rank, rank)
        right = every[(3 + k) * rank : (4 + k) * rank]
        turned = jnp.dot(target, right, preferred_element_type=F32)
        total += jnp.sum(turned.reshape(examples, rank, tokens) * left.astype(F32)[None], 1)
    domain = lax.broadcasted_iota(jnp.int32, (DOMAINS, examples), 0)
    domains = (domains[...] == domain).astype(F32)
    total = jnp.dot(domains, total, precision=HIGHEST, preferred_element_type=F32)
    scores = transposed_dot(onehot_of(ids[...], tokens), total, HIGHEST)
    counts = transposed_dot(jnp.ones((SEQS // 2, examples), F32), domains, HIGHEST)
    rest = out.shape[2] - 3 * DOMAINS
    parts = [scores[: SEQS // 2], scores[SEQS // 2 :], counts, jnp.zeros((SEQS // 2, rest), F32)]
    parts = jnp.concatenate(parts, 1)
    for i in range(out.shape[0]):
        out[i] = parts


def sketch_kernel(rank, vectors, ids, sketches, norms):
    tokens = ids.shape[1]
    every = rows_of(vectors, rank)
    masks = onehot_of(ids[...], tokens).astype(BF16)
    norm = jnp.zeros((SEQS, 1), F32)
    for k in range(3):
        left = every[k * rank : (k + 1) * rank]
        right = every[(3 + k) * rank : (4 + k) * rank]
        rows = jnp.concatenate([left * masks[s : s + 1, :] for s in range(SEQS)], 0)
        sketch = transposed_dot(rows, right).reshape(SEQS, rank, rank)
        sketches[:, k] = sketch
        norm += jnp.sum(jnp.sum(sketch * sketch, 1), 1, keepdims=True)
    norms[...] = jnp.broadcast_to(norm, norms.shape)


def score_kernel(parts, norms, scores):
    total = parts[0]
    for i in range(1, parts.shape[0]):
        total += parts[i]
    counts = total[:, 2 * DOMAINS : 3 * DOMAINS]
    half = SEQS // 2
    for i in range(2):
        mean = total[:, i * DOMAINS : (i + 1) * DOMAINS] / counts
        norm = norms[i * half : (i + 1) * half, :DOMAINS]
        scores[i * half : (i + 1) * half, :] = mean * lax.rsqrt(norm + 1e-06)


def on_device(
    count,
    activations,
    cotangent,
    w_gate,
    w_up,
    w_down,
    proj_model,
    proj_hidden,
    seq_ids,
    targets,
    target_domain,
):
    sizes = axis_sizes(count)
    rank = proj_model.shape[1] // 3
    model_cols = proj_model.shape[0]
    tokens = count * activations.shape[0]
    window = max(model_cols, 128)
    proj_m = proj_model.T
    if window > model_cols:
        at = lax.rem(lax.axis_index("dp"), window // model_cols)
        spots = [
            jnp.where(at == i, proj_m, jnp.zeros_like(proj_m)) for i in range(window // model_cols)
        ]
        proj_m = jnp.concatenate(spots, 1)

    proj = jnp.concatenate([proj_m, proj_hidden.T], 1)

    inner = list(range(1, len(sizes) - 1))
    each = activations.shape[0]
    both = lax.optimization_barrier(jnp.concatenate([activations, cotangent], 0))
    in_pieces, in_backs, (proj,) = gather_rows(activations, both[:each], [proj], sizes, inner)
    out_pieces, out_backs, _ = gather_rows(cotangent, both[each:], [], sizes, inner[::-1])

    vectors = products(
        in_pieces, out_pieces, (in_backs, out_backs), sizes, proj, w_gate, w_up, w_down
    )
    vectors = exchange(sum_copies(exchange(vectors)))

    ids = slot_order(seq_ids, sizes)[None, :]
    parts = pl.pallas_call(
        functools.partial(target_kernel, rank),
        out_shape=jax.ShapeDtypeStruct((count, SEQS // 2, 128), F32),
        in_specs=[VMEM] * 4,
        out_specs=VMEM,
        compiler_params=small_kernel(16),
        name="target_products",
    )(vectors, ids, targets, target_domain[None, :])
    parts, vectors = lax.optimization_barrier((parts, vectors))
    parts = exchange(parts)
    sketches, norms = pl.pallas_call(
        functools.partial(sketch_kernel, rank),
        out_shape=(
            jax.ShapeDtypeStruct((SEQS, 3, rank, rank), F32),
            jax.ShapeDtypeStruct((SEQS, 128), F32),
        ),
        in_specs=[VMEM] * 2,
        out_specs=(VMEM, VMEM),
        compiler_params=small_kernel(24),
        name="sketches",
    )(vectors, ids)
    scores = pl.pallas_call(
        score_kernel,
        out_shape=jax.ShapeDtypeStruct((SEQS, DOMAINS), F32),
        in_specs=[VMEM] * 2,
        out_specs=VMEM,
        compiler_params=small_kernel(4),
        name="scores",
    )(parts, norms)
    return sketches, scores


def solution(mesh):
    in_specs = (
        P(("groups", "dp"), None),
        P(("groups", "dp"), None),
        P("dp", None),
        P("dp", None),
        P("dp", None),
        P("dp", None),
        P("dp", None),
        P("groups"),
        P(("groups", "dp"), None, None, None),
        P(("groups", "dp")),
    )
    out_specs = (P("groups", None, None, None), P("groups", None))
    return jax.shard_map(
        functools.partial(on_device, mesh.shape["dp"]),
        mesh=mesh,
        in_specs=in_specs,
        out_specs=out_specs,
        check_vma=False,
    )
```

```python
import functools

import jax
import jax.numpy as jnp
import numpy as np
from jax import lax
from jax.experimental import pallas as pl
from jax.experimental.pallas import tpu as pltpu
from jax.sharding import PartitionSpec as P

DOMAINS = 32
SEQS = 16
HIGHEST = lax.Precision.HIGHEST
F32 = jnp.float32
BF16 = jnp.bfloat16
VMEM = pl.BlockSpec(memory_space=pltpu.VMEM)
HBM = pl.BlockSpec(memory_space=pltpu.HBM)


def axis_sizes(count):
    if count == 32:
        return (4, 2, 2, 2)
    if count == 128:
        return (8, 8, 2)
    return (count, 1)


def strides_of(sizes):
    return [int(np.prod(sizes[i + 1 :])) for i in range(len(sizes))]


def shift(value, sizes, axis, amount):
    size, stride = sizes[axis], strides_of(sizes)[axis]
    pairs = []
    for source in range(int(np.prod(sizes))):
        at = (source // stride) % size
        pairs.append((source, source + ((at + amount) % size - at) * stride))
    return lax.ppermute(value, "dp", pairs)


def partner(value, sizes, axis, bit):
    size, stride = sizes[axis], strides_of(sizes)[axis]
    pairs = []
    for source in range(int(np.prod(sizes))):
        at = (source // stride) % size
        pairs.append((source, source + ((at ^ bit) - at) * stride))
    return lax.ppermute(value, "dp", pairs)


def spread_axis(value, sizes, axis):
    if sizes[axis] == 4:
        far, near = partner(value, sizes, axis, 2), partner(value, sizes, axis, 1)
        return [value, near, far, partner(far, sizes, axis, 1)]
    return [value] + [shift(value, sizes, axis, k) for k in range(1, sizes[axis])]


def origin(at, distance, size):
    if size == 4:
        return lax.bitwise_xor(at, distance)
    return lax.rem(at + size - distance, size)


def coordinate(me, sizes, axis):
    return lax.rem(lax.div(me, strides_of(sizes)[axis]), sizes[axis])


def gather_rows(rows, own, made, sizes, order):
    backs = [tuple(0 for _ in sizes)]

    def moved(axis, amount):
        return [tuple(amount if i == axis else b for i, b in enumerate(back)) for back in backs]

    piece = jnp.concatenate([own] + spread_axis(rows, sizes, 0)[1:], 0)
    piece, *made = lax.optimization_barrier((piece, *made))
    for axis in order[:-1]:
        piece = jnp.concatenate([piece] + spread_axis(piece, sizes, axis)[1:], 0)
        backs = sum([moved(axis, k) for k in range(1, sizes[axis])], backs)
    pieces = [(piece, backs)]
    for axis in order[-1:]:
        others = zip(spread_axis(piece, sizes, axis)[1:], range(1, sizes[axis]))
        pieces += [(other, moved(axis, k)) for other, k in others]
    core = len(sizes) - 1
    for piece, backs in list(pieces):
        others = zip(spread_axis(piece, sizes, core)[1:], range(1, sizes[core]))
        pieces += [(other, moved(core, k)) for other, k in others]
    return [piece for piece, _ in pieces], [backs for _, backs in pieces], made


def slot_order(per_token, sizes):
    rest = int(np.prod(sizes[1:]))
    return per_token.reshape(sizes[0], rest, -1).transpose(1, 0, 2).reshape(-1)


def exchange(blocks, groups=None):
    return lax.all_to_all(
        blocks, "dp", split_axis=0, concat_axis=0, axis_index_groups=groups, tiled=True
    )


def transposed_dot(left, right, precision=None):
    return lax.dot_general(
        left, right, (((1,), (1,)), ((), ())), precision=precision, preferred_element_type=F32
    )


def place_pieces(pieces, backs, sizes, into):
    me = lax.axis_index("dp")
    for piece, lines in zip(pieces, backs):
        rows = piece.shape[0] // len(lines)
        for i, back in enumerate(lines):
            slot = 0
            for axis in range(1, len(sizes)):
                at = origin(coordinate(me, sizes, axis), back[axis], sizes[axis])
                slot = slot * sizes[axis] + at
            start = pl.multiple_of(slot * rows, rows)
            into[pl.ds(start, rows), :] = piece[i * rows : (i + 1) * rows, :]


def model_side(proj, tokens, model_cols):
    window = proj.shape[1]
    start = lax.div(lax.axis_index("dp") * model_cols, window) * window
    columns = pl.ds(pl.multiple_of(start, window), window)
    return transposed_dot(proj, tokens[:, columns])


def repeated(used, count):
    return [*range(used // 2, used), *range(used // 2)][: count - used]


def product_kernel(backs, sizes, model_cols, *refs):
    pieces, refs = refs[: len(backs[0])], refs[len(backs[0]) :]
    out_pieces, refs = refs[: len(backs[1])], refs[len(backs[1]) :]
    proj, *weights, out, sums, tokens, stacked, buffers, arrived = refs
    sides = (0, 0, 1)
    depth, _, block, chunk = buffers.shape
    hidden_units, count = sums.shape[1:]
    steps = tokens.shape[2] // chunk
    total = steps * (hidden_units // block)

    def places(step):
        rows = pl.ds(pl.multiple_of(lax.div(step, steps) * block, block), block)
        return rows, pl.ds(pl.multiple_of(lax.rem(step, steps) * chunk, chunk), chunk)

    def copy(step, w):
        slot = lax.rem(step, depth)
        return pltpu.make_async_copy(
            weights[w].at[places(step)], buffers.at[slot, w], arrived.at[slot, w]
        )

    for step in range(min(depth, total)):
        for w in range(3):
            copy(step, w).start()
    place_pieces(pieces, backs[0], sizes, tokens.at[0])
    place_pieces(out_pieces, backs[1], sizes, tokens.at[1])
    sums[...] = jnp.zeros_like(sums)

    @pl.loop(0, total)
    def _(step):
        rows, columns = places(step)
        for w in range(3):
            copy(step, w).wait()
            sums[w, rows, :] += transposed_dot(
                buffers[lax.rem(step, depth), w], tokens[sides[w], :, columns]
            )

            @pl.when(step + depth < total)
            def _():
                copy(step + depth, w).start()

    rank = proj.shape[0] // 3
    window = proj.shape[1] - hidden_units
    right = [
        model_side(proj[: 2 * rank, :window], tokens.at[0], model_cols),
        model_side(proj[2 * rank :, :window], tokens.at[1], model_cols),
    ]
    tile = 128 if hidden_units % 128 == 0 else 32

    @pl.loop(0, hidden_units // tile)
    def _(step):
        rows = pl.ds(pl.multiple_of(step * tile, tile), tile)
        gate_value, up_value, grad = sums[0, rows, :], sums[1, rows, :], sums[2, rows, :]
        s = 1.0 / (1.0 + jnp.exp(-gate_value))
        silu = gate_value * s
        stacked[0, rows, :] = (
            grad * up_value * s * (1.0 + gate_value * (1.0 - s))
        ).astype(BF16)
        stacked[1, rows, :] = (grad * silu).astype(BF16)
        stacked[2, rows, :] = (silu * up_value).astype(BF16)

    sides = [
        jnp.dot(proj[p * rank : (p + 1) * rank, window:], stacked[k], preferred_element_type=F32)
        for k, p in enumerate((1, 2, 0))
    ]
    every = jnp.concatenate(sides + right, 0)
    size, each = sizes[0], count // int(np.prod(sizes))
    line = size * each
    source = lax.broadcasted_iota(jnp.int32, (count, count), 0)
    target = lax.broadcasted_iota(jnp.int32, (count, count), 1)
    back = lax.rem(lax.div(source, each), size)
    at = origin(coordinate(lax.axis_index("dp"), sizes, 0), back, size)
    place = lax.div(source, line) * line + at * each + lax.rem(source, each)
    order = (place == target).astype(F32)
    every = jnp.dot(every, order, precision=HIGHEST, preferred_element_type=F32)
    used = every.shape[0] // out.shape[1]
    every = every.reshape((used,) + out.shape[1:])
    out[:used] = every
    again = repeated(used, out.shape[0])
    for i, block in enumerate(again):
        out[used + i] = every[block]
    if used + len(again) < out.shape[0]:
        out[used + len(again) :] = jnp.zeros_like(out[used + len(again) :])


def products(in_pieces, out_pieces, backs, sizes, proj, w_gate, w_up, w_down):
    hidden, width = w_gate.shape
    count = int(np.prod(sizes))
    tokens = sum(piece.shape[0] for piece in in_pieces)
    model_cols = width // count
    chunk = min(width, 2048)
    block = hidden // 2 if hidden % 32 == 0 and hidden > 256 else hidden
    height = 16 * -(-2 * proj.shape[0] // (16 * count))
    return pl.pallas_call(
        functools.partial(product_kernel, backs, sizes, model_cols),
        out_shape=jax.ShapeDtypeStruct((count, height, tokens), F32),
        in_specs=[VMEM] * (len(in_pieces) + len(out_pieces) + 1) + [HBM] * 3,
        out_specs=VMEM,
        scratch_shapes=[
            pltpu.VMEM((3, hidden, tokens), F32),
            pltpu.VMEM((2, tokens, width), BF16),
            pltpu.VMEM((3, hidden, tokens), BF16),
            pltpu.VMEM((2, 3, block, chunk), BF16),
            pltpu.SemaphoreType.DMA((2, 3)),
        ],
        compiler_params=pltpu.CompilerParams(vmem_limit_bytes=44 * 2**20),
        cost_estimate=pl.CostEstimate(
            flops=6 * hidden * width * tokens,
            bytes_accessed=6 * hidden * width,
            transcendentals=hidden * tokens,
        ),
        name="products",
    )(*in_pieces, *out_pieces, proj, w_gate, w_up, w_down)


def small_kernel(megabytes):
    return pltpu.CompilerParams(vmem_limit_bytes=megabytes * 2**20)


def sum_kernel(used, values, out):
    total = values[0]
    for i in range(1, values.shape[0]):
        total += values[i]
    rounded = total.astype(BF16)
    spare = lax.axis_index("dp") >= used
    rounded = jnp.where(spare, total - rounded.astype(F32), total).astype(BF16)
    for i in range(out.shape[0]):
        out[i] = rounded


def sum_copies(values, used):
    return pl.pallas_call(
        functools.partial(sum_kernel, used),
        out_shape=jax.ShapeDtypeStruct(values.shape, BF16),
        in_specs=[VMEM],
        out_specs=VMEM,
        compiler_params=small_kernel(8),
        name="sum_copies",
    )(values)


def sides_of(vectors, rank):
    height, tokens = vectors.shape[1:]
    used = 6 * rank // height
    every = vectors[:used].reshape(6 * rank, tokens)
    again = repeated(used, vectors.shape[0])[: used // 2]
    rest = vectors[used : used + len(again)].reshape(-1, tokens) if again else every[:0]
    sides = []
    for k in range(3):
        rights = [every[(3 + k) * rank : (4 + k) * rank]]
        if rest.shape[0] >= (k + 1) * rank:
            rights.append(rest[k * rank : (k + 1) * rank])
        sides.append((every[k * rank : (k + 1) * rank], rights))
    return sides


def onehot_of(ids, tokens):
    return (ids == lax.broadcasted_iota(jnp.int32, (SEQS, tokens), 0)).astype(F32)


def target_kernel(rank, vectors, ids, targets, domains, out):
    tokens = ids.shape[1]
    examples = targets.shape[0]
    total = jnp.zeros((examples, tokens), F32)
    for k, (left, rights) in enumerate(sides_of(vectors, rank)):
        target = targets[:, k].reshape(examples * rank, rank)
        turned = sum(jnp.dot(target, right, preferred_element_type=F32) for right in rights)
        total += jnp.sum(turned.reshape(examples, rank, tokens) * left.astype(F32)[None], 1)
    domain = lax.broadcasted_iota(jnp.int32, (DOMAINS, examples), 0)
    domains = (domains[...] == domain).astype(F32)
    total = jnp.dot(domains, total, precision=HIGHEST, preferred_element_type=F32)
    scores = transposed_dot(onehot_of(ids[...], tokens), total, HIGHEST)
    counts = transposed_dot(jnp.ones((SEQS // 2, examples), F32), domains, HIGHEST)
    rest = out.shape[2] - 3 * DOMAINS
    parts = [scores[: SEQS // 2], scores[SEQS // 2 :], counts, jnp.zeros((SEQS // 2, rest), F32)]
    parts = jnp.concatenate(parts, 1)
    for i in range(out.shape[0]):
        out[i] = parts


def sketch_kernel(rank, vectors, ids, sketches, norms):
    tokens = ids.shape[1]
    masks = onehot_of(ids[...], tokens).astype(BF16)
    norm = jnp.zeros((SEQS, 1), F32)
    for k, (left, rights) in enumerate(sides_of(vectors, rank)):
        rows = jnp.concatenate([left * masks[s : s + 1, :] for s in range(SEQS)], 0)
        sketch = sum(transposed_dot(rows, right) for right in rights)
        sketch = sketch.reshape(SEQS, rank, rank)
        sketches[:, k] = sketch
        norm += jnp.sum(jnp.sum(sketch * sketch, 1), 1, keepdims=True)
    norms[...] = jnp.broadcast_to(norm, norms.shape)


def score_kernel(parts, norms, scores):
    total = parts[0]
    for i in range(1, parts.shape[0]):
        total += parts[i]
    counts = total[:, 2 * DOMAINS : 3 * DOMAINS]
    half = SEQS // 2
    for i in range(2):
        mean = total[:, i * DOMAINS : (i + 1) * DOMAINS] / counts
        norm = norms[i * half : (i + 1) * half, :DOMAINS]
        scores[i * half : (i + 1) * half, :] = mean * lax.rsqrt(norm + 1e-06)


def on_device(
    count,
    activations,
    cotangent,
    w_gate,
    w_up,
    w_down,
    proj_model,
    proj_hidden,
    seq_ids,
    targets,
    target_domain,
):
    sizes = axis_sizes(count)
    rank = proj_model.shape[1] // 3
    model_cols = proj_model.shape[0]
    tokens = count * activations.shape[0]
    window = max(model_cols, 128)
    proj_m = proj_model.T
    if window > model_cols:
        at = lax.rem(lax.axis_index("dp"), window // model_cols)
        spots = [
            jnp.where(at == i, proj_m, jnp.zeros_like(proj_m)) for i in range(window // model_cols)
        ]
        proj_m = jnp.concatenate(spots, 1)

    proj = jnp.concatenate([proj_m, proj_hidden.T], 1)

    inner = list(range(1, len(sizes) - 1))
    each = activations.shape[0]
    both = lax.optimization_barrier(jnp.concatenate([activations, cotangent], 0))
    in_pieces, in_backs, (proj,) = gather_rows(activations, both[:each], [proj], sizes, inner)
    out_pieces, out_backs, _ = gather_rows(cotangent, both[each:], [], sizes, inner[::-1])

    vectors = products(
        in_pieces, out_pieces, (in_backs, out_backs), sizes, proj, w_gate, w_up, w_down
    )
    vectors = exchange(vectors)
    vectors = exchange(sum_copies(vectors, 6 * rank // vectors.shape[1]))

    ids = slot_order(seq_ids, sizes)[None, :]
    parts = pl.pallas_call(
        functools.partial(target_kernel, rank),
        out_shape=jax.ShapeDtypeStruct((count, SEQS // 2, 128), F32),
        in_specs=[VMEM] * 4,
        out_specs=VMEM,
        compiler_params=small_kernel(16),
        name="target_products",
    )(vectors, ids, targets, target_domain[None, :])
    parts, vectors = lax.optimization_barrier((parts, vectors))
    parts = exchange(parts)
    sketches, norms = pl.pallas_call(
        functools.partial(sketch_kernel, rank),
        out_shape=(
            jax.ShapeDtypeStruct((SEQS, 3, rank, rank), F32),
            jax.ShapeDtypeStruct((SEQS, 128), F32),
        ),
        in_specs=[VMEM] * 2,
        out_specs=(VMEM, VMEM),
        compiler_params=small_kernel(24),
        name="sketches",
    )(vectors, ids)
    scores = pl.pallas_call(
        score_kernel,
        out_shape=jax.ShapeDtypeStruct((SEQS, DOMAINS), F32),
        in_specs=[VMEM] * 2,
        out_specs=VMEM,
        compiler_params=small_kernel(4),
        name="scores",
    )(parts, norms)
    return sketches, scores


def solution(mesh):
    in_specs = (
        P(("groups", "dp"), None),
        P(("groups", "dp"), None),
        P("dp", None),
        P("dp", None),
        P("dp", None),
        P("dp", None),
        P("dp", None),
        P("groups"),
        P(("groups", "dp"), None, None, None),
        P(("groups", "dp")),
    )
    out_specs = (P("groups", None, None, None), P("groups", None))
    return jax.shard_map(
        functools.partial(on_device, mesh.shape["dp"]),
        mesh=mesh,
        in_specs=in_specs,
        out_specs=out_specs,
        check_vma=False,
    )
```

```python
import functools

import jax
import jax.numpy as jnp
import numpy as np
from jax import lax
from jax.experimental import pallas as pl
from jax.experimental.pallas import tpu as pltpu
from jax.sharding import PartitionSpec as P

DOMAINS = 32
SEQS = 16
HIGHEST = lax.Precision.HIGHEST
F32 = jnp.float32
BF16 = jnp.bfloat16
VMEM = pl.BlockSpec(memory_space=pltpu.VMEM)
HBM = pl.BlockSpec(memory_space=pltpu.HBM)


def axis_sizes(count):
    if count == 32:
        return (4, 2, 2, 2)
    if count == 128:
        return (8, 8, 2)
    return (count, 1)


def strides_of(sizes):
    return [int(np.prod(sizes[i + 1 :])) for i in range(len(sizes))]


def shift(value, sizes, axis, amount):
    size, stride = sizes[axis], strides_of(sizes)[axis]
    pairs = []
    for source in range(int(np.prod(sizes))):
        at = (source // stride) % size
        pairs.append((source, source + ((at + amount) % size - at) * stride))
    return lax.ppermute(value, "dp", pairs)


def partner(value, sizes, axis, bit):
    size, stride = sizes[axis], strides_of(sizes)[axis]
    pairs = []
    for source in range(int(np.prod(sizes))):
        at = (source // stride) % size
        pairs.append((source, source + ((at ^ bit) - at) * stride))
    return lax.ppermute(value, "dp", pairs)


def spread_axis(value, sizes, axis):
    if sizes[axis] == 4:
        far, near = partner(value, sizes, axis, 2), partner(value, sizes, axis, 1)
        return [value, near, far, partner(far, sizes, axis, 1)]
    return [value] + [shift(value, sizes, axis, k) for k in range(1, sizes[axis])]


def origin(at, distance, size):
    if size == 4:
        return lax.bitwise_xor(at, distance)
    return lax.rem(at + size - distance, size)


def coordinate(me, sizes, axis):
    return lax.rem(lax.div(me, strides_of(sizes)[axis]), sizes[axis])


def gather_rows(rows, own, made, sizes, order):
    backs = [tuple(0 for _ in sizes)]

    def moved(axis, amount):
        return [tuple(amount if i == axis else b for i, b in enumerate(back)) for back in backs]

    piece = jnp.concatenate([own] + spread_axis(rows, sizes, 0)[1:], 0)
    piece, *made = lax.optimization_barrier((piece, *made))
    for axis in order[:-1]:
        piece = jnp.concatenate([piece] + spread_axis(piece, sizes, axis)[1:], 0)
        backs = sum([moved(axis, k) for k in range(1, sizes[axis])], backs)
    pieces = [(piece, backs)]
    for axis in order[-1:]:
        others = zip(spread_axis(piece, sizes, axis)[1:], range(1, sizes[axis]))
        pieces += [(other, moved(axis, k)) for other, k in others]
    core = len(sizes) - 1
    for piece, backs in list(pieces):
        others = zip(spread_axis(piece, sizes, core)[1:], range(1, sizes[core]))
        pieces += [(other, moved(core, k)) for other, k in others]
    return [piece for piece, _ in pieces], [backs for _, backs in pieces], made


def slot_order(per_token, sizes):
    rest = int(np.prod(sizes[1:]))
    return per_token.reshape(sizes[0], rest, -1).transpose(1, 0, 2).reshape(-1)


def exchange(blocks, groups=None):
    return lax.all_to_all(
        blocks, "dp", split_axis=0, concat_axis=0, axis_index_groups=groups, tiled=True
    )


def transposed_dot(left, right, precision=None):
    return lax.dot_general(
        left, right, (((1,), (1,)), ((), ())), precision=precision, preferred_element_type=F32
    )


def place_pieces(pieces, backs, sizes, into):
    me = lax.axis_index("dp")
    for piece, lines in zip(pieces, backs):
        rows = piece.shape[0] // len(lines)
        for i, back in enumerate(lines):
            slot = 0
            for axis in range(1, len(sizes)):
                at = origin(coordinate(me, sizes, axis), back[axis], sizes[axis])
                slot = slot * sizes[axis] + at
            start = pl.multiple_of(slot * rows, rows)
            into[pl.ds(start, rows), :] = piece[i * rows : (i + 1) * rows, :]


def model_side(proj, tokens, model_cols):
    window = proj.shape[1]
    start = lax.div(lax.axis_index("dp") * model_cols, window) * window
    columns = pl.ds(pl.multiple_of(start, window), window)
    return transposed_dot(proj, tokens[:, columns])


def repeated(used, count):
    return [*range(used // 2, used), *range(used // 2)][: count - used]


def product_kernel(backs, sizes, model_cols, *refs):
    pieces, refs = refs[: len(backs[0])], refs[len(backs[0]) :]
    out_pieces, refs = refs[: len(backs[1])], refs[len(backs[1]) :]
    proj, *weights, out, sums, tokens, stacked, buffers, arrived = refs
    sides = (0, 0, 1)
    depth, _, block, chunk = buffers.shape
    hidden_units, count = sums.shape[1:]
    steps = tokens.shape[2] // chunk
    total = steps * (hidden_units // block)

    def places(step):
        rows = pl.ds(pl.multiple_of(lax.div(step, steps) * block, block), block)
        return rows, pl.ds(pl.multiple_of(lax.rem(step, steps) * chunk, chunk), chunk)

    def copy(step, w):
        slot = lax.rem(step, depth)
        return pltpu.make_async_copy(
            weights[w].at[places(step)], buffers.at[slot, w], arrived.at[slot, w]
        )

    for step in range(min(depth, total)):
        for w in range(3):
            copy(step, w).start()
    place_pieces(pieces, backs[0], sizes, tokens.at[0])
    place_pieces(out_pieces, backs[1], sizes, tokens.at[1])
    sums[...] = jnp.zeros_like(sums)

    @pl.loop(0, total)
    def _(step):
        rows, columns = places(step)
        for w in range(3):
            copy(step, w).wait()
            sums[w, rows, :] += transposed_dot(
                buffers[lax.rem(step, depth), w], tokens[sides[w], :, columns]
            )

            @pl.when(step + depth < total)
            def _():
                copy(step + depth, w).start()

    rank = proj.shape[0] // 3
    window = proj.shape[1] - hidden_units
    right = [
        model_side(proj[: 2 * rank, :window], tokens.at[0], model_cols),
        model_side(proj[2 * rank :, :window], tokens.at[1], model_cols),
    ]
    tile = 128 if hidden_units % 128 == 0 else 32

    @pl.loop(0, hidden_units // tile)
    def _(step):
        rows = pl.ds(pl.multiple_of(step * tile, tile), tile)
        gate_value, up_value, grad = sums[0, rows, :], sums[1, rows, :], sums[2, rows, :]
        s = 1.0 / (1.0 + jnp.exp(-gate_value))
        silu = gate_value * s
        stacked[0, rows, :] = (
            grad * up_value * s * (1.0 + gate_value * (1.0 - s))
        ).astype(BF16)
        stacked[1, rows, :] = (grad * silu).astype(BF16)
        stacked[2, rows, :] = (silu * up_value).astype(BF16)

    sides = [
        jnp.dot(proj[p * rank : (p + 1) * rank, window:], stacked[k], preferred_element_type=F32)
        for k, p in enumerate((1, 2, 0))
    ]
    every = jnp.concatenate(sides + right, 0)
    size, each = sizes[0], count // int(np.prod(sizes))
    line = size * each
    source = lax.broadcasted_iota(jnp.int32, (count, count), 0)
    target = lax.broadcasted_iota(jnp.int32, (count, count), 1)
    back = lax.rem(lax.div(source, each), size)
    at = origin(coordinate(lax.axis_index("dp"), sizes, 0), back, size)
    place = lax.div(source, line) * line + at * each + lax.rem(source, each)
    order = (place == target).astype(F32)
    every = jnp.dot(every, order, precision=HIGHEST, preferred_element_type=F32)
    used = every.shape[0] // out.shape[1]
    every = every.reshape((used,) + out.shape[1:])
    out[:used] = every
    again = repeated(used, out.shape[0])
    for i, block in enumerate(again):
        out[used + i] = every[block]
    if used + len(again) < out.shape[0]:
        out[used + len(again) :] = jnp.zeros_like(out[used + len(again) :])


def products(in_pieces, out_pieces, backs, sizes, proj, w_gate, w_up, w_down):
    hidden, width = w_gate.shape
    count = int(np.prod(sizes))
    tokens = sum(piece.shape[0] for piece in in_pieces)
    model_cols = width // count
    chunk = min(width, 1024)
    block = hidden // 2 if hidden % 32 == 0 and hidden > 256 else hidden
    height = 16 * -(-2 * proj.shape[0] // (16 * count))
    return pl.pallas_call(
        functools.partial(product_kernel, backs, sizes, model_cols),
        out_shape=jax.ShapeDtypeStruct((count, height, tokens), F32),
        in_specs=[VMEM] * (len(in_pieces) + len(out_pieces) + 1) + [HBM] * 3,
        out_specs=VMEM,
        scratch_shapes=[
            pltpu.VMEM((3, hidden, tokens), F32),
            pltpu.VMEM((2, tokens, width), BF16),
            pltpu.VMEM((3, hidden, tokens), BF16),
            pltpu.VMEM((4, 3, block, chunk), BF16),
            pltpu.SemaphoreType.DMA((4, 3)),
        ],
        compiler_params=pltpu.CompilerParams(vmem_limit_bytes=44 * 2**20),
        cost_estimate=pl.CostEstimate(
            flops=6 * hidden * width * tokens,
            bytes_accessed=6 * hidden * width,
            transcendentals=hidden * tokens,
        ),
        name="products",
    )(*in_pieces, *out_pieces, proj, w_gate, w_up, w_down)


def small_kernel(megabytes):
    return pltpu.CompilerParams(vmem_limit_bytes=megabytes * 2**20)


def sum_kernel(used, values, out):
    total = values[0]
    for i in range(1, values.shape[0]):
        total += values[i]
    rounded = total.astype(BF16)
    spare = lax.axis_index("dp") >= used
    rounded = jnp.where(spare, total - rounded.astype(F32), total).astype(BF16)
    for i in range(out.shape[0]):
        out[i] = rounded


def sum_copies(values, used):
    return pl.pallas_call(
        functools.partial(sum_kernel, used),
        out_shape=jax.ShapeDtypeStruct(values.shape, BF16),
        in_specs=[VMEM],
        out_specs=VMEM,
        compiler_params=small_kernel(8),
        name="sum_copies",
    )(values)


def sides_of(vectors, rank):
    height, tokens = vectors.shape[1:]
    used = 6 * rank // height
    every = vectors[:used].reshape(6 * rank, tokens)
    again = repeated(used, vectors.shape[0])[: used // 2]
    rest = vectors[used : used + len(again)].reshape(-1, tokens) if again else every[:0]
    sides = []
    for k in range(3):
        rights = [every[(3 + k) * rank : (4 + k) * rank]]
        if rest.shape[0] >= (k + 1) * rank:
            rights.append(rest[k * rank : (k + 1) * rank])
        sides.append((every[k * rank : (k + 1) * rank], rights))
    return sides


def onehot_of(ids, tokens):
    return (ids == lax.broadcasted_iota(jnp.int32, (SEQS, tokens), 0)).astype(F32)


def target_kernel(rank, vectors, ids, targets, domains, out):
    tokens = ids.shape[1]
    examples = targets.shape[0]
    total = jnp.zeros((examples, tokens), F32)
    for k, (left, rights) in enumerate(sides_of(vectors, rank)):
        target = targets[:, k].reshape(examples * rank, rank)
        turned = sum(jnp.dot(target, right, preferred_element_type=F32) for right in rights)
        total += jnp.sum(turned.reshape(examples, rank, tokens) * left.astype(F32)[None], 1)
    domain = lax.broadcasted_iota(jnp.int32, (DOMAINS, examples), 0)
    domains = (domains[...] == domain).astype(F32)
    total = sum(domains[:, e : e + 1] * total[e : e + 1, :] for e in range(examples))
    scores = transposed_dot(onehot_of(ids[...], tokens), total, HIGHEST)
    counts = transposed_dot(jnp.ones((SEQS // 2, examples), BF16), domains.astype(BF16))
    rest = out.shape[2] - 3 * DOMAINS
    parts = [scores[: SEQS // 2], scores[SEQS // 2 :], counts, jnp.zeros((SEQS // 2, rest), F32)]
    parts = jnp.concatenate(parts, 1)
    for i in range(out.shape[0]):
        out[i] = parts


def sketch_kernel(rank, vectors, ids, sketches, norms):
    tokens = ids.shape[1]
    masks = onehot_of(ids[...], tokens).astype(BF16)
    norm = jnp.zeros((SEQS, 1), F32)
    for k, (left, rights) in enumerate(sides_of(vectors, rank)):
        rows = jnp.concatenate([left * masks[s : s + 1, :] for s in range(SEQS)], 0)
        sketch = sum(transposed_dot(rows, right) for right in rights)
        sketch = sketch.reshape(SEQS, rank, rank)
        sketches[:, k] = sketch
        norm += jnp.sum(jnp.sum(sketch * sketch, 1), 1, keepdims=True)
    norms[...] = jnp.broadcast_to(norm, norms.shape)


def score_kernel(parts, norms, scores):
    total = parts[0]
    for i in range(1, parts.shape[0]):
        total += parts[i]
    counts = total[:, 2 * DOMAINS : 3 * DOMAINS]
    half = SEQS // 2
    for i in range(2):
        mean = total[:, i * DOMAINS : (i + 1) * DOMAINS] / counts
        norm = norms[i * half : (i + 1) * half, :DOMAINS]
        scores[i * half : (i + 1) * half, :] = mean * lax.rsqrt(norm + 1e-06)


def on_device(
    count,
    activations,
    cotangent,
    w_gate,
    w_up,
    w_down,
    proj_model,
    proj_hidden,
    seq_ids,
    targets,
    target_domain,
):
    sizes = axis_sizes(count)
    rank = proj_model.shape[1] // 3
    model_cols = proj_model.shape[0]
    tokens = count * activations.shape[0]
    window = max(model_cols, 128)
    proj_m = proj_model.T
    if window > model_cols:
        at = lax.rem(lax.axis_index("dp"), window // model_cols)
        spots = [
            jnp.where(at == i, proj_m, jnp.zeros_like(proj_m)) for i in range(window // model_cols)
        ]
        proj_m = jnp.concatenate(spots, 1)

    proj = jnp.concatenate([proj_m, proj_hidden.T], 1)

    inner = list(range(1, len(sizes) - 1))
    each = activations.shape[0]
    both = lax.optimization_barrier(jnp.concatenate([activations, cotangent], 0))
    in_pieces, in_backs, (proj,) = gather_rows(activations, both[:each], [proj], sizes, inner)
    out_pieces, out_backs, _ = gather_rows(cotangent, both[each:], [], sizes, inner[::-1])

    vectors = products(
        in_pieces, out_pieces, (in_backs, out_backs), sizes, proj, w_gate, w_up, w_down
    )
    vectors = exchange(vectors)
    vectors = exchange(sum_copies(vectors, 6 * rank // vectors.shape[1]))

    ids = slot_order(seq_ids, sizes)[None, :]
    parts = pl.pallas_call(
        functools.partial(target_kernel, rank),
        out_shape=jax.ShapeDtypeStruct((count, SEQS // 2, 128), F32),
        in_specs=[VMEM] * 4,
        out_specs=VMEM,
        compiler_params=small_kernel(16),
        name="target_products",
    )(vectors, ids, targets, target_domain[None, :])
    parts, vectors = lax.optimization_barrier((parts, vectors))
    parts = exchange(parts)
    sketches, norms = pl.pallas_call(
        functools.partial(sketch_kernel, rank),
        out_shape=(
            jax.ShapeDtypeStruct((SEQS, 3, rank, rank), F32),
            jax.ShapeDtypeStruct((SEQS, 128), F32),
        ),
        in_specs=[VMEM] * 2,
        out_specs=(VMEM, VMEM),
        compiler_params=small_kernel(24),
        name="sketches",
    )(vectors, ids)
    scores = pl.pallas_call(
        score_kernel,
        out_shape=jax.ShapeDtypeStruct((SEQS, DOMAINS), F32),
        in_specs=[VMEM] * 2,
        out_specs=VMEM,
        compiler_params=small_kernel(4),
        name="scores",
    )(parts, norms)
    return sketches, scores


def solution(mesh):
    in_specs = (
        P(("groups", "dp"), None),
        P(("groups", "dp"), None),
        P("dp", None),
        P("dp", None),
        P("dp", None),
        P("dp", None),
        P("dp", None),
        P("groups"),
        P(("groups", "dp"), None, None, None),
        P(("groups", "dp")),
    )
    out_specs = (P("groups", None, None, None), P("groups", None))
    return jax.shard_map(
        functools.partial(on_device, mesh.shape["dp"]),
        mesh=mesh,
        in_specs=in_specs,
        out_specs=out_specs,
        check_vma=False,
    )
```

```python
import functools

import jax
import jax.numpy as jnp
import numpy as np
from jax import lax
from jax.experimental import pallas as pl
from jax.experimental.pallas import tpu as pltpu
from jax.sharding import PartitionSpec as P

DOMAINS = 32
SEQS = 16
HIGHEST = lax.Precision.HIGHEST
F32 = jnp.float32
BF16 = jnp.bfloat16
VMEM = pl.BlockSpec(memory_space=pltpu.VMEM)
HBM = pl.BlockSpec(memory_space=pltpu.HBM)


def axis_sizes(count):
    if count == 32:
        return (4, 2, 2, 2)
    if count == 128:
        return (8, 8, 2)
    return (count, 1)


def strides_of(sizes):
    return [int(np.prod(sizes[i + 1 :])) for i in range(len(sizes))]


def shift(value, sizes, axis, amount):
    size, stride = sizes[axis], strides_of(sizes)[axis]
    pairs = []
    for source in range(int(np.prod(sizes))):
        at = (source // stride) % size
        pairs.append((source, source + ((at + amount) % size - at) * stride))
    return lax.ppermute(value, "dp", pairs)


def partner(value, sizes, axis, bit):
    size, stride = sizes[axis], strides_of(sizes)[axis]
    pairs = []
    for source in range(int(np.prod(sizes))):
        at = (source // stride) % size
        pairs.append((source, source + ((at ^ bit) - at) * stride))
    return lax.ppermute(value, "dp", pairs)


def spread_axis(value, sizes, axis):
    if sizes[axis] == 4:
        far, near = partner(value, sizes, axis, 2), partner(value, sizes, axis, 1)
        return [value, near, far, partner(far, sizes, axis, 1)]
    return [value] + [shift(value, sizes, axis, k) for k in range(1, sizes[axis])]


def origin(at, distance, size):
    if size == 4:
        return lax.bitwise_xor(at, distance)
    return lax.rem(at + size - distance, size)


def coordinate(me, sizes, axis):
    return lax.rem(lax.div(me, strides_of(sizes)[axis]), sizes[axis])


def gather_rows(rows, own, made, sizes, order):
    backs = [tuple(0 for _ in sizes)]

    def moved(axis, amount):
        return [tuple(amount if i == axis else b for i, b in enumerate(back)) for back in backs]

    piece = jnp.concatenate([own] + spread_axis(rows, sizes, 0)[1:], 0)
    piece, *made = lax.optimization_barrier((piece, *made))
    for axis in order[:-1]:
        piece = jnp.concatenate([piece] + spread_axis(piece, sizes, axis)[1:], 0)
        backs = sum([moved(axis, k) for k in range(1, sizes[axis])], backs)
    pieces = [(piece, backs)]
    for axis in order[-1:]:
        others = zip(spread_axis(piece, sizes, axis)[1:], range(1, sizes[axis]))
        pieces += [(other, moved(axis, k)) for other, k in others]
    core = len(sizes) - 1
    for piece, backs in list(pieces):
        others = zip(spread_axis(piece, sizes, core)[1:], range(1, sizes[core]))
        pieces += [(other, moved(core, k)) for other, k in others]
    return [piece for piece, _ in pieces], [backs for _, backs in pieces], made


def slot_order(per_token, sizes):
    rest = int(np.prod(sizes[1:]))
    return per_token.reshape(sizes[0], rest, -1).transpose(1, 0, 2).reshape(-1)


def exchange(blocks, groups=None):
    return lax.all_to_all(
        blocks, "dp", split_axis=0, concat_axis=0, axis_index_groups=groups, tiled=True
    )


def transposed_dot(left, right, precision=None):
    return lax.dot_general(
        left, right, (((1,), (1,)), ((), ())), precision=precision, preferred_element_type=F32
    )


def place_pieces(pieces, backs, sizes, into):
    me = lax.axis_index("dp")
    for piece, lines in zip(pieces, backs):
        rows = piece.shape[0] // len(lines)
        for i, back in enumerate(lines):
            slot = 0
            for axis in range(1, len(sizes)):
                at = origin(coordinate(me, sizes, axis), back[axis], sizes[axis])
                slot = slot * sizes[axis] + at
            start = pl.multiple_of(slot * rows, rows)
            into[pl.ds(start, rows), :] = piece[i * rows : (i + 1) * rows, :]


def model_side(proj, tokens, model_cols):
    window = proj.shape[1]
    start = lax.div(lax.axis_index("dp") * model_cols, window) * window
    columns = pl.ds(pl.multiple_of(start, window), window)
    return transposed_dot(proj, tokens[:, columns])


def repeated(used, count):
    return [*range(used // 2, used), *range(used // 2)][: count - used]


def product_kernel(backs, sizes, model_cols, *refs):
    pieces, refs = refs[: len(backs[0])], refs[len(backs[0]) :]
    out_pieces, refs = refs[: len(backs[1])], refs[len(backs[1]) :]
    proj, *weights, out, sums, tokens, stacked, buffers, arrived = refs
    sides = (0, 0, 1)
    depth, _, block, chunk = buffers.shape
    hidden_units, count = sums.shape[1:]
    steps = tokens.shape[2] // chunk
    total = steps * (hidden_units // block)

    def places(step):
        rows = pl.ds(pl.multiple_of(lax.div(step, steps) * block, block), block)
        return rows, pl.ds(pl.multiple_of(lax.rem(step, steps) * chunk, chunk), chunk)

    def copy(step, w):
        slot = lax.rem(step, depth)
        return pltpu.make_async_copy(
            weights[w].at[places(step)], buffers.at[slot, w], arrived.at[slot, w]
        )

    for step in range(min(depth, total)):
        for w in range(3):
            copy(step, w).start()
    place_pieces(pieces, backs[0], sizes, tokens.at[0])
    place_pieces(out_pieces, backs[1], sizes, tokens.at[1])
    sums[...] = jnp.zeros_like(sums)

    def add(step, w):
        rows, columns = places(step)
        sums[w, rows, :] += transposed_dot(
            buffers[lax.rem(step, depth), w], tokens[sides[w], :, columns]
        )

    def refill(step):
        @pl.when(step + depth < total)
        def _():
            for w in range(3):
                copy(step + depth, w).start()

    for w in range(3):
        copy(0, w).wait()
        add(0, w)
    refill(0)

    @pl.loop(1, total)
    def _(step):
        for w in range(3):
            copy(step, w).wait()
        for w in range(3):
            add(step, w)
        refill(step)

    rank = proj.shape[0] // 3
    window = proj.shape[1] - hidden_units
    right = [
        model_side(proj[: 2 * rank, :window], tokens.at[0], model_cols),
        model_side(proj[2 * rank :, :window], tokens.at[1], model_cols),
    ]
    tile = 128 if hidden_units % 128 == 0 else 32

    @pl.loop(0, hidden_units // tile)
    def _(step):
        rows = pl.ds(pl.multiple_of(step * tile, tile), tile)
        gate_value, up_value, grad = sums[0, rows, :], sums[1, rows, :], sums[2, rows, :]
        s = 1.0 / (1.0 + jnp.exp(-gate_value))
        silu = gate_value * s
        stacked[0, rows, :] = (
            grad * up_value * s * (1.0 + gate_value * (1.0 - s))
        ).astype(BF16)
        stacked[1, rows, :] = (grad * silu).astype(BF16)
        stacked[2, rows, :] = (silu * up_value).astype(BF16)

    sides = [
        jnp.dot(proj[p * rank : (p + 1) * rank, window:], stacked[k], preferred_element_type=F32)
        for k, p in enumerate((1, 2, 0))
    ]
    every = jnp.concatenate(sides + right, 0)
    size, each = sizes[0], count // int(np.prod(sizes))
    line = size * each
    source = lax.broadcasted_iota(jnp.int32, (count, count), 0)
    target = lax.broadcasted_iota(jnp.int32, (count, count), 1)
    back = lax.rem(lax.div(source, each), size)
    at = origin(coordinate(lax.axis_index("dp"), sizes, 0), back, size)
    place = lax.div(source, line) * line + at * each + lax.rem(source, each)
    order = (place == target).astype(F32)
    every = jnp.dot(every, order, precision=HIGHEST, preferred_element_type=F32)
    used = every.shape[0] // out.shape[1]
    every = every.reshape((used,) + out.shape[1:])
    out[:used] = every
    again = repeated(used, out.shape[0])
    for i, block in enumerate(again):
        out[used + i] = every[block]
    if used + len(again) < out.shape[0]:
        out[used + len(again) :] = jnp.zeros_like(out[used + len(again) :])


def products(in_pieces, out_pieces, backs, sizes, proj, w_gate, w_up, w_down):
    hidden, width = w_gate.shape
    count = int(np.prod(sizes))
    tokens = sum(piece.shape[0] for piece in in_pieces)
    model_cols = width // count
    chunk = min(width, 2048)
    block = hidden // 2 if hidden % 32 == 0 and hidden > 256 else hidden
    height = 16 * -(-2 * proj.shape[0] // (16 * count))
    return pl.pallas_call(
        functools.partial(product_kernel, backs, sizes, model_cols),
        out_shape=jax.ShapeDtypeStruct((count, height, tokens), F32),
        in_specs=[VMEM] * (len(in_pieces) + len(out_pieces) + 1) + [HBM] * 3,
        out_specs=VMEM,
        scratch_shapes=[
            pltpu.VMEM((3, hidden, tokens), F32),
            pltpu.VMEM((2, tokens, width), BF16),
            pltpu.VMEM((3, hidden, tokens), BF16),
            pltpu.VMEM((3, 3, block, chunk), BF16),
            pltpu.SemaphoreType.DMA((3, 3)),
        ],
        compiler_params=pltpu.CompilerParams(vmem_limit_bytes=44 * 2**20),
        cost_estimate=pl.CostEstimate(
            flops=6 * hidden * width * tokens,
            bytes_accessed=6 * hidden * width,
            transcendentals=hidden * tokens,
        ),
        name="products",
    )(*in_pieces, *out_pieces, proj, w_gate, w_up, w_down)


def small_kernel(megabytes):
    return pltpu.CompilerParams(vmem_limit_bytes=megabytes * 2**20)


def sum_kernel(used, values, out):
    total = values[0]
    for i in range(1, values.shape[0]):
        total += values[i]
    rounded = total.astype(BF16)
    spare = lax.axis_index("dp") >= used
    rounded = jnp.where(spare, total - rounded.astype(F32), total).astype(BF16)
    for i in range(out.shape[0]):
        out[i] = rounded


def sum_copies(values, used):
    return pl.pallas_call(
        functools.partial(sum_kernel, used),
        out_shape=jax.ShapeDtypeStruct(values.shape, BF16),
        in_specs=[VMEM],
        out_specs=VMEM,
        compiler_params=small_kernel(8),
        name="sum_copies",
    )(values)


def sides_of(vectors, rank):
    height, tokens = vectors.shape[1:]
    used = 6 * rank // height
    every = vectors[:used].reshape(6 * rank, tokens)
    again = repeated(used, vectors.shape[0])[: used // 2]
    rest = vectors[used : used + len(again)].reshape(-1, tokens) if again else every[:0]
    sides = []
    for k in range(3):
        rights = [every[(3 + k) * rank : (4 + k) * rank]]
        if rest.shape[0] >= (k + 1) * rank:
            rights.append(rest[k * rank : (k + 1) * rank])
        sides.append((every[k * rank : (k + 1) * rank], rights))
    return sides


def onehot_of(ids, tokens):
    return (ids == lax.broadcasted_iota(jnp.int32, (SEQS, tokens), 0)).astype(F32)


def target_kernel(rank, vectors, ids, targets, domains, out):
    tokens = ids.shape[1]
    examples = targets.shape[0]
    total = jnp.zeros((examples, tokens), F32)
    for k, (left, rights) in enumerate(sides_of(vectors, rank)):
        target = targets[:, k].reshape(examples * rank, rank)
        turned = sum(jnp.dot(target, right, preferred_element_type=F32) for right in rights)
        total += jnp.sum(turned.reshape(examples, rank, tokens) * left.astype(F32)[None], 1)
    domain = lax.broadcasted_iota(jnp.int32, (DOMAINS, examples), 0)
    domains = (domains[...] == domain).astype(F32)
    total = sum(domains[:, e : e + 1] * total[e : e + 1, :] for e in range(examples))
    scores = transposed_dot(onehot_of(ids[...], tokens), total, HIGHEST)
    counts = transposed_dot(jnp.ones((SEQS // 2, examples), BF16), domains.astype(BF16))
    rest = out.shape[2] - 3 * DOMAINS
    parts = [scores[: SEQS // 2], scores[SEQS // 2 :], counts, jnp.zeros((SEQS // 2, rest), F32)]
    parts = jnp.concatenate(parts, 1)
    for i in range(out.shape[0]):
        out[i] = parts


def sketch_kernel(rank, vectors, ids, sketches, norms):
    tokens = ids.shape[1]
    masks = onehot_of(ids[...], tokens).astype(BF16)
    norm = jnp.zeros((SEQS, 1), F32)
    for k, (left, rights) in enumerate(sides_of(vectors, rank)):
        rows = jnp.concatenate([left * masks[s : s + 1, :] for s in range(SEQS)], 0)
        sketch = sum(transposed_dot(rows, right) for right in rights)
        sketch = sketch.reshape(SEQS, rank, rank)
        sketches[:, k] = sketch
        norm += jnp.sum(jnp.sum(sketch * sketch, 1), 1, keepdims=True)
    norms[...] = jnp.broadcast_to(norm, norms.shape)


def score_kernel(parts, norms, scores):
    total = parts[0]
    for i in range(1, parts.shape[0]):
        total += parts[i]
    counts = total[:, 2 * DOMAINS : 3 * DOMAINS]
    half = SEQS // 2
    for i in range(2):
        mean = total[:, i * DOMAINS : (i + 1) * DOMAINS] / counts
        norm = norms[i * half : (i + 1) * half, :DOMAINS]
        scores[i * half : (i + 1) * half, :] = mean * lax.rsqrt(norm + 1e-06)


def on_device(
    count,
    activations,
    cotangent,
    w_gate,
    w_up,
    w_down,
    proj_model,
    proj_hidden,
    seq_ids,
    targets,
    target_domain,
):
    sizes = axis_sizes(count)
    rank = proj_model.shape[1] // 3
    model_cols = proj_model.shape[0]
    tokens = count * activations.shape[0]
    window = max(model_cols, 128)
    proj_m = proj_model.T
    if window > model_cols:
        at = lax.rem(lax.axis_index("dp"), window // model_cols)
        spots = [
            jnp.where(at == i, proj_m, jnp.zeros_like(proj_m)) for i in range(window // model_cols)
        ]
        proj_m = jnp.concatenate(spots, 1)

    proj = jnp.concatenate([proj_m, proj_hidden.T], 1)

    inner = list(range(1, len(sizes) - 1))
    each = activations.shape[0]
    both = lax.optimization_barrier(jnp.concatenate([activations, cotangent], 0))
    in_pieces, in_backs, (proj,) = gather_rows(activations, both[:each], [proj], sizes, inner)
    out_pieces, out_backs, _ = gather_rows(cotangent, both[each:], [], sizes, inner[::-1])

    vectors = products(
        in_pieces, out_pieces, (in_backs, out_backs), sizes, proj, w_gate, w_up, w_down
    )
    vectors = exchange(vectors)
    vectors = exchange(sum_copies(vectors, 6 * rank // vectors.shape[1]))

    ids = slot_order(seq_ids, sizes)[None, :]
    parts = pl.pallas_call(
        functools.partial(target_kernel, rank),
        out_shape=jax.ShapeDtypeStruct((count, SEQS // 2, 128), F32),
        in_specs=[VMEM] * 4,
        out_specs=VMEM,
        compiler_params=small_kernel(16),
        name="target_products",
    )(vectors, ids, targets, target_domain[None, :])
    parts, vectors = lax.optimization_barrier((parts, vectors))
    parts = exchange(parts)
    sketches, norms = pl.pallas_call(
        functools.partial(sketch_kernel, rank),
        out_shape=(
            jax.ShapeDtypeStruct((SEQS, 3, rank, rank), F32),
            jax.ShapeDtypeStruct((SEQS, 128), F32),
        ),
        in_specs=[VMEM] * 2,
        out_specs=(VMEM, VMEM),
        compiler_params=small_kernel(24),
        name="sketches",
    )(vectors, ids)
    scores = pl.pallas_call(
        score_kernel,
        out_shape=jax.ShapeDtypeStruct((SEQS, DOMAINS), F32),
        in_specs=[VMEM] * 2,
        out_specs=VMEM,
        compiler_params=small_kernel(4),
        name="scores",
    )(parts, norms)
    return sketches, scores


def solution(mesh):
    in_specs = (
        P(("groups", "dp"), None),
        P(("groups", "dp"), None),
        P("dp", None),
        P("dp", None),
        P("dp", None),
        P("dp", None),
        P("dp", None),
        P("groups"),
        P(("groups", "dp"), None, None, None),
        P(("groups", "dp")),
    )
    out_specs = (P("groups", None, None, None), P("groups", None))
    return jax.shard_map(
        functools.partial(on_device, mesh.shape["dp"]),
        mesh=mesh,
        in_specs=in_specs,
        out_specs=out_specs,
        check_vma=False,
    )
```

```python
import functools

import jax
import jax.numpy as jnp
import numpy as np
from jax import lax
from jax.experimental import pallas as pl
from jax.experimental.pallas import tpu as pltpu
from jax.sharding import PartitionSpec as P

DOMAINS = 32
SEQS = 16
HIGHEST = lax.Precision.HIGHEST
F32 = jnp.float32
BF16 = jnp.bfloat16
VMEM = pl.BlockSpec(memory_space=pltpu.VMEM)
HBM = pl.BlockSpec(memory_space=pltpu.HBM)


def axis_sizes(count):
    if count == 32:
        return (4, 2, 2, 2)
    if count == 128:
        return (8, 8, 2)
    return (count, 1)


def strides_of(sizes):
    return [int(np.prod(sizes[i + 1 :])) for i in range(len(sizes))]


def shift(value, sizes, axis, amount):
    size, stride = sizes[axis], strides_of(sizes)[axis]
    pairs = []
    for source in range(int(np.prod(sizes))):
        at = (source // stride) % size
        pairs.append((source, source + ((at + amount) % size - at) * stride))
    return lax.ppermute(value, "dp", pairs)


def partner(value, sizes, axis, bit):
    size, stride = sizes[axis], strides_of(sizes)[axis]
    pairs = []
    for source in range(int(np.prod(sizes))):
        at = (source // stride) % size
        pairs.append((source, source + ((at ^ bit) - at) * stride))
    return lax.ppermute(value, "dp", pairs)


def spread_axis(value, sizes, axis):
    if sizes[axis] == 4:
        far, near = partner(value, sizes, axis, 2), partner(value, sizes, axis, 1)
        return [value, near, far, partner(far, sizes, axis, 1)]
    return [value] + [shift(value, sizes, axis, k) for k in range(1, sizes[axis])]


def origin(at, distance, size):
    if size == 4:
        return lax.bitwise_xor(at, distance)
    return lax.rem(at + size - distance, size)


def coordinate(me, sizes, axis):
    return lax.rem(lax.div(me, strides_of(sizes)[axis]), sizes[axis])


def gather_rows(rows, own, made, sizes, order):
    backs = [tuple(0 for _ in sizes)]

    def moved(axis, amount):
        return [tuple(amount if i == axis else b for i, b in enumerate(back)) for back in backs]

    piece = jnp.concatenate([own] + spread_axis(rows, sizes, 0)[1:], 0)
    piece, *made = lax.optimization_barrier((piece, *made))
    for axis in order[:-1]:
        piece = jnp.concatenate([piece] + spread_axis(piece, sizes, axis)[1:], 0)
        backs = sum([moved(axis, k) for k in range(1, sizes[axis])], backs)
    pieces = [(piece, backs)]
    for axis in order[-1:]:
        others = zip(spread_axis(piece, sizes, axis)[1:], range(1, sizes[axis]))
        pieces += [(other, moved(axis, k)) for other, k in others]
    core = len(sizes) - 1
    for piece, backs in list(pieces):
        others = zip(spread_axis(piece, sizes, core)[1:], range(1, sizes[core]))
        pieces += [(other, moved(core, k)) for other, k in others]
    return [piece for piece, _ in pieces], [backs for _, backs in pieces], made


def slot_order(per_token, sizes):
    rest = int(np.prod(sizes[1:]))
    return per_token.reshape(sizes[0], rest, -1).transpose(1, 0, 2).reshape(-1)


def exchange(blocks, groups=None):
    return lax.all_to_all(
        blocks, "dp", split_axis=0, concat_axis=0, axis_index_groups=groups, tiled=True
    )


def transposed_dot(left, right, precision=None):
    return lax.dot_general(
        left, right, (((1,), (1,)), ((), ())), precision=precision, preferred_element_type=F32
    )


def place_pieces(pieces, backs, sizes, into):
    me = lax.axis_index("dp")
    for piece, lines in zip(pieces, backs):
        rows = piece.shape[0] // len(lines)
        for i, back in enumerate(lines):
            slot = 0
            for axis in range(1, len(sizes)):
                at = origin(coordinate(me, sizes, axis), back[axis], sizes[axis])
                slot = slot * sizes[axis] + at
            start = pl.multiple_of(slot * rows, rows)
            into[pl.ds(start, rows), :] = piece[i * rows : (i + 1) * rows, :]


def model_side(proj, tokens, model_cols):
    window = proj.shape[1]
    start = lax.div(lax.axis_index("dp") * model_cols, window) * window
    columns = pl.ds(pl.multiple_of(start, window), window)
    return transposed_dot(proj, tokens[:, columns])


def repeated(used, count):
    return [*range(used // 2, used), *range(used // 2)][: count - used]


def product_kernel(backs, sizes, model_cols, *refs):
    pieces, refs = refs[: len(backs[0])], refs[len(backs[0]) :]
    out_pieces, refs = refs[: len(backs[1])], refs[len(backs[1]) :]
    proj, *weights, out, sums, tokens, stacked, buffers, arrived = refs
    sides = (0, 0, 1)
    depth, _, block, chunk = buffers.shape
    hidden_units, count = sums.shape[1:]
    steps = tokens.shape[2] // chunk
    total = steps * (hidden_units // block)

    def places(step):
        rows = pl.ds(pl.multiple_of(lax.div(step, steps) * block, block), block)
        return rows, pl.ds(pl.multiple_of(lax.rem(step, steps) * chunk, chunk), chunk)

    def copy(step, w):
        slot = lax.rem(step, depth)
        return pltpu.make_async_copy(
            weights[w].at[places(step)], buffers.at[slot, w], arrived.at[slot, w]
        )

    for step in range(min(depth, total)):
        for w in range(3):
            copy(step, w).start()
    place_pieces(pieces, backs[0], sizes, tokens.at[0])
    place_pieces(out_pieces, backs[1], sizes, tokens.at[1])
    sums[...] = jnp.zeros_like(sums)

    def add(step, w):
        rows, columns = places(step)
        sums[w, rows, :] += transposed_dot(
            buffers[lax.rem(step, depth), w], tokens[sides[w], :, columns]
        )

    def refill(step):
        @pl.when(step + depth < total)
        def _():
            for w in range(3):
                copy(step + depth, w).start()

    def add_both(step):
        rows, columns = places(step)
        pair = buffers[lax.rem(step, depth), :2].reshape(2 * block, chunk)
        part = transposed_dot(pair, tokens[0, :, columns])
        sums[:2, rows, :] += part.reshape(2, block, count)

    for w in range(3):
        copy(0, w).wait()
        add(0, w)
    refill(0)

    @pl.loop(1, total)
    def _(step):
        for w in range(3):
            copy(step, w).wait()
        add_both(step)
        add(step, 2)
        refill(step)

    rank = proj.shape[0] // 3
    window = proj.shape[1] - hidden_units
    right = [
        model_side(proj[: 2 * rank, :window], tokens.at[0], model_cols),
        model_side(proj[2 * rank :, :window], tokens.at[1], model_cols),
    ]
    tile = 128 if hidden_units % 128 == 0 else 32

    @pl.loop(0, hidden_units // tile)
    def _(step):
        rows = pl.ds(pl.multiple_of(step * tile, tile), tile)
        gate_value, up_value, grad = sums[0, rows, :], sums[1, rows, :], sums[2, rows, :]
        s = 1.0 / (1.0 + jnp.exp(-gate_value))
        silu = gate_value * s
        stacked[0, rows, :] = (
            grad * up_value * s * (1.0 + gate_value * (1.0 - s))
        ).astype(BF16)
        stacked[1, rows, :] = (grad * silu).astype(BF16)
        stacked[2, rows, :] = (silu * up_value).astype(BF16)

    sides = [
        jnp.dot(proj[p * rank : (p + 1) * rank, window:], stacked[k], preferred_element_type=F32)
        for k, p in enumerate((1, 2, 0))
    ]
    every = jnp.concatenate(sides + right, 0)
    size, each = sizes[0], count // int(np.prod(sizes))
    line = size * each
    source = lax.broadcasted_iota(jnp.int32, (count, count), 0)
    target = lax.broadcasted_iota(jnp.int32, (count, count), 1)
    back = lax.rem(lax.div(source, each), size)
    at = origin(coordinate(lax.axis_index("dp"), sizes, 0), back, size)
    place = lax.div(source, line) * line + at * each + lax.rem(source, each)
    order = (place == target).astype(F32)
    every = jnp.dot(every, order, precision=HIGHEST, preferred_element_type=F32)
    used = every.shape[0] // out.shape[1]
    every = every.reshape((used,) + out.shape[1:])
    out[:used] = every
    again = repeated(used, out.shape[0])
    for i, block in enumerate(again):
        out[used + i] = every[block]
    if used + len(again) < out.shape[0]:
        out[used + len(again) :] = jnp.zeros_like(out[used + len(again) :])


def products(in_pieces, out_pieces, backs, sizes, proj, w_gate, w_up, w_down):
    hidden, width = w_gate.shape
    count = int(np.prod(sizes))
    tokens = sum(piece.shape[0] for piece in in_pieces)
    model_cols = width // count
    chunk = min(width, 2048)
    block = hidden // 2 if hidden % 32 == 0 and hidden > 256 else hidden
    height = 16 * -(-2 * proj.shape[0] // (16 * count))
    return pl.pallas_call(
        functools.partial(product_kernel, backs, sizes, model_cols),
        out_shape=jax.ShapeDtypeStruct((count, height, tokens), F32),
        in_specs=[VMEM] * (len(in_pieces) + len(out_pieces) + 1) + [HBM] * 3,
        out_specs=VMEM,
        scratch_shapes=[
            pltpu.VMEM((3, hidden, tokens), F32),
            pltpu.VMEM((2, tokens, width), BF16),
            pltpu.VMEM((3, hidden, tokens), BF16),
            pltpu.VMEM((3, 3, block, chunk), BF16),
            pltpu.SemaphoreType.DMA((3, 3)),
        ],
        compiler_params=pltpu.CompilerParams(vmem_limit_bytes=44 * 2**20),
        cost_estimate=pl.CostEstimate(
            flops=6 * hidden * width * tokens,
            bytes_accessed=6 * hidden * width,
            transcendentals=hidden * tokens,
        ),
        name="products",
    )(*in_pieces, *out_pieces, proj, w_gate, w_up, w_down)


def small_kernel(megabytes):
    return pltpu.CompilerParams(vmem_limit_bytes=megabytes * 2**20)


def sum_kernel(used, values, out):
    total = values[0]
    for i in range(1, values.shape[0]):
        total += values[i]
    rounded = total.astype(BF16)
    spare = lax.axis_index("dp") >= used
    rounded = jnp.where(spare, total - rounded.astype(F32), total).astype(BF16)
    for i in range(out.shape[0]):
        out[i] = rounded


def sum_copies(values, used):
    return pl.pallas_call(
        functools.partial(sum_kernel, used),
        out_shape=jax.ShapeDtypeStruct(values.shape, BF16),
        in_specs=[VMEM],
        out_specs=VMEM,
        compiler_params=small_kernel(8),
        name="sum_copies",
    )(values)


def sides_of(vectors, rank):
    height, tokens = vectors.shape[1:]
    used = 6 * rank // height
    every = vectors[:used].reshape(6 * rank, tokens)
    again = repeated(used, vectors.shape[0])[: used // 2]
    rest = vectors[used : used + len(again)].reshape(-1, tokens) if again else every[:0]
    sides = []
    for k in range(3):
        rights = [every[(3 + k) * rank : (4 + k) * rank]]
        if rest.shape[0] >= (k + 1) * rank:
            rights.append(rest[k * rank : (k + 1) * rank])
        sides.append((every[k * rank : (k + 1) * rank], rights))
    return sides


def onehot_of(ids, tokens):
    return (ids == lax.broadcasted_iota(jnp.int32, (SEQS, tokens), 0)).astype(F32)


def target_kernel(rank, vectors, ids, targets, domains, out):
    tokens = ids.shape[1]
    examples = targets.shape[0]
    total = jnp.zeros((examples, tokens), F32)
    for k, (left, rights) in enumerate(sides_of(vectors, rank)):
        target = targets[:, k].reshape(examples * rank, rank)
        turned = sum(jnp.dot(target, right, preferred_element_type=F32) for right in rights)
        total += jnp.sum(turned.reshape(examples, rank, tokens) * left.astype(F32)[None], 1)
    domain = lax.broadcasted_iota(jnp.int32, (DOMAINS, examples), 0)
    domains = (domains[...] == domain).astype(F32)
    total = sum(domains[:, e : e + 1] * total[e : e + 1, :] for e in range(examples))
    scores = transposed_dot(onehot_of(ids[...], tokens), total, HIGHEST)
    counts = transposed_dot(jnp.ones((SEQS // 2, examples), BF16), domains.astype(BF16))
    rest = out.shape[2] - 3 * DOMAINS
    parts = [scores[: SEQS // 2], scores[SEQS // 2 :], counts, jnp.zeros((SEQS // 2, rest), F32)]
    parts = jnp.concatenate(parts, 1)
    for i in range(out.shape[0]):
        out[i] = parts


def sketch_kernel(rank, vectors, ids, sketches, norms):
    tokens = ids.shape[1]
    masks = onehot_of(ids[...], tokens).astype(BF16)
    norm = jnp.zeros((SEQS, 1), F32)
    for k, (left, rights) in enumerate(sides_of(vectors, rank)):
        rows = jnp.concatenate([left * masks[s : s + 1, :] for s in range(SEQS)], 0)
        sketch = sum(transposed_dot(rows, right) for right in rights)
        sketch = sketch.reshape(SEQS, rank, rank)
        sketches[:, k] = sketch
        norm += jnp.sum(jnp.sum(sketch * sketch, 1), 1, keepdims=True)
    norms[...] = jnp.broadcast_to(norm, norms.shape)


def score_kernel(parts, norms, scores):
    total = parts[0]
    for i in range(1, parts.shape[0]):
        total += parts[i]
    counts = total[:, 2 * DOMAINS : 3 * DOMAINS]
    half = SEQS // 2
    for i in range(2):
        mean = total[:, i * DOMAINS : (i + 1) * DOMAINS] / counts
        norm = norms[i * half : (i + 1) * half, :DOMAINS]
        scores[i * half : (i + 1) * half, :] = mean * lax.rsqrt(norm + 1e-06)


def on_device(
    count,
    activations,
    cotangent,
    w_gate,
    w_up,
    w_down,
    proj_model,
    proj_hidden,
    seq_ids,
    targets,
    target_domain,
):
    sizes = axis_sizes(count)
    rank = proj_model.shape[1] // 3
    model_cols = proj_model.shape[0]
    tokens = count * activations.shape[0]
    window = max(model_cols, 128)
    proj_m = proj_model.T
    if window > model_cols:
        at = lax.rem(lax.axis_index("dp"), window // model_cols)
        spots = [
            jnp.where(at == i, proj_m, jnp.zeros_like(proj_m)) for i in range(window // model_cols)
        ]
        proj_m = jnp.concatenate(spots, 1)

    proj = jnp.concatenate([proj_m, proj_hidden.T], 1)

    inner = list(range(1, len(sizes) - 1))
    each = activations.shape[0]
    both = lax.optimization_barrier(jnp.concatenate([activations, cotangent], 0))
    in_pieces, in_backs, (proj,) = gather_rows(activations, both[:each], [proj], sizes, inner)
    out_pieces, out_backs, _ = gather_rows(cotangent, both[each:], [], sizes, inner[::-1])

    vectors = products(
        in_pieces, out_pieces, (in_backs, out_backs), sizes, proj, w_gate, w_up, w_down
    )
    vectors = exchange(vectors)
    vectors = exchange(sum_copies(vectors, 6 * rank // vectors.shape[1]))

    ids = slot_order(seq_ids, sizes)[None, :]
    parts = pl.pallas_call(
        functools.partial(target_kernel, rank),
        out_shape=jax.ShapeDtypeStruct((count, SEQS // 2, 128), F32),
        in_specs=[VMEM] * 4,
        out_specs=VMEM,
        compiler_params=small_kernel(16),
        name="target_products",
    )(vectors, ids, targets, target_domain[None, :])
    parts, vectors = lax.optimization_barrier((parts, vectors))
    parts = exchange(parts)
    sketches, norms = pl.pallas_call(
        functools.partial(sketch_kernel, rank),
        out_shape=(
            jax.ShapeDtypeStruct((SEQS, 3, rank, rank), F32),
            jax.ShapeDtypeStruct((SEQS, 128), F32),
        ),
        in_specs=[VMEM] * 2,
        out_specs=(VMEM, VMEM),
        compiler_params=small_kernel(24),
        name="sketches",
    )(vectors, ids)
    scores = pl.pallas_call(
        score_kernel,
        out_shape=jax.ShapeDtypeStruct((SEQS, DOMAINS), F32),
        in_specs=[VMEM] * 2,
        out_specs=VMEM,
        compiler_params=small_kernel(4),
        name="scores",
    )(parts, norms)
    return sketches, scores


def solution(mesh):
    in_specs = (
        P(("groups", "dp"), None),
        P(("groups", "dp"), None),
        P("dp", None),
        P("dp", None),
        P("dp", None),
        P("dp", None),
        P("dp", None),
        P("groups"),
        P(("groups", "dp"), None, None, None),
        P(("groups", "dp")),
    )
    out_specs = (P("groups", None, None, None), P("groups", None))
    return jax.shard_map(
        functools.partial(on_device, mesh.shape["dp"]),
        mesh=mesh,
        in_specs=in_specs,
        out_specs=out_specs,
        check_vma=False,
    )
```
